32 devices in a mesh: tower: 2 (over y), dp: 4 (over z), fsdp: 4 (over x, core).
Axes of the slice: x: 2, y: 2, z: 4, core: 2. Of those that a mesh axis runs over, the one named last changes fastest.
Arguments:
- tokens_in: bfloat16 [2, 2, 16, 512, 768], P('tower', None, ('dp', 'fsdp')), may hold values from -6 to 6
- query_lengths: int32 [2, 16, 8], P(None, ('dp', 'fsdp')), may hold values from 1 to 256, 512 in all within a row
- positive_ids: int32 [2, 16, 8], P(None, ('dp', 'fsdp')), may hold values from 0 to 15
- gain_attn: float32 [768], P('fsdp'), may hold values from 0.1 to 1.9
- gain_ffn: float32 [768], P('fsdp'), may hold values from 0.1 to 1.9
- w_query: float32 [768, 768], P('fsdp'), may hold values from -0.09375 to 0.09375
- w_key: float32 [768, 768], P('fsdp'), may hold values from -0.09375 to 0.09375
- w_value: float32 [768, 768], P('fsdp'), may hold values from -0.21875 to 0.21875
- w_out: float32 [768, 768], P('fsdp'), may hold values from -1.75 to 1.75
- rel_bias: float32 [32, 12], P('fsdp'), may hold values from -4 to 4
- w_in: float32 [768, 3072], P('fsdp'), may hold values from -0.21875 to 0.21875
- w_ffn_out: float32 [3072, 768], P('fsdp'), may hold values from -0.109375 to 0.109375
- w_proj: float32 [768, 768], P('fsdp'), may hold values from -0.21875 to 0.21875
Outputs:
- query_loss: float32 [2, 16, 8], P(None, ('dp', 'fsdp'))
- grad_tokens: bfloat16 [2, 2, 16, 512, 768], P('tower', None, ('dp', 'fsdp'))
- grad_gain_attn: float32 [768], P('fsdp')
- grad_gain_ffn: float32 [768], P('fsdp')
- grad_w_query: float32 [768, 768], P('fsdp')
- grad_w_key: float32 [768, 768], P('fsdp')
- grad_w_value: float32 [768, 768], P('fsdp')
- grad_w_out: float32 [768, 768], P('fsdp')
- grad_rel_bias: float32 [32, 12], P('fsdp')
- grad_w_in: float32 [768, 3072], P('fsdp')
- grad_w_ffn_out: float32 [3072, 768], P('fsdp')
- grad_w_proj: float32 [768, 768], P('fsdp')
The draws below stay inside these ranges and needn't reach their ends.
Inputs may be any that keep to these rules, and one draw needn't show every extreme that they name: `query_lengths`: in every row the 8 lengths sum to 512, and the longest is exactly 256.
All inputs are finite; a program needn't handle non-finite values.
Results may differ from the reference program's by a relative error of at most 0.018.
The reference program's roundings to bfloat16 on the way count: a program that leaves them out, or rounds other values in their place, can miss the bound.
Values may be sent and summed in bfloat16 or wider, within the bound.
No kernel may reach another device: no remote copies, remote signals or barrier semaphores. Data moves between devices by JAX's collectives and lax.ppermute only.
A program may use at most 192 MiB of HBM per device.

```python
import functools
import math
import jax
import jax.numpy as jnp
import numpy as np
from jax import lax

D = 768
H = 12
DH = 64
FF = 3072
P_SIZE = 768
NB = 32
SEQ = 512
PLEN = 512
QSEG = 8
QMAX = 256
MB = 2
PSEG = 1
ROWS = 16


def touch_ends(array, key, least, largest):
    dims = array.shape
    place = [jax.random.randint(jax.random.fold_in(key, axis), (), 0, dims[axis]) for axis in range(len(dims))]
    array = array.at[tuple(place)].set(least)
    longest = dims.index(max(dims))
    place[longest] = (place[longest] + 1) % dims[longest]
    return array.at[tuple(place)].set(largest)


def steps_of(stream_key, shape, pieces, low, top_value):
    factor_of, own = 1.0, jax.random.fold_in(stream_key, 6)
    for position, blocks in pieces:
        steps = jnp.exp(jax.random.uniform(jax.random.fold_in(own, position), (blocks,), jnp.float32, low / len(pieces), top_value / len(pieces)))
        factor_of = factor_of * jnp.repeat(steps, shape[position] // blocks).reshape([-1 if axis == position else 1 for axis in range(len(shape))])
    return factor_of


def split_up(count, total, reach, lean):
    loads = [(1 << 20) // math.isqrt(rank ** lean) + 1 for rank in range(2, count + 1)]
    rest, holding = total - reach - (count - 1), [1] * (count - 1)
    while rest > 0:
        candidates = [i for i in range(count - 1) if holding[i] < reach]
        mass, budget = sum([loads[i] for i in candidates]), rest
        for i in candidates:
            extra = min(reach - holding[i], max(1, budget * loads[i] // mass), rest)
            holding[i] = holding[i] + extra
            rest = rest - extra
    return np.array([reach] + holding)


def uneven_parts(key, number_of, total, limit, slope):
    if number_of == 2:
        one = jax.random.randint(key, (), max(1, total - limit), min(limit, total - 1) + 1)
        return jnp.stack([one, total - one])
    sizes = jnp.asarray(split_up(number_of, total, limit, slope), jnp.int32)
    pairs = (number_of - 1) // 2
    giver, taker = sizes[1:1 + 2 * pairs:2], sizes[2:2 + 2 * pairs:2]
    room = jnp.minimum(giver - 1, limit - taker)
    shifted = jax.random.randint(jax.random.fold_in(key, 1), (pairs,), 0, 1 << 20) % (room + 1)
    sizes = sizes.at[1:1 + 2 * pairs:2].set(giver - shifted).at[2:2 + 2 * pairs:2].set(taker + shifted)
    return sizes[jax.random.permutation(jax.random.fold_in(key, 2), number_of)]


def scatter_about(rng, shape, deviation, reach, pieces=(), kind=jnp.bfloat16):
    factor_of = steps_of(rng, shape, pieces, -0.22, 0.18) if pieces else 1.0
    values = jax.random.normal(rng, shape, jnp.float32) * deviation * factor_of
    return jnp.minimum(jnp.maximum(values, -reach), reach).astype(kind)


def setup_inputs(seed: int = 0) -> dict:
    arg_keys = jax.random.split(jax.random.key(seed), 14)
    tokens_in = scatter_about(arg_keys[0], (2, MB, ROWS, SEQ, D), 1.0, 6.0, ((0, 2), (2, 16)))
    query_lengths = jax.vmap(lambda own: uneven_parts(own, QSEG, SEQ, QMAX, 2))(jax.random.split(arg_keys[1], MB * ROWS)).reshape((MB, ROWS, QSEG)).astype(jnp.int32)
    positive_ids = touch_ends(jax.random.randint(arg_keys[2], (MB, ROWS, QSEG), 0, ROWS * PSEG), jax.random.fold_in(arg_keys[2], 1), 0, (ROWS * PSEG) - 1).astype(jnp.int32)
    gain_attn = jnp.clip(1.0 + 0.18 * jax.random.normal(arg_keys[3], (D,), jnp.float32), 0.1, 1.9)
    gain_ffn = jnp.clip(1.0 + 0.18 * jax.random.normal(arg_keys[4], (D,), jnp.float32), 0.1, 1.9)
    w_query = scatter_about(arg_keys[5], (D, H * DH), (6 * D) ** -0.5, 0.09375, ((0, 4),), jnp.float32)
    w_key = scatter_about(arg_keys[6], (D, H * DH), (6 * D) ** -0.5, 0.09375, ((0, 4),), jnp.float32)
    w_value = scatter_about(arg_keys[7], (D, H * DH), D ** -0.5, 0.21875, ((0, 4),), jnp.float32)
    w_out = scatter_about(arg_keys[8], (H * DH, D), H ** -0.5, 1.75, ((0, 4),), jnp.float32)
    rel_bias = scatter_about(arg_keys[9], (NB, H), 1.0, 4.0, ((0, 4),), jnp.float32)
    w_in = scatter_about(arg_keys[10], (D, FF), D ** -0.5, 0.21875, ((0, 4),), jnp.float32)
    w_ffn_out = scatter_about(arg_keys[11], (FF, D), FF ** -0.5, 0.109375, ((0, 4),), jnp.float32)
    w_proj = scatter_about(arg_keys[12], (D, P_SIZE), D ** -0.5, 0.21875, ((0, 4),), jnp.float32)
    return {"tokens_in": tokens_in, "query_lengths": query_lengths, "positive_ids": positive_ids, "gain_attn": gain_attn, "gain_ffn": gain_ffn, "w_query": w_query, "w_key": w_key, "w_value": w_value, "w_out": w_out, "rel_bias": rel_bias, "w_in": w_in, "w_ffn_out": w_ffn_out, "w_proj": w_proj}


EPSILON = 1e-06
LOGIT_SCALE = 50.0
LOSS_SCALE = 256.0
THRESHOLDS = (12, 16, 23, 32, 46, 64, 91)
MASKED = -1e+30
HIGHEST = lax.Precision.HIGHEST

@jax.custom_vjp
def low(v):
    return lax.optimization_barrier(v.astype(jnp.bfloat16)).astype(jnp.float32)

@jax.custom_vjp
def low_back(v):
    return v

def low_keep(v):
    return (low(v), None)

def low_pass(kept, grad):
    return (grad,)

def back_keep(v):
    return (v, None)

def back_low(kept, grad):
    return (low(grad),)
low.defvjp(low_keep, low_pass)
low_back.defvjp(back_keep, back_low)

def matmul(left, right):
    return jnp.dot(left, right, precision=HIGHEST, preferred_element_type=jnp.float32)

def bucket_matrix(length):
    query_place = lax.broadcasted_iota(jnp.int32, (length, length), 0)
    key_place = lax.broadcasted_iota(jnp.int32, (length, length), 1)
    offset = key_place - query_place
    distance = jnp.abs(offset)
    far_bucket = 8 + sum(((distance >= threshold).astype(jnp.int32) for threshold in THRESHOLDS))
    inside = jnp.where(distance < 8, distance, far_bucket)
    return (jnp.where(offset > 0, 16, 0) + inside).astype(jnp.int32)

def query_segments(lengths):
    ends_at = jnp.cumsum(lengths, axis=-1).astype(jnp.int32)
    places = jnp.arange(SEQ, dtype=jnp.int32)
    segment = lax.optimization_barrier(jnp.sum((places[None, :, None] >= ends_at[:, None, :]).astype(jnp.int32), axis=-1)).astype(jnp.int32)
    return (segment, lengths.astype(jnp.int32))

def passage_segments(row_count):
    places = jnp.arange(SEQ, dtype=jnp.int32)
    segment = jnp.broadcast_to(places // PLEN, (row_count, SEQ)).astype(jnp.int32)
    counts = jnp.where(jnp.arange(QSEG, dtype=jnp.int32) < PSEG, PLEN, 0).astype(jnp.int32)
    return (segment, jnp.broadcast_to(counts, (row_count, QSEG)))

def embed_row(weights, bias_full, operands):
    gain_one, gain_two, query_mat, key_mat, value_mat, out_mat, in_mat, ffn_mat, proj_mat = weights
    tokens_row, segment, counts = operands
    scaled_one = tokens_row * lax.rsqrt(lax.optimization_barrier(jnp.mean(tokens_row * tokens_row, axis=-1, keepdims=True)) + EPSILON)
    normed_one = low(scaled_one * gain_one)
    queries = low(low_back(matmul(normed_one, query_mat))).reshape(SEQ, H, DH)
    keys_all = low(low_back(matmul(normed_one, key_mat))).reshape(SEQ, H, DH)
    values_all = low(low_back(matmul(normed_one, value_mat))).reshape(SEQ, H, DH)
    scores = jnp.einsum('ihd,jhd->hij', queries, keys_all, precision=HIGHEST) + bias_full
    scores = low_back(scores)
    same_segment = segment[:, None] == segment[None, :]
    scores = jnp.where(same_segment[None], scores, MASKED)
    weights_low = low(jax.nn.softmax(scores, axis=-1))
    attended = jnp.einsum('hij,jhd->ihd', weights_low, values_all, precision=HIGHEST).reshape(SEQ, H * DH)
    attended = low(low_back(attended))
    after_attn = tokens_row + low_back(matmul(attended, out_mat))
    scaled_two = after_attn * lax.rsqrt(lax.optimization_barrier(jnp.mean(after_attn * after_attn, axis=-1, keepdims=True)) + EPSILON)
    normed_two = low(scaled_two * gain_two)
    hidden_pre = low_back(matmul(normed_two, in_mat))
    hidden = low(jax.nn.gelu(hidden_pre))
    after_ffn = after_attn + low_back(matmul(hidden, ffn_mat))
    slot_index = jnp.arange(QSEG, dtype=jnp.int32)
    pool_weights = (segment[None, :] == slot_index[:, None]).astype(jnp.float32)
    pool_weights = pool_weights / jnp.maximum(counts, 1).astype(jnp.float32)[:, None]
    pooled = low(matmul(pool_weights, after_ffn))
    projected = low_back(matmul(pooled, proj_mat))
    return low(projected * lax.rsqrt(lax.optimization_barrier(jnp.sum(projected * projected, axis=-1, keepdims=True)) + EPSILON))

def micro_objective(params, query_rows, passage_rows, lengths_micro, positives_micro):
    weights = tuple((low(master) for master in params))
    gain_one, gain_two, query_mat, key_mat, value_mat, out_mat, table_mat, in_mat, ffn_mat, proj_mat = weights
    dense = (gain_one, gain_two, query_mat, key_mat, value_mat, out_mat, in_mat, ffn_mat, proj_mat)
    buckets = bucket_matrix(SEQ)
    bias_full = jnp.transpose(table_mat[buckets], (2, 0, 1))
    query_segment, query_counts = query_segments(lengths_micro)
    passage_segment, passage_counts = passage_segments(passage_rows.shape[0])
    row_function = jax.checkpoint(functools.partial(embed_row, dense, bias_full))
    query_embed = lax.map(row_function, (query_rows, query_segment, query_counts))
    passage_embed = lax.map(row_function, (passage_rows, passage_segment, passage_counts))[:, :PSEG]
    flat_queries = query_embed.reshape(query_rows.shape[0] * QSEG, P_SIZE)
    flat_passages = passage_embed.reshape(passage_rows.shape[0] * PSEG, P_SIZE)
    logits = LOGIT_SCALE * matmul(flat_queries, flat_passages.T)
    logit_top = lax.optimization_barrier(jnp.max(logits, axis=-1, keepdims=True))
    log_total = logit_top[:, 0] + jnp.log(lax.optimization_barrier(jnp.sum(jnp.exp(logits - logit_top), axis=-1)))
    chosen = jnp.take_along_axis(logits, positives_micro.reshape(-1, 1).astype(jnp.int32), axis=1)[:, 0]
    losses = log_total - chosen
    return (LOSS_SCALE * jnp.sum(losses), losses.reshape(query_rows.shape[0], QSEG))

def reference(tokens_in, query_lengths, positive_ids, gain_attn, gain_ffn, w_query, w_key, w_value, w_out, rel_bias, w_in, w_ffn_out, w_proj):
    params = (gain_attn, gain_ffn, w_query, w_key, w_value, w_out, rel_bias, w_in, w_ffn_out, w_proj)
    totals = tuple((jnp.zeros(master.shape, jnp.float32) for master in params))
    rows_float = tokens_in.astype(jnp.float32)
    losses_all = []
    token_grads = []
    for micro_step in range(MB):

        def objective(weights_in, query_rows, passage_rows):
            return micro_objective(weights_in, query_rows, passage_rows, query_lengths[micro_step], positive_ids[micro_step])
        value_out, pullback, losses = jax.vjp(objective, params, rows_float[0, micro_step], rows_float[1, micro_step], has_aux=True)
        grads_params, grad_query_rows, grad_passage_rows = pullback(jnp.ones((), jnp.float32))
        totals = tuple((before + added for before, added in zip(totals, grads_params)))
        losses_all.append(losses)
        token_grads.append(jnp.stack([grad_query_rows, grad_passage_rows]))
    grad_tokens = jnp.stack(token_grads, axis=1).astype(jnp.bfloat16)
    return (jnp.stack(losses_all), grad_tokens, totals[0], totals[1], totals[2], totals[3], totals[4], totals[5], totals[6], totals[7], totals[8], totals[9])
```

```python
import functools

import jax
import jax.numpy as jnp
from jax import lax
from jax.experimental import pallas as pl
from jax.experimental.pallas import tpu as pltpu
from jax.sharding import PartitionSpec as P

D = 768
H = 12
DH = 64
FF = 3072
NB = 32
SEQ = 512
QSEG = 8
MB = 2
T = MB * SEQ
SLOTS = MB * QSEG
PAY = D + 128
EPSILON = 1e-06
LOGIT_SCALE = 50.0
LOSS_SCALE = 256.0
THRESHOLDS = (12, 16, 23, 32, 46, 64, 91)
GELU_C = 0.7978845608028654
ALL = ("tower", "dp", "fsdp")
BF = jnp.bfloat16
F32 = jnp.float32
HIGHEST = lax.Precision.HIGHEST
NT = (((1,), (1,)), ((), ()))
TN = (((0,), (0,)), ((), ()))

def bucket_of(m):
    a=jnp.abs(m)
    far=8+sum((a>=t).astype(jnp.int32) for t in THRESHOLDS)
    return jnp.where(m>0,16,0)+jnp.where(a<8,a,far)

def diag_hot():
    col=lax.broadcasted_iota(jnp.int32,(NB,1024),1)
    m=(col//128-3)*128-col%128
    return (bucket_of(m)==lax.broadcasted_iota(jnp.int32,(NB,1024),0)).astype(BF)

def bias_kernel(tab_ref, hot_ref, out_ref):
    w=jnp.dot(tab_ref[...],hot_ref[...],preferred_element_type=F32)
    jj=lax.broadcasted_iota(jnp.int32,(128,128),0); ii=lax.broadcasted_iota(jnp.int32,(128,128),1)
    up=ii>=jj
    for h in range(H):
        prev=None
        for e in range(8):
            r=pltpu.roll(jnp.broadcast_to(w[h:h+1,e*128:(e+1)*128],(128,128)),0,1,stride=1,stride_axis=0)
            if e>0: out_ref[h,e-1]=jnp.where(up,prev,r)
            prev=r
def bias_blocks(table_t, hot):
    return pl.pallas_call(bias_kernel,out_shape=jax.ShapeDtypeStruct((H,7,128,128),F32),name="bias_blocks")(table_t,hot)

def attn_fwd_kernel(q_ref,k_ref,v_ref,fq_ref,fk_ref,bias_ref,o_ref,ot_ref,e_ref,li_ref):
    lane=lax.broadcasted_iota(jnp.int32,(SEQ,128),1)
    q=q_ref[...];k=k_ref[...];fq=fq_ref[...];fk=fk_ref[...]
    vt=v_ref[...].T
    outs=[]
    for s in range(2):
        own=(lane<64) if s==0 else (lane>=64)
        qa=jnp.where(own,q,fq); ka=jnp.where(own,k,fk)
        st=lax.dot_general(ka,qa,(((1,),(1,)),((),())),preferred_element_type=F32)
        b=jnp.concatenate([jnp.concatenate([bias_ref[s,bj-bi+3] for bi in range(4)],axis=1) for bj in range(4)],axis=0)
        st=st+b
        top=jnp.max(st,axis=0,keepdims=True)
        e=jnp.exp(st-top).astype(BF)
        e_ref[0,s]=e
        va=jnp.concatenate([vt[64*s:64*s+64],jnp.ones((16,SEQ),BF)],axis=0)
        ot=jnp.dot(va,e,preferred_element_type=F32)
        linv=1.0/ot[64:65]
        li_ref[0,s]=jnp.broadcast_to(linv,(8,SEQ))
        outs.append((ot[:64]*linv).astype(BF))
    ot=jnp.concatenate(outs,axis=0)
    ot_ref[...]=ot
    o_ref[...]=ot.T

def attn_fwd(qkv,fq,fk,bias):
    grid=(6,2)
    return pl.pallas_call(attn_fwd_kernel,grid=grid,
      in_specs=[pl.BlockSpec((SEQ,128),lambda p,r:(r,p)),pl.BlockSpec((SEQ,128),lambda p,r:(r,6+p)),pl.BlockSpec((SEQ,128),lambda p,r:(r,12+p)),
        pl.BlockSpec((SEQ,128),lambda p,r:(r,0)),pl.BlockSpec((SEQ,128),lambda p,r:(r,0)),
        pl.BlockSpec((2,7,128,128),lambda p,r:(p,0,0,0))],
      out_specs=[pl.BlockSpec((SEQ,128),lambda p,r:(r,p)),pl.BlockSpec((128,SEQ),lambda p,r:(p,r)),
        pl.BlockSpec((1,2,SEQ,SEQ),lambda p,r:(r,p,0,0)),pl.BlockSpec((1,2,8,SEQ),lambda p,r:(r,p,0,0))],
      out_shape=[jax.ShapeDtypeStruct((T,D),BF),jax.ShapeDtypeStruct((D,T),BF),jax.ShapeDtypeStruct((2,H,SEQ,SEQ),BF),jax.ShapeDtypeStruct((2,H,8,SEQ),F32)],
      compiler_params=pltpu.CompilerParams(dimension_semantics=("arbitrary","arbitrary"),vmem_limit_bytes=48*2**20),name="attn_fwd")(qkv,qkv,qkv,fq,fk,bias)

def attn_bwd_kernel(q_ref,k_ref,v_ref,do_ref,ot_ref,e_ref,li_ref,dq_ref,dk_ref,dv_ref,diag_ref,acc):
    r=pl.program_id(1)
    lane=lax.broadcasted_iota(jnp.int32,(SEQ,128),1)
    q=q_ref[...];k=k_ref[...];v=v_ref[...];do=do_ref[...]
    kt=k.T
    dot_=do.T
    dqs=[]
    prod=dot_.astype(F32)*ot_ref[...].astype(F32)
    for s in range(2):
        own=(lane<64) if s==0 else (lane>=64)
        linv=li_ref[0,s,0:1,:]
        delta=jnp.sum(prod[64*s:64*s+64],axis=0,keepdims=True)
        vm=jnp.where(own,v,jnp.zeros_like(v))
        dp=lax.dot_general(vm,do,(((1,),(1,)),((),())),preferred_element_type=F32)
        p=e_ref[0,s].astype(F32)*linv
        ds32=p*(dp-delta)
        ds=ds32.astype(BF)
        pb=p.astype(BF)
        dvh=jnp.dot(pb,do,preferred_element_type=F32)
        dkh=jnp.dot(ds,q,preferred_element_type=F32)
        dqt=jnp.dot(kt[64*s:64*s+64],ds,preferred_element_type=F32)
        dqs.append(dqt.astype(BF))
        if s==0: dv0,dk0=dvh,dkh
        else:
            dv_ref[...]=jnp.where(lane<64,dv0,dvh).astype(BF)
            dk_ref[...]=jnp.where(lane<64,dk0,dkh).astype(BF)
        sums=[]
        for d in range(-3,4):
            t=None
            for bj in range(4):
                bi=bj-d
                if 0<=bi<4:
                    blk=ds32[128*bj:128*bj+128,128*bi:128*bi+128]
                    t=blk if t is None else t+blk
            sums.append(t)
        for d in range(7):
            prev=jnp.where(r==0,jnp.zeros((128,128),F32),acc[s,d])
            acc[s,d]=prev+sums[d]
    dq_ref[...]=jnp.concatenate(dqs,axis=0).T
    @pl.when(r==1)
    def _():
        jj=lax.broadcasted_iota(jnp.int32,(128,128),0); ii=lax.broadcasted_iota(jnp.int32,(128,128),1)
        up=ii>=jj
        for s in range(2):
            rows=[]
            for e in range(8):
                a=acc[s,e] if e<7 else jnp.zeros((128,128),F32)
                b=acc[s,e-1] if e>0 else jnp.zeros((128,128),F32)
                c=jnp.where(up,a,b)
                t=c[0:8]
                for g in range(1,16):
                    t=t+pltpu.roll(c[8*g:8*g+8],128-8*g,1)
                rows.append(t)
            diag_ref[0,s]=jnp.concatenate(rows,axis=1)

def diag_hot2():
    c=lax.broadcasted_iota(jnp.int32,(8192,NB),0)
    s=c//1024; col=c%1024
    m=(col//128-3)*128-(col%128-s)%128
    return (bucket_of(m)==lax.broadcasted_iota(jnp.int32,(8192,NB),1)).astype(F32)

def attn_bwd(qkv,do,ot,e,li):
    return pl.pallas_call(attn_bwd_kernel,grid=(6,2),
      in_specs=[pl.BlockSpec((SEQ,128),lambda p,r:(r,p)),pl.BlockSpec((SEQ,128),lambda p,r:(r,6+p)),pl.BlockSpec((SEQ,128),lambda p,r:(r,12+p)),
        pl.BlockSpec((SEQ,128),lambda p,r:(r,p)),pl.BlockSpec((128,SEQ),lambda p,r:(p,r)),
        pl.BlockSpec((1,2,SEQ,SEQ),lambda p,r:(r,p,0,0)),pl.BlockSpec((1,2,8,SEQ),lambda p,r:(r,p,0,0))],
      out_specs=[pl.BlockSpec((SEQ,128),lambda p,r:(r,p))]*3+[pl.BlockSpec((1,2,8,1024),lambda p,r:(p,0,0,0))],
      out_shape=[jax.ShapeDtypeStruct((T,D),BF)]*3+[jax.ShapeDtypeStruct((6,2,8,1024),F32)],
      scratch_shapes=[pltpu.VMEM((2,7,128,128),F32)],
      compiler_params=pltpu.CompilerParams(dimension_semantics=("arbitrary","arbitrary"),vmem_limit_bytes=48*2**20),name="attn_bwd")(qkv,qkv,qkv,do,ot,e,li)


def swap(block, axis, bit):
    size = lax.axis_size(axis)
    return lax.ppermute(block, axis, [(i, i ^ bit) for i in range(size)])


def gather_group(shard):
    rows, cols = shard.shape
    half = rows // 2
    f = lax.axis_index("fsdp")
    t = lax.axis_index("tower")
    sent = lax.dynamic_slice_in_dim(shard, t * half, half, 0)
    near = swap(sent, "fsdp", 2)
    mate = swap(shard, "fsdp", 1)
    far = swap(near, "tower", 1)
    near_mate = swap(near, "fsdp", 1)
    far_mate = swap(far, "fsdp", 1)
    full = jnp.zeros((4 * rows, cols), shard.dtype)
    for piece, start in (
        (shard, f * rows),
        (mate, (f ^ 1) * rows),
        (near, (f ^ 2) * rows + t * half),
        (far, (f ^ 2) * rows + (1 - t) * half),
        (near_mate, (f ^ 3) * rows + t * half),
        (far_mate, (f ^ 3) * rows + (1 - t) * half),
    ):
        full = lax.dynamic_update_slice_in_dim(full, piece, start, 0)
    return full


def pick(parts, index):
    return lax.dynamic_index_in_dim(parts, index, 0, keepdims=False)


def added(kept, got):
    return lax.optimization_barrier((kept.astype(F32) + got.astype(F32)).astype(BF))


def reduce_group(grads):
    rows, cols = grads.shape
    quarter = rows // 4
    f = lax.axis_index("fsdp")
    a, b = f // 2, f % 2
    t = lax.axis_index("tower")
    parts = grads.reshape(2, 2, quarter, cols)
    sent = lax.dynamic_index_in_dim(parts, 1 - b, 1, keepdims=False)
    kept = lax.dynamic_index_in_dim(parts, b, 1, keepdims=False)
    total = added(kept, swap(sent, "fsdp", 1))
    total = added(pick(total, a), swap(pick(total, 1 - a), "fsdp", 2))
    total = total.reshape(2, quarter // 2, cols)
    total = added(pick(total, t), swap(pick(total, 1 - t), "tower", 1))
    bit = 1
    while bit < lax.axis_size("dp"):
        total = added(total, swap(total, "dp", bit))
        bit *= 2
    other = swap(total, "tower", 1)
    first = jnp.where(t == 0, total, other)
    second = jnp.where(t == 0, other, total)
    return jnp.concatenate([first, second], axis=0).astype(F32)


def loss_kernel(rows, pos_ref, buf_ref, proj_ref, loss_ref, own_ref, all_ref, gproj_ref, scr, gp_scr, sem):
    me, is_query, row, quarter = pos_ref[0], pos_ref[1], pos_ref[2], pos_ref[3]
    nq, np_ = rows * SLOTS, rows * MB
    for k in range(2 * rows):
        a = me ^ k
        start = ((a >> 2) & 1) * nq + ((a >> 3) * 4 + (a & 3)) * SLOTS
        pltpu.make_async_copy(
            buf_ref.at[pl.ds(k * SLOTS, SLOTS)], scr.at[pl.ds(pl.multiple_of(start, SLOTS), SLOTS)], sem
        ).start()
    pltpu.make_async_copy(buf_ref, scr, sem).wait()
    picker = (
        lax.broadcasted_iota(jnp.int32, (np_, nq), 1) == QSEG * lax.broadcasted_iota(jnp.int32, (np_, nq), 0)
    ).astype(BF)
    q_all = scr[:nq]
    p_all = jnp.dot(picker, scr[nq:], preferred_element_type=F32).astype(BF)
    both = jnp.concatenate([q_all[:, :D], p_all[:, :D]], axis=0)
    extra = jnp.concatenate([q_all[:, D:], p_all[:, D:]], axis=0).astype(F32)
    z = jnp.dot(both, proj_ref[...], preferred_element_type=F32)
    inv = lax.rsqrt(jnp.sum(z * z, axis=-1, keepdims=True) + EPSILON)
    w = z * inv
    e = w.astype(BF)
    eq, ep = e[:nq], e[nq:]
    logits = LOGIT_SCALE * lax.dot_general(eq, ep, NT, preferred_element_type=F32)
    q_row = lax.broadcasted_iota(jnp.int32, (nq, np_), 0)
    p_col = lax.broadcasted_iota(jnp.int32, (nq, np_), 1)
    micro = (q_row // QSEG) % MB
    same = micro == p_col % MB
    logits = jnp.where(same, logits, -1e30)
    top = jnp.max(logits, axis=-1, keepdims=True)
    log_total = top + jnp.log(jnp.sum(jnp.exp(logits - top), axis=-1, keepdims=True))
    positive = extra[:nq, 1:2].astype(jnp.int32)
    hot = jnp.where(same & (p_col // MB == positive), 1.0, 0.0)
    chosen = jnp.sum(logits * hot, axis=-1, keepdims=True)
    loss = log_total - chosen
    gl = LOSS_SCALE * (jnp.exp(logits - log_total) - hot)
    g_eq = LOGIT_SCALE * jnp.dot(gl, ep.astype(F32), precision=HIGHEST, preferred_element_type=F32)
    g_ep = LOGIT_SCALE * lax.dot_general(gl, eq.astype(F32), TN, precision=HIGHEST, preferred_element_type=F32)
    ge = jnp.concatenate([g_eq, g_ep], axis=0)
    gz = (inv * (ge - w * jnp.sum(w * ge, axis=-1, keepdims=True))).astype(BF)
    gp_scr[...] = lax.dot_general(both, gz, TN, preferred_element_type=F32)
    gproj_ref[...] = gp_scr[pl.ds(pl.multiple_of(quarter * (D // 4), D // 4), D // 4), :]
    g_pooled = lax.dot_general(gz, proj_ref[...], NT, preferred_element_type=F32)
    g_x3 = g_pooled / jnp.maximum(extra[:, 0:1], 1.0)
    gp3 = jnp.concatenate([g_x3[nq:]], axis=0)
    hi = gp3.astype(BF)
    lo = (gp3 - hi.astype(F32)).astype(BF)
    spread = lambda v: lax.dot_general(picker, v, TN, preferred_element_type=F32)
    all_ref[0] = g_x3[:nq].astype(BF)
    p_hi = spread(hi)
    all_ref[1] = p_hi.astype(BF)
    p_full = p_hi + spread(lo)
    scr_q = jnp.where(is_query == 1, g_x3[:nq], p_full)
    gp_big = scr_q
    own_sel = (
        lax.broadcasted_iota(jnp.int32, (SLOTS, nq), 1) == row * SLOTS + lax.broadcasted_iota(jnp.int32, (SLOTS, nq), 0)
    ).astype(F32)
    own_ref[...] = jnp.dot(own_sel, gp_big, precision=HIGHEST, preferred_element_type=F32)
    loss_ref[...] = jnp.dot(
        own_sel, jnp.broadcast_to(loss, (nq, 128)), precision=HIGHEST, preferred_element_type=F32
    )


def loss_call(place, buf, proj, rows):
    nq = rows * SLOTS
    return pl.pallas_call(
        functools.partial(loss_kernel, rows),
        in_specs=[
            pl.BlockSpec(memory_space=pltpu.SMEM),
            pl.BlockSpec(memory_space=pl.ANY),
            pl.BlockSpec(memory_space=pltpu.VMEM),
        ],
        out_specs=[pl.BlockSpec(memory_space=pltpu.VMEM)] * 4,
        out_shape=[
            jax.ShapeDtypeStruct((SLOTS, 128), F32),
            jax.ShapeDtypeStruct((SLOTS, D), F32),
            jax.ShapeDtypeStruct((2, nq, D), BF),
            jax.ShapeDtypeStruct((D // 4, D), F32),
        ],
        scratch_shapes=[pltpu.VMEM((2 * nq, PAY), BF), pltpu.VMEM((D, D), F32), pltpu.SemaphoreType.DMA],
        compiler_params=pltpu.CompilerParams(vmem_limit_bytes=60 * 2**20),
        name="loss",
    )(place, buf, proj)


def split(v):
    hi = v.astype(BF)
    return hi, (v - hi.astype(F32)).astype(BF)


def dot(a, b):
    return jnp.dot(a, b, preferred_element_type=F32)


def dot_nt(a, b):
    return lax.dot_general(a, b, NT, preferred_element_type=F32)


def dot_tn(a, b):
    return lax.dot_general(a, b, TN, preferred_element_type=F32)


def norm(x, gain):
    inv = lax.rsqrt(jnp.mean(x * x, axis=-1, keepdims=True) + EPSILON)
    scaled = x * inv
    return inv, scaled, (scaled * gain).astype(BF)


def norm_back(g, inv, scaled, gain):
    gs = g * gain
    return inv * (gs - scaled * jnp.mean(gs * scaled, axis=-1, keepdims=True)), jnp.sum(g * scaled, axis=0)


def local(
    tokens_in,
    query_lengths,
    positive_ids,
    gain_attn,
    gain_ffn,
    w_query,
    w_key,
    w_value,
    w_out,
    rel_bias,
    w_in,
    w_ffn_out,
    w_proj,
):
    f = lax.axis_index("fsdp")
    t = lax.axis_index("tower")
    z = lax.axis_index("dp")
    n_dp = lax.axis_size("dp")
    rows = n_dp * 4
    is_query = t == 0
    small = jnp.concatenate(
        [gain_attn, gain_ffn, rel_bias.reshape(-1), jnp.zeros((32,), F32)]
    ).astype(BF)
    small = lax.all_gather(small, "fsdp", axis=0)
    gain_one = small[:, :192].reshape(1, D).astype(F32)
    gain_two = small[:, 192:384].reshape(1, D).astype(F32)
    table = small[:, 384 : 384 + 96].reshape(NB, H)
    w_qkv = gather_group(jnp.concatenate([w_query, w_key, w_value], axis=1).astype(BF))
    w_mid = gather_group(jnp.concatenate([w_out, w_in], axis=1).astype(BF))
    w_o, w_i = w_mid[:, :D], w_mid[:, D:]
    w_f = gather_group(w_ffn_out.astype(BF))
    w_p = gather_group(w_proj.astype(BF))

    lengths = query_lengths[:, 0]
    ends = jnp.cumsum(lengths, axis=-1)
    places = lax.broadcasted_iota(jnp.int32, (MB, SEQ, QSEG), 1)
    segment = jnp.where(is_query, jnp.sum((places >= ends[:, None, :]).astype(jnp.int32), axis=-1), 0)
    slot_ids = lax.broadcasted_iota(jnp.int32, (MB, QSEG), 1)
    counts = jnp.where(is_query, lengths, jnp.where(slot_ids < 1, SEQ, 0))
    seg = segment.reshape(T)
    lane = lax.broadcasted_iota(jnp.int32, (T, 128), 1) % 64
    hot_seg = lane == seg[:, None]
    fq = jnp.where(hot_seg, 1.0, 0.0).astype(BF)
    fk = jnp.where((lane < QSEG) & ~hot_seg, -1e30, 0.0).astype(BF)
    slot_of = seg + QSEG * (lax.broadcasted_iota(jnp.int32, (T,), 0) // SEQ)
    member = (slot_of[:, None] == lax.broadcasted_iota(jnp.int32, (T, SLOTS), 1)).astype(BF)
    member_t = (slot_of[None, :] == lax.broadcasted_iota(jnp.int32, (SLOTS, T), 0)).astype(BF)
    bias = bias_blocks(jnp.pad(table.T, ((0, 4), (0, 0))), diag_hot())

    x = tokens_in.reshape(T, D).astype(F32)
    inv1, r1, n1 = norm(x, gain_one)
    qkv = dot(n1, w_qkv).astype(BF)
    o, ot, e, li = attn_fwd(qkv, fq, fk, bias)
    x2 = x + dot(o, w_o)
    inv2, r2, n2 = norm(x2, gain_two)
    u = dot(n2, w_i)
    th = jnp.tanh(GELU_C * (u + 0.044715 * u * u * u))
    hh = (0.5 * u * (1.0 + th)).astype(BF)
    gp = (0.5 * (1.0 + th) + 0.5 * u * (1.0 - th * th) * (GELU_C * (1.0 + 3 * 0.044715 * u * u))).astype(BF)
    acts = dot(member_t, hh)
    x2_hi, x2_lo = split(x2)
    acts_hi, acts_lo = split(acts)
    count = jnp.maximum(counts, 1).astype(F32).reshape(SLOTS, 1)
    pooled = (dot(member_t, x2_hi) + dot(member_t, x2_lo) + dot(acts_hi, w_f) + dot(acts_lo, w_f)) / count
    info = jnp.concatenate(
        [
            counts.reshape(SLOTS, 1).astype(F32),
            positive_ids.reshape(SLOTS, 1).astype(F32),
            jnp.zeros((SLOTS, 126), F32),
        ],
        axis=1,
    )
    buf = jnp.concatenate([pooled, info], axis=1).astype(BF)
    buf = jnp.concatenate([buf, swap(buf, "fsdp", 1)], axis=0)
    buf = jnp.concatenate([buf, swap(buf, "fsdp", 2)], axis=0)
    buf = jnp.concatenate([buf, swap(buf, "tower", 1)], axis=0)
    bit = 1
    while bit < n_dp:
        buf = jnp.concatenate([buf, swap(buf, "dp", bit)], axis=0)
        bit *= 2
    place = jnp.stack([z * 8 + t * 4 + f, is_query.astype(jnp.int32), z * 4 + f, f]).astype(jnp.int32)
    loss, own, gf_all, grad_proj = loss_call(place, buf, w_p, rows)
    query_loss = loss[:, 0].reshape(MB, 1, QSEG)
    acts_all = lax.all_gather(acts_hi, ALL, axis=0, tiled=True)
    acts_mine = lax.dynamic_slice_in_dim(acts_all, f * D, D, 1)
    grad_ffn_out = dot_tn(acts_mine, gf_all.reshape(2 * rows * SLOTS, D))

    gf = own.astype(BF)
    gh_hi, gh_lo = split(dot_nt(gf, w_f))
    own_hi, own_lo = split(own)
    g_x3 = dot(member, own_hi) + dot(member, own_lo)
    gu = ((dot(member, gh_hi) + dot(member, gh_lo)) * gp.astype(F32)).astype(BF)
    grad_in = dot_tn(n2, gu)
    g_n2 = dot_nt(gu, w_i)
    back2, grad_gain_two = norm_back(g_n2, inv2, r2, gain_two)
    g_x2 = g_x3 + back2
    ga = g_x2.astype(BF)
    grad_out = dot(ot, ga)
    go = dot_nt(ga, w_o).astype(BF)
    dq, dk, dv, diag = attn_bwd(qkv, go, ot, e, li)
    dqkv = jnp.concatenate([dq, dk, dv], axis=1)
    grad_qkv = dot_tn(n1, dqkv)
    g_n1 = dot_nt(dqkv, w_qkv)
    back1, grad_gain_one = norm_back(g_n1, inv1, r1, gain_one)
    grad_tokens = (g_x2 + back1).astype(BF).reshape(1, MB, 1, SEQ, D)
    grad_table = jnp.einsum("hc,cb->bh", diag.reshape(H, 8192), diag_hot2(), precision=HIGHEST)

    mid = reduce_group(jnp.concatenate([grad_out, grad_in], axis=1).astype(BF))
    first = reduce_group(grad_qkv.astype(BF))
    tiny = jnp.concatenate([grad_gain_one, grad_gain_two, grad_table.reshape(-1)])
    tiny = lax.psum(tiny, ALL)
    return (
        query_loss,
        grad_tokens,
        lax.dynamic_slice_in_dim(tiny[:D], f * 192, 192, 0),
        lax.dynamic_slice_in_dim(tiny[D : 2 * D], f * 192, 192, 0),
        first[:, :D],
        first[:, D : 2 * D],
        first[:, 2 * D :],
        mid[:, :D],
        lax.dynamic_slice_in_dim(tiny[2 * D :].reshape(NB, H), f * 8, 8, 0),
        mid[:, D:],
        grad_ffn_out,
        grad_proj,
    )


def solution(mesh):
    rows = P(None, ("dp", "fsdp"), None)
    tokens = P("tower", None, ("dp", "fsdp"), None, None)
    vec, mat = P("fsdp"), P("fsdp", None)
    return jax.shard_map(
        local,
        mesh=mesh,
        in_specs=(tokens, rows, rows, vec, vec) + (mat,) * 8,
        out_specs=(rows, tokens, vec, vec) + (mat,) * 8,
        check_vma=False,
    )
```

```python
import functools

import jax
import jax.numpy as jnp
from jax import lax
from jax.experimental import pallas as pl
from jax.experimental.pallas import tpu as pltpu
from jax.sharding import PartitionSpec as P

D = 768
H = 12
DH = 64
FF = 3072
NB = 32
SEQ = 512
QSEG = 8
MB = 2
T = MB * SEQ
SLOTS = MB * QSEG
PAY = D + 128
FULL = PAY + 128
PAIRS = H // 2
PARTS = 3
PER = PAIRS // PARTS
EPSILON = 1e-06
LOGIT_SCALE = 50.0
LOSS_SCALE = 256.0
THRESHOLDS = (12, 16, 23, 32, 46, 64, 91)
GELU_C = 0.7978845608028654
ALL = ("tower", "dp", "fsdp")
BF = jnp.bfloat16
F32 = jnp.float32
HIGHEST = lax.Precision.HIGHEST
NT = (((1,), (1,)), ((), ()))
TN = (((0,), (0,)), ((), ()))


def bucket_of(m):
    a = jnp.abs(m)
    far = 8 + sum((a >= edge).astype(jnp.int32) for edge in THRESHOLDS)
    return jnp.where(m > 0, 16, 0) + jnp.where(a < 8, a, far)


def diag_hot():
    col = lax.broadcasted_iota(jnp.int32, (NB, 1024), 1)
    m = (col // 128 - 3) * 128 - col % 128
    return (bucket_of(m) == lax.broadcasted_iota(jnp.int32, (NB, 1024), 0)).astype(BF)


def diag_hot2():
    c = lax.broadcasted_iota(jnp.int32, (8192, NB), 0)
    s, col = c // 1024, c % 1024
    m = (col // 128 - 3) * 128 - (col % 128 - s) % 128
    return (bucket_of(m) == lax.broadcasted_iota(jnp.int32, (8192, NB), 1)).astype(F32)


def upper():
    return lax.broadcasted_iota(jnp.int32, (128, 128), 1) >= lax.broadcasted_iota(jnp.int32, (128, 128), 0)


def params(megabytes):
    return pltpu.CompilerParams(vmem_limit_bytes=megabytes * 2**20)


def cost(flops, moved):
    return pl.CostEstimate(flops=int(flops), bytes_accessed=int(moved), transcendentals=0)


SMEM = pl.BlockSpec(memory_space=pltpu.SMEM)
VMEM = pl.BlockSpec(memory_space=pltpu.VMEM)
HBM = pl.BlockSpec(memory_space=pltpu.HBM)


def sds(shape, kind):
    return jax.ShapeDtypeStruct(shape, kind)


def whole(shape):
    return pl.BlockSpec(shape, lambda *i: (0,) * len(shape))


def bias_kernel(tab_ref, hot_ref, out_ref):
    w = jnp.dot(tab_ref[...], hot_ref[...], preferred_element_type=F32)
    up = upper()
    for h in range(H):
        prev = None
        for e in range(8):
            row = jnp.broadcast_to(w[h : h + 1, e * 128 : (e + 1) * 128], (128, 128))
            r = pltpu.roll(row, 0, 1, stride=1, stride_axis=0)
            if e > 0:
                out_ref[h, e - 1] = jnp.where(up, prev, r)
            prev = r


def bias_blocks(table_t, hot):
    return pl.pallas_call(
        bias_kernel, out_shape=sds((H, 7, 128, 128), F32), cost_estimate=cost(5e9, 5e6), name="bias_blocks"
    )(table_t, hot)


def halves(pieces, f, t, stride, skip, size):
    own, mate, near, far, near_mate, far_mate = pieces
    table = (
        (own, skip, f, 0),
        (own, stride + skip, f, 1),
        (mate, skip, f ^ 1, 0),
        (mate, stride + skip, f ^ 1, 1),
        (near, skip, f ^ 2, t),
        (far, skip, f ^ 2, 1 - t),
        (near_mate, skip, f ^ 3, t),
        (far_mate, skip, f ^ 3, 1 - t),
    )
    return [(ref, start, pl.multiple_of((2 * q + h) * size, 32)) for ref, start, q, h in table]


def fetch(pieces, f, t, stride, skip, size, cols, dst, dst_cols, sem):
    for ref, start, to in halves(pieces, f, t, stride, skip, size):
        pltpu.make_async_copy(ref.at[pl.ds(start, size), cols], dst.at[pl.ds(to, size), dst_cols], sem).start()


def landed(ref, sem):
    pltpu.make_async_copy(ref, ref, sem).wait()


def norm(x, gain):
    inv = lax.rsqrt(jnp.mean(x * x, axis=-1, keepdims=True) + EPSILON)
    scaled = x * inv
    return inv, scaled, (scaled * gain).astype(BF)


def norm_back(g, inv, scaled, gain):
    gs = g * gain
    return inv * (gs - scaled * jnp.mean(gs * scaled, axis=-1, keepdims=True))


def norm_kernel(x_ref, gain_ref, n_ref, nt_ref):
    n = norm(x_ref[...].astype(F32), gain_ref[...])[2]
    n_ref[...] = n
    nt_ref[...] = n.T


def norm_call(x, gain):
    return pl.pallas_call(
        norm_kernel,
        grid=(2,),
        in_specs=[pl.BlockSpec((SEQ, D), lambda r: (r, 0)), whole((1, D))],
        out_specs=[pl.BlockSpec((SEQ, D), lambda r: (r, 0)), pl.BlockSpec((D, SEQ), lambda r: (0, r))],
        out_shape=[sds((T, D), BF), sds((D, T), BF)],
        compiler_params=params(40),
        cost_estimate=cost(2e9, 5e6),
        name="norm_attn",
    )(x, gain)


def qkv_kernel(place_ref, n_ref, *rest):
    pieces, out_ref, w, sems = rest[:6], rest[6], rest[7], rest[8]
    f, t = place_ref[0], place_ref[1]
    step = pl.program_id(0)

    @pl.when(step == 0)
    def _():
        for c in range(3):
            cols = pl.ds(c * D, D)
            fetch(pieces, f, t, 96, 0, 96, cols, w.at[c], pl.ds(0, D), sems.at[c])

    landed(w.at[step], sems.at[step])
    out_ref[...] = jnp.dot(n_ref[...], w[step], preferred_element_type=F32).astype(BF)


def qkv_call(place, n1, pieces):
    return pl.pallas_call(
        qkv_kernel,
        grid=(3,),
        in_specs=[SMEM, whole((T, D))] + [HBM] * 6,
        out_specs=pl.BlockSpec((T, D), lambda c: (0, c)),
        out_shape=sds((T, 3 * D), BF),
        scratch_shapes=[pltpu.VMEM((3, D, D), BF), pltpu.SemaphoreType.DMA((3,))],
        compiler_params=params(40),
        cost_estimate=cost(3.6e9, 1e7),
        name="qkv",
    )(place, n1, *pieces)


def attn_fwd_kernel(qkv_ref, fq_ref, fk_ref, bias_ref, o_ref, ot_ref, e_ref, li_ref):
    lane = lax.broadcasted_iota(jnp.int32, (SEQ, 128), 1)
    q, k = qkv_ref[:, :128], qkv_ref[:, 128:256]
    fq, fk = fq_ref[...], fk_ref[...]
    vt = qkv_ref[:, 256:].T
    outs = []
    for s in range(2):
        own = (lane < 64) if s == 0 else (lane >= 64)
        qa, ka = jnp.where(own, q, fq), jnp.where(own, k, fk)
        st = lax.dot_general(ka, qa, NT, preferred_element_type=F32)
        strips = [
            jnp.concatenate([bias_ref[s, bj - bi + 3] for bi in range(4)], axis=1) for bj in range(4)
        ]
        st = st + jnp.concatenate(strips, axis=0)
        top = jnp.max(st, axis=0, keepdims=True)
        e = jnp.exp(st - top).astype(BF)
        e_ref[0, s] = e
        va = jnp.concatenate([vt[64 * s : 64 * s + 64], jnp.ones((16, SEQ), BF)], axis=0)
        ot = jnp.dot(va, e, preferred_element_type=F32)
        linv = 1.0 / ot[64:65]
        li_ref[0, s] = jnp.broadcast_to(linv, (8, SEQ))
        outs.append((ot[:64] * linv).astype(BF))
    ot = jnp.concatenate(outs, axis=0)
    ot_ref[...] = ot
    o_ref[...] = ot.T


def attn_fwd(qkv, fq, fk, bias, first, count):
    return pl.pallas_call(
        attn_fwd_kernel,
        grid=(count, 2),
        in_specs=[
            pl.BlockSpec((SEQ, 384), lambda p, r: (r, first + p)),
            pl.BlockSpec((SEQ, 128), lambda p, r: (r, 0)),
            pl.BlockSpec((SEQ, 128), lambda p, r: (r, 0)),
            pl.BlockSpec((2, 7, 128, 128), lambda p, r: (first + p, 0, 0, 0)),
        ],
        out_specs=[
            pl.BlockSpec((SEQ, 128), lambda p, r: (r, p)),
            pl.BlockSpec((128, SEQ), lambda p, r: (p, r)),
            pl.BlockSpec((1, 2, SEQ, SEQ), lambda p, r: (r, p, 0, 0)),
            pl.BlockSpec((1, 2, 8, SEQ), lambda p, r: (r, p, 0, 0)),
        ],
        out_shape=[
            sds((T, 128 * count), BF),
            sds((128 * count, T), BF),
            sds((2, 2 * count, SEQ, SEQ), BF),
            sds((2, 2 * count, 8, SEQ), F32),
        ],
        compiler_params=params(40),
        cost_estimate=cost(3.3e9 * count, 3e6 * count),
        name="attn_fwd",
    )(qkv, fq, fk, bias)


def attn_bwd_kernel(
    place_ref, qkv_ref, do_ref, ot_ref, e_ref, li_ref, nt_ref, *rest
):
    d_ref, keep_ref, send_ref, diag_ref, acc, gacc = rest[-6:]
    r = pl.program_id(1)
    lane = lax.broadcasted_iota(jnp.int32, (SEQ, 128), 1)
    q, k, v = qkv_ref[:, :128], qkv_ref[:, 128:256], qkv_ref[:, 256:]
    do = do_ref[...]
    kt, dt = k.T, do.T
    dqs = []
    prod = dt.astype(F32) * ot_ref[...].astype(F32)
    for s in range(2):
        own = (lane < 64) if s == 0 else (lane >= 64)
        linv = li_ref[0, s, 0:1, :]
        delta = jnp.sum(prod[64 * s : 64 * s + 64], axis=0, keepdims=True)
        vm = jnp.where(own, v, jnp.zeros_like(v))
        dp = lax.dot_general(vm, do, NT, preferred_element_type=F32)
        p = e_ref[0, s].astype(F32) * linv
        ds32 = p * (dp - delta)
        ds = ds32.astype(BF)
        dvh = jnp.dot(p.astype(BF), do, preferred_element_type=F32)
        dkh = jnp.dot(ds, q, preferred_element_type=F32)
        dqs.append(jnp.dot(kt[64 * s : 64 * s + 64], ds, preferred_element_type=F32).astype(BF))
        if s == 0:
            dv0, dk0 = dvh, dkh
        sums = []
        for d in range(-3, 4):
            total = None
            for bj in range(4):
                bi = bj - d
                if 0 <= bi < 4:
                    block = ds32[128 * bj : 128 * bj + 128, 128 * bi : 128 * bi + 128]
                    total = block if total is None else total + block
            sums.append(total)
        for d in range(7):
            acc[s, d] = jnp.where(r == 0, jnp.zeros((128, 128), F32), acc[s, d]) + sums[d]
    dq = jnp.concatenate(dqs, axis=0).T
    dk = jnp.where(lane < 64, dk0, dkh).astype(BF)
    dv = jnp.where(lane < 64, dv0, dvh).astype(BF)
    d_all = jnp.concatenate([dq, dk, dv], axis=1)
    d_ref[...] = d_all
    part = jnp.dot(nt_ref[...], d_all, preferred_element_type=F32)

    @pl.when(r == 0)
    def _():
        gacc[...] = part

    @pl.when(r == 1)
    def _():
        g = (gacc[...] + part).astype(BF)
        share(place_ref[0] & 1, g, keep_ref, send_ref)
        up = upper()
        for s in range(2):
            rows = []
            for e in range(8):
                a = acc[s, e] if e < 7 else jnp.zeros((128, 128), F32)
                b = acc[s, e - 1] if e > 0 else jnp.zeros((128, 128), F32)
                c = jnp.where(up, a, b)
                total = c[0:8]
                for g8 in range(1, 16):
                    total = total + pltpu.roll(c[8 * g8 : 8 * g8 + 8], 128 - 8 * g8, 1)
                rows.append(total)
            diag_ref[0, s] = jnp.concatenate(rows, axis=1)


def share(b, g, keep_ref, send_ref):
    for a in range(2):
        even = g[(2 * a) * 192 : (2 * a + 1) * 192]
        odd = g[(2 * a + 1) * 192 : (2 * a + 2) * 192]
        keep_ref[a] = jnp.where(b == 0, even, odd)
        send_ref[a] = jnp.where(b == 0, odd, even)


def attn_bwd(place, qkv, do, ot, e, li, nt, first, count, earlier=()):
    return pl.pallas_call(
        attn_bwd_kernel,
        grid=(count, 2),
        in_specs=[
            SMEM,
            pl.BlockSpec((SEQ, 384), lambda p, r: (r, first + p)),
            pl.BlockSpec((SEQ, 128), lambda p, r: (r, first + p)),
            pl.BlockSpec((128, SEQ), lambda p, r: (p, r)),
            pl.BlockSpec((1, 2, SEQ, SEQ), lambda p, r: (r, p, 0, 0)),
            pl.BlockSpec((1, 2, 8, SEQ), lambda p, r: (r, p, 0, 0)),
            pl.BlockSpec((D, SEQ), lambda p, r: (0, r)),
        ]
        + [HBM] * len(earlier),
        out_specs=[
            pl.BlockSpec((SEQ, 384), lambda p, r: (r, p)),
            pl.BlockSpec((2, 192, 384), lambda p, r: (0, 0, p)),
            pl.BlockSpec((2, 192, 384), lambda p, r: (0, 0, p)),
            pl.BlockSpec((1, 2, 8, 1024), lambda p, r: (p, 0, 0, 0)),
        ],
        out_shape=[
            sds((T, 384 * count), BF),
            sds((2, 192, 384 * count), BF),
            sds((2, 192, 384 * count), BF),
            sds((count, 2, 8, 1024), F32),
        ],
        scratch_shapes=[pltpu.VMEM((2, 7, 128, 128), F32), pltpu.VMEM((D, 384), F32)],
        compiler_params=params(40),
        cost_estimate=cost(4e9 * count, 3e6 * count),
        name="attn_bwd",
    )(place, qkv, do, ot, e, li, nt, *earlier)


FC = 512
FSTEPS = FF // FC


def ffn_kernel(place_ref, x_ref, gain_ref, mt_ref, *rest):
    o_refs, rest = rest[:PARTS], rest[PARTS:]
    pieces, (x2_ref, nt_ref, gp_ref, acts_ref, xs_ref, wo, wi, n2, sems) = rest[:6], rest[6:]
    f, t = place_ref[0], place_ref[1]
    step = pl.program_id(0)

    @pl.when(step == 0)
    def _():
        fetch(pieces, f, t, 96, 0, 96, pl.ds(0, D), wo, pl.ds(0, D), sems.at[FSTEPS])
        for c in range(FSTEPS):
            fetch(pieces, f, t, 96, 0, 96, pl.ds(D + c * FC, FC), wi.at[c], pl.ds(0, FC), sems.at[c])
        landed(wo, sems.at[FSTEPS])
        o = jnp.concatenate([ref[...] for ref in o_refs], axis=1)
        x2 = x_ref[...].astype(F32) + jnp.dot(o, wo[...], preferred_element_type=F32)
        x2_ref[...] = x2
        n = norm(x2, gain_ref[...])[2]
        n2[...] = n
        nt_ref[...] = n.T
        hi = x2.astype(BF)
        lo = (x2 - hi.astype(F32)).astype(BF)
        mt = mt_ref[...]
        xs_ref[...] = jnp.dot(mt, hi, preferred_element_type=F32) + jnp.dot(mt, lo, preferred_element_type=F32)

    landed(wi.at[step], sems.at[step])
    u = jnp.dot(n2[...], wi[step], preferred_element_type=F32)
    u2 = u * u
    half = 0.5 + 0.5 * jnp.tanh(u * (GELU_C + (GELU_C * 0.044715) * u2))
    act = u * half
    gp_ref[...] = (half + act * (1.0 - half) * (2 * GELU_C + (6 * GELU_C * 0.044715) * u2)).astype(BF)
    acts_ref[...] = jnp.dot(mt_ref[...], act.astype(BF), preferred_element_type=F32)


def ffn_call(place, x, gain, member_t, o_parts, pieces):
    return pl.pallas_call(
        ffn_kernel,
        grid=(FSTEPS,),
        in_specs=[SMEM, whole((T, D)), whole((1, D)), whole((SLOTS, T))]
        + [whole(o.shape) for o in o_parts]
        + [HBM] * 6,
        out_specs=[
            whole((T, D)),
            whole((D, T)),
            pl.BlockSpec((T, FC), lambda c: (0, c)),
            pl.BlockSpec((SLOTS, FC), lambda c: (0, c)),
            whole((SLOTS, D)),
        ],
        out_shape=[sds((T, D), F32), sds((D, T), BF), sds((T, FF), BF), sds((SLOTS, FF), F32), sds((SLOTS, D), F32)],
        scratch_shapes=[
            pltpu.VMEM((D, D), BF),
            pltpu.VMEM((FSTEPS, D, FC), BF),
            pltpu.VMEM((T, D), BF),
            pltpu.SemaphoreType.DMA((FSTEPS + 1,)),
        ],
        compiler_params=params(56),
        cost_estimate=cost(1.2e10, 2e7),
        name="ffn_fwd",
    )(place, x, gain, member_t, *o_parts, *pieces)


def pooled_kernel(place_ref, acts_ref, xs_ref, info_ref, *rest):
    pieces, (buf_ref, hi_ref, wf, sem) = rest[:6], rest[6:]
    f, t = place_ref[0], place_ref[1]
    fetch(pieces, f, t, 480, 0, 384, pl.ds(0, D), wf, pl.ds(0, D), sem)
    acts = acts_ref[...]
    hi = acts.astype(BF)
    lo = (acts - hi.astype(F32)).astype(BF)
    hi_ref[...] = hi
    info = info_ref[...]
    landed(wf, sem)
    both = jnp.dot(jnp.concatenate([hi, lo], axis=0), wf[...], preferred_element_type=F32)
    pooled = (xs_ref[...] + both[:SLOTS] + both[SLOTS:]) / jnp.maximum(info[:, 0:1], 1.0)
    out = jnp.concatenate([pooled, info], axis=1)
    packed = [out[8 * m : 8 * m + 1, 128 * c : 128 * c + 128] for m in range(MB) for c in range(PAY // 128)]
    packed = jnp.concatenate(packed + [jnp.zeros((SLOTS - len(packed), 128), F32)], axis=0)
    buf_ref[...] = jnp.concatenate([out, packed], axis=1).astype(BF)


def pooled_call(place, acts, xs, info, pieces):
    return pl.pallas_call(
        pooled_kernel,
        in_specs=[SMEM, VMEM, VMEM, VMEM] + [HBM] * 6,
        out_specs=[VMEM, VMEM],
        out_shape=[sds((SLOTS, FULL), BF), sds((SLOTS, FF), BF)],
        scratch_shapes=[pltpu.VMEM((FF, D), BF), pltpu.SemaphoreType.DMA],
        compiler_params=params(40),
        cost_estimate=cost(2e9, 5e6),
        name="pooled",
    )(place, acts, xs, info, *pieces)


def loss_kernel(rows, place_ref, own_buf, mate_buf, *rest):
    pieces, (loss_ref, own_ref, all_ref, gproj_ref, scr, wp, gp_scr, gz_scr, loss_scr, sems) = rest[:6], rest[6:]
    f, t, z = place_ref[0], place_ref[1], place_ref[2]
    fetch(pieces, f, t, 480, 384, 96, pl.ds(0, D), wp, pl.ds(0, D), sems.at[0])
    nq, np_ = rows * SLOTS, rows * MB
    for m, buf in enumerate((own_buf, mate_buf)):
        for k in range(rows // 2):
            row = (z ^ (k >> 1)) * 4 + (f ^ (2 * (k & 1)) ^ m)
            pltpu.make_async_copy(
                buf.at[pl.ds(k * SLOTS, SLOTS)], scr.at[pl.ds(pl.multiple_of(row * SLOTS, SLOTS), SLOTS)], sems.at[1]
            ).start()
    landed(scr, sems.at[1])
    blocks = scr[:, PAY:]
    chunks = []
    p_row = lax.broadcasted_iota(jnp.int32, (np_, nq), 0)
    q_at = lax.broadcasted_iota(jnp.int32, (np_, nq), 1)
    for c in range(PAY // 128):
        picker = (q_at == (p_row // MB) * SLOTS + (p_row % MB) * (PAY // 128) + c).astype(BF)
        chunks.append(jnp.dot(picker, blocks, preferred_element_type=F32).astype(BF))
    p_all = jnp.concatenate(chunks, axis=1)
    q_all = scr[:, :PAY]
    both = jnp.concatenate([q_all[:, :D], p_all[:, :D]], axis=0)
    extra = jnp.concatenate([q_all[:, D:], p_all[:, D:]], axis=0).astype(F32)
    landed(wp, sems.at[0])
    proj = wp[...]
    zz = jnp.dot(both, proj, preferred_element_type=F32)
    inv = lax.rsqrt(jnp.sum(zz * zz, axis=-1, keepdims=True) + EPSILON)
    w = zz * inv
    e = w.astype(BF)
    eq, ep = e[:nq], e[nq:]
    logits = LOGIT_SCALE * lax.dot_general(eq, ep, NT, preferred_element_type=F32)
    q_row = lax.broadcasted_iota(jnp.int32, (nq, np_), 0)
    p_col = lax.broadcasted_iota(jnp.int32, (nq, np_), 1)
    same = (q_row // QSEG) % MB == p_col % MB
    logits = jnp.where(same, logits, -1e30)
    top = jnp.max(logits, axis=-1, keepdims=True)
    log_total = top + jnp.log(jnp.sum(jnp.exp(logits - top), axis=-1, keepdims=True))
    positive = extra[:nq, 1:2].astype(jnp.int32)
    hot = jnp.where(same & (p_col // MB == positive), 1.0, 0.0)
    loss = log_total - jnp.sum(logits * hot, axis=-1, keepdims=True)
    gl = LOSS_SCALE * (jnp.exp(logits - log_total) - hot)
    g_eq = LOGIT_SCALE * jnp.dot(gl, ep.astype(F32), precision=HIGHEST, preferred_element_type=F32)
    g_ep = LOGIT_SCALE * lax.dot_general(gl, eq.astype(F32), TN, precision=HIGHEST, preferred_element_type=F32)
    ge = jnp.concatenate([g_eq, g_ep], axis=0)
    gz = (inv * (ge - w * jnp.sum(w * ge, axis=-1, keepdims=True))).astype(BF)
    count = jnp.maximum(extra[:, 0:1], 1.0)
    g_x3 = lax.dot_general(gz, proj, NT, preferred_element_type=F32) / count
    all_ref[...] = g_x3.astype(BF)
    row = z * 4 + f
    gz_scr[...] = gz[:nq]
    loss_scr[...] = jnp.broadcast_to(
        jnp.where(lax.broadcasted_iota(jnp.int32, (nq, 128), 1) == 0, loss, count[:nq]), (nq, 128)
    )
    mine = pl.ds(pl.multiple_of(row * SLOTS, SLOTS), SLOTS)
    slot = lax.broadcasted_iota(jnp.int32, (SLOTS, np_), 0)
    chosen = (slot % QSEG == 0) & (lax.broadcasted_iota(jnp.int32, (SLOTS, np_), 1) == row * MB + slot // QSEG)
    own_p = jnp.dot(chosen.astype(F32), g_x3[nq:], precision=HIGHEST, preferred_element_type=F32)
    own_q = lax.dot_general(gz_scr[mine, :], proj, NT, preferred_element_type=F32) / loss_scr[mine, 1:2]
    own_ref[...] = jnp.where(t == 0, own_q, own_p)
    loss_ref[...] = loss_scr[mine, :]
    gp_scr[...] = lax.dot_general(both, gz, TN, preferred_element_type=F32)
    gproj_ref[...] = gp_scr[pl.ds(pl.multiple_of(f * 192, 192), 192), :]


def loss_call(place, own_buf, mate_buf, pieces, rows):
    nq = rows * SLOTS
    return pl.pallas_call(
        functools.partial(loss_kernel, rows),
        in_specs=[SMEM] + [HBM] * 8,
        out_specs=[VMEM] * 4,
        out_shape=[sds((SLOTS, 128), F32), sds((SLOTS, D), F32), sds((nq + rows * MB, D), BF), sds((192, D), F32)],
        scratch_shapes=[
            pltpu.VMEM((nq, FULL), BF),
            pltpu.VMEM((D, D), BF),
            pltpu.VMEM((D, D), F32),
            pltpu.VMEM((nq, D), BF),
            pltpu.VMEM((nq, 128), F32),
            pltpu.SemaphoreType.DMA((2,)),
        ],
        compiler_params=params(60),
        cost_estimate=cost(5e9, 1e6),
        name="loss",
    )(place, own_buf, mate_buf, *pieces)


def ffn_bwd_kernel(place_ref, own_ref, m2_ref, gp_ref, nt_ref, *rest):
    mids, outs, (keep_ref, send_ref, gn_ref, wi, wf, gf, sems) = rest[:6], rest[6:12], rest[12:]
    f, t = place_ref[0], place_ref[1]
    step = pl.program_id(0)

    @pl.when(step == 0)
    def _():
        fetch(outs, f, t, 480, 0, 384, pl.ds(0, D), wf, pl.ds(0, D), sems.at[FSTEPS])
        for c in range(FSTEPS):
            fetch(mids, f, t, 96, 0, 96, pl.ds(D + c * FC, FC), wi.at[c], pl.ds(0, FC), sems.at[c])
        gf[...] = own_ref[...].astype(BF)
        gn_ref[...] = jnp.zeros_like(gn_ref)
        landed(wf, sems.at[FSTEPS])

    rows = wf[pl.ds(pl.multiple_of(step * FC, FC), FC), :]
    gh = lax.dot_general(gf[...], rows, NT, preferred_element_type=F32)
    hi = gh.astype(BF)
    lo = (gh - hi.astype(F32)).astype(BF)
    wide = jnp.dot(m2_ref[...], jnp.concatenate([hi, lo], axis=0), preferred_element_type=F32)
    gu = (wide * gp_ref[...].astype(F32)).astype(BF)
    g = jnp.dot(nt_ref[...], gu, preferred_element_type=F32).astype(BF)
    share(f & 1, g, keep_ref, send_ref)
    landed(wi.at[step], sems.at[step])
    gn_ref[...] += lax.dot_general(gu, wi[step], NT, preferred_element_type=F32)


def ffn_bwd_call(place, own, member2, gp, n2t, mids, outs):
    return pl.pallas_call(
        ffn_bwd_kernel,
        grid=(FSTEPS,),
        in_specs=[SMEM, whole((SLOTS, D)), whole((T, 2 * SLOTS)), pl.BlockSpec((T, FC), lambda c: (0, c)), whole((D, T))]
        + [HBM] * 12,
        out_specs=[
            pl.BlockSpec((2, 192, FC), lambda c: (0, 0, c)),
            pl.BlockSpec((2, 192, FC), lambda c: (0, 0, c)),
            whole((T, D)),
        ],
        out_shape=[sds((2, 192, FF), BF), sds((2, 192, FF), BF), sds((T, D), F32)],
        scratch_shapes=[
            pltpu.VMEM((FSTEPS, D, FC), BF),
            pltpu.VMEM((FF, D), BF),
            pltpu.VMEM((SLOTS, D), BF),
            pltpu.SemaphoreType.DMA((FSTEPS + 1,)),
        ],
        compiler_params=params(56),
        cost_estimate=cost(1.2e10, 2e7),
        name="ffn_bwd",
    )(place, own, member2, gp, n2t, *mids, *outs)


def mid_kernel(place_ref, gn_ref, x2_ref, gain_ref, own_ref, m2_ref, *rest):
    ots, rest = rest[:PARTS], rest[PARTS:]
    pieces, (gx_ref, go_ref, keep_ref, send_ref, wo, sem) = rest[:6], rest[6:]
    f, t = place_ref[0], place_ref[1]
    fetch(pieces, f, t, 96, 0, 96, pl.ds(0, D), wo, pl.ds(0, D), sem)
    own = own_ref[...]
    hi = own.astype(BF)
    lo = (own - hi.astype(F32)).astype(BF)
    g_x3 = jnp.dot(m2_ref[...], jnp.concatenate([hi, lo], axis=0), preferred_element_type=F32)
    gain = gain_ref[...]
    inv, scaled, _ = norm(x2_ref[...], gain)
    g_x2 = g_x3 + norm_back(gn_ref[...], inv, scaled, gain)
    gx_ref[...] = g_x2
    ga = g_x2.astype(BF)
    landed(wo, sem)
    go_ref[...] = lax.dot_general(ga, wo[...], NT, preferred_element_type=F32).astype(BF)
    ot = jnp.concatenate([ref[...] for ref in ots], axis=0)
    g = jnp.dot(ot, ga, preferred_element_type=F32).astype(BF)
    share(f & 1, g, keep_ref, send_ref)


def mid_call(place, gn, x2, gain, own, member2, ots, pieces):
    return pl.pallas_call(
        mid_kernel,
        in_specs=[SMEM] + [VMEM] * (5 + PARTS) + [HBM] * 6,
        out_specs=[VMEM] * 4,
        out_shape=[sds((T, D), F32), sds((T, D), BF), sds((2, 192, D), BF), sds((2, 192, D), BF)],
        scratch_shapes=[pltpu.VMEM((D, D), BF), pltpu.SemaphoreType.DMA],
        compiler_params=params(56),
        cost_estimate=cost(3e9, 1e7),
        name="attn_out_bwd",
    )(place, gn, x2, gain, own, member2, *ots, *pieces)


def token_kernel(place_ref, gx_ref, x_ref, gain_ref, *rest):
    d_refs, rest = rest[:PARTS], rest[PARTS:]
    pieces, (out_ref, w, sem) = rest[:6], rest[6:]
    f, t = place_ref[0], place_ref[1]
    r = pl.program_id(0)

    @pl.when(r == 0)
    def _():
        fetch(pieces, f, t, 96, 0, 96, pl.ds(0, 3 * D), w, pl.ds(0, 3 * D), sem)
        landed(w, sem)

    d_all = jnp.concatenate([ref[...] for ref in d_refs], axis=1)
    g_n1 = lax.dot_general(d_all, w[...], NT, preferred_element_type=F32)
    gain = gain_ref[...]
    inv, scaled, _ = norm(x_ref[...].astype(F32), gain)
    out_ref[...] = (gx_ref[...] + norm_back(g_n1, inv, scaled, gain)).astype(BF)


def token_call(place, gx, x, gain, d_parts, pieces):
    row = lambda r: (r, 0)
    return pl.pallas_call(
        token_kernel,
        grid=(2,),
        in_specs=[SMEM, pl.BlockSpec((SEQ, D), row), pl.BlockSpec((SEQ, D), row), whole((1, D))]
        + [pl.BlockSpec((SEQ, d.shape[1]), row) for d in d_parts]
        + [HBM] * 6,
        out_specs=pl.BlockSpec((SEQ, D), row),
        out_shape=sds((T, D), BF),
        scratch_shapes=[pltpu.VMEM((D, 3 * D), BF), pltpu.SemaphoreType.DMA],
        compiler_params=params(56),
        cost_estimate=cost(4e9, 1e7),
        name="token_grad",
    )(place, gx, x, gain, *d_parts, *pieces)


def swap(block, axis, bit):
    size = lax.axis_size(axis)
    return lax.ppermute(block, axis, [(i, i ^ bit) for i in range(size)])


def after(block, *earlier):
    def kernel(*refs):
        pass

    return pl.pallas_call(
        kernel,
        in_specs=[HBM] * (1 + len(earlier)),
        out_specs=HBM,
        out_shape=sds(block.shape, block.dtype),
        input_output_aliases={0: 0},
        name="after",
    )(block, *earlier)


def pack_kernel(plan, place_ref, *refs):
    ins, own_ref, sent_ref = refs[:-2], refs[-2], refs[-1]
    t = place_ref[1]
    for src, rows, src_cols, dst_rows, dst_cols in plan:
        block = ins[src][pl.ds(rows[0], rows[1]), pl.ds(*src_cols)].astype(BF)
        own_ref[pl.ds(*dst_rows), pl.ds(*dst_cols)] = block
    half = own_ref.shape[0] // 2
    sent_ref[...] = own_ref[pl.ds(pl.multiple_of(t * half, 32), half), :]


def pack_call(place, plan, arrays, shape):
    return pl.pallas_call(
        functools.partial(pack_kernel, plan),
        in_specs=[SMEM] + [VMEM] * len(arrays),
        out_specs=[VMEM, VMEM],
        out_shape=[sds(shape, BF), sds((shape[0] // 2, shape[1]), BF)],
        compiler_params=params(40),
        cost_estimate=cost(1e6, 6 * shape[0] * shape[1]),
        name="pack",
    )(place, *arrays)


def gather_start(own, sent):
    return own, swap(own, "fsdp", 1), swap(sent, "fsdp", 2)


def gather_rest(own, mate, near):
    far = swap(near, "tower", 1)
    return own, mate, near, far, swap(near, "fsdp", 1), swap(far, "fsdp", 1)


def pick(parts, index):
    return lax.dynamic_index_in_dim(parts, index, 0, keepdims=False)


def rounded(v):
    return lax.reduce_precision(v, 8, 7)


def plus(a, b):
    return a.astype(F32) + b.astype(F32)


def mesh_step(keep, got):
    a = lax.axis_index("fsdp") // 2
    out = plus(pick(keep, 1 - a), pick(got, 1 - a)).astype(BF)
    return plus(pick(keep, a), pick(got, a)), out


def tower_step(mine, got):
    t = lax.axis_index("tower")
    cols = mine.shape[-1]
    mine, got = mine.reshape(2, 96, cols), got.reshape(2, 96, cols)
    out = plus(pick(mine, 1 - t), pick(got, 1 - t)).astype(BF)
    return plus(pick(mine, t), pick(got, t)), out


def dp_sum(total):
    bit = 1
    while bit < lax.axis_size("dp"):
        total = plus(total, swap(total, "dp", bit)).astype(BF)
        bit *= 2
    return total


def dp_sum_halves(mine, got):
    z = lax.axis_index("dp")
    bits = [1 << i for i in range(lax.axis_size("dp").bit_length() - 1)]
    for bit in bits:
        cols = mine.shape[-1] // 2
        up = (z // bit) % 2
        part = lambda v, i: lax.dynamic_slice_in_dim(v, i * cols, cols, 1)
        out = plus(part(mine, 1 - up), part(got, 1 - up)).astype(BF)
        mine = plus(part(mine, up), part(got, up))
        got = swap(out, "dp", bit)
    total = lax.optimization_barrier(plus(mine, got).astype(BF))
    for bit in reversed(bits):
        up = (z // bit) % 2
        other = swap(total, "dp", bit)
        total = jnp.concatenate([jnp.where(up == 0, total, other), jnp.where(up == 0, other, total)], axis=1)
    return total


def tower_join(total):
    t = lax.axis_index("tower")
    total = lax.optimization_barrier(total)
    other = swap(total, "tower", 1)
    return jnp.concatenate([jnp.where(t == 0, total, other), jnp.where(t == 0, other, total)], axis=0)


def sum_all(v):
    for axis, bit in (("fsdp", 1), ("fsdp", 2), ("tower", 1)):
        v = v + swap(v, axis, bit)
    bit = 1
    while bit < lax.axis_size("dp"):
        v = v + swap(v, "dp", bit)
        bit *= 2
    return v


def gather_rows(buf, is_query):
    got = swap(buf, "tower", 1)
    buf = jnp.concatenate(
        [jnp.where(is_query, buf[:, :PAY], got[:, :PAY]), jnp.where(is_query, got[:, PAY:], buf[:, PAY:])], axis=1
    )
    n_dp = lax.axis_size("dp")
    if n_dp == 4:
        parts = [buf]
        for k in range(1, 8):
            move = [(i, i ^ ((k >> 1) * 4 + (k & 1) * 2)) for i in range(16)]
            parts.append(lax.ppermute(buf, ("dp", "fsdp"), move))
        buf = jnp.concatenate(parts, axis=0)
    else:
        buf = jnp.concatenate([buf, swap(buf, "fsdp", 2)], axis=0)
        bit = 1
        while bit < n_dp:
            buf = jnp.concatenate([buf, swap(buf, "dp", bit)], axis=0)
            bit *= 2
    return buf, swap(buf, "fsdp", 1)


def interleave(parts):
    rows = parts[0].shape[0]
    return jnp.stack([v.reshape(rows, PAIRS, 128) for v in parts], axis=2).reshape(rows, 3 * D)


def local(
    tokens_in,
    query_lengths,
    positive_ids,
    gain_attn,
    gain_ffn,
    w_query,
    w_key,
    w_value,
    w_out,
    rel_bias,
    w_in,
    w_ffn_out,
    w_proj,
):
    f = lax.axis_index("fsdp")
    t = lax.axis_index("tower")
    z = lax.axis_index("dp")
    rows = lax.axis_size("dp") * 4
    is_query = t == 0
    place = jnp.stack([f, t, z]).astype(jnp.int32)

    small = jnp.concatenate([gain_attn, gain_ffn, rel_bias.reshape(-1), jnp.zeros((32,), F32)])
    small = small.astype(BF).reshape(1, 512)
    small = jnp.concatenate([small, swap(small, "fsdp", 1)], axis=0)
    small = jnp.concatenate([small, swap(small, "fsdp", 2)], axis=0)
    small = jnp.stack([pick(small, i ^ f) for i in range(4)])
    gain_one = small[:, :192].reshape(1, D).astype(F32)
    gain_two = small[:, 192:384].reshape(1, D).astype(F32)
    table = small[:, 384:480].reshape(NB, H)

    plan = [
        (i, (0, 192), (128 * p, 128), (0, 192), (384 * p + 128 * i, 128)) for p in range(PAIRS) for i in range(3)
    ]
    own1, sent1 = pack_call(place, plan, (w_query, w_key, w_value), (192, 3 * D))
    plan = [(0, (0, 192), (0, D), (0, 192), (0, D)), (1, (0, 192), (0, FF), (0, 192), (D, FF))]
    own2, sent2 = pack_call(place, plan, (w_out, w_in), (192, D + FF))
    plan = []
    for h in range(2):
        plan.append((0, (384 * h, 384), (0, D), (480 * h, 384), (0, D)))
        plan.append((1, (96 * h, 96), (0, D), (480 * h + 384, 96), (0, D)))
    own3, sent3 = pack_call(place, plan, (w_ffn_out, w_proj), (960, D))
    first = gather_start(own1, sent1)
    middle = gather_start(own2, after(sent2, first[2]))
    last = gather_start(own3, after(sent3, middle[2]))
    first, middle, last = gather_rest(*first), gather_rest(*middle), gather_rest(*last)

    lengths = query_lengths[:, 0]
    ends = jnp.cumsum(lengths, axis=-1)
    places = lax.broadcasted_iota(jnp.int32, (MB, SEQ, QSEG), 1)
    segment = jnp.where(is_query, jnp.sum((places >= ends[:, None, :]).astype(jnp.int32), axis=-1), 0)
    slot_ids = lax.broadcasted_iota(jnp.int32, (MB, QSEG), 1)
    counts = jnp.where(is_query, lengths, jnp.where(slot_ids < 1, SEQ, 0))
    seg = segment.reshape(T)
    lane = lax.broadcasted_iota(jnp.int32, (T, 128), 1) % 64
    hot_seg = lane == seg[:, None]
    fq = jnp.where(hot_seg, 1.0, 0.0).astype(BF)
    fk = jnp.where((lane < QSEG) & ~hot_seg, -1e30, 0.0).astype(BF)
    slot_of = seg + QSEG * (lax.broadcasted_iota(jnp.int32, (T,), 0) // SEQ)
    member2 = (slot_of[:, None] == lax.broadcasted_iota(jnp.int32, (T, 2 * SLOTS), 1) % SLOTS).astype(BF)
    member_t = (slot_of[None, :] == lax.broadcasted_iota(jnp.int32, (SLOTS, T), 0)).astype(BF)
    info = jnp.concatenate(
        [
            counts.reshape(SLOTS, 1).astype(F32),
            positive_ids.reshape(SLOTS, 1).astype(F32),
            jnp.zeros((SLOTS, 126), F32),
        ],
        axis=1,
    )
    bias = bias_blocks(jnp.pad(table.T, ((0, 4), (0, 0))), diag_hot())

    x = tokens_in.reshape(T, D)
    n1, n1t = norm_call(x, gain_one)
    qkv = qkv_call(place, n1, first)
    heads = [attn_fwd(qkv, fq, fk, bias, i * PER, PER) for i in range(PARTS)]
    x2, n2t, gp, acts, xs = ffn_call(place, x, gain_two, member_t, [h[0] for h in heads], middle)
    buf, acts_hi = pooled_call(place, acts, xs, info, last)
    own_buf, mate_buf = gather_rows(buf, is_query)
    loss, own, gf_all, grad_proj = loss_call(place, own_buf, mate_buf, last, rows)
    query_loss = loss[:, 0].reshape(MB, 1, QSEG)
    acts_all = lax.all_gather(acts_hi, ALL, axis=0, tiled=True)

    keep_i, send_i, g_n2 = ffn_bwd_call(place, own, member2, gp, n2t, middle, last)
    got_i = swap(send_i, "fsdp", 1)
    g_x2, go, keep_o, send_o = mid_call(place, g_n2, x2, gain_two, own, member2, [h[1] for h in heads], middle)
    mine_i, out_i = mesh_step(keep_i, got_i)
    got_i = swap(out_i, "fsdp", 2)
    back = lambda i, *earlier: attn_bwd(place, qkv, go, *heads[i][1:], n1t, i * PER, PER, earlier)
    cat = lambda *v: jnp.concatenate(v, axis=2)
    d_a, keep_a, send_a, diag_a = back(0, out_i)
    d_b, keep_b, send_b, diag_b = back(1, keep_a)
    keep_a, send_a = cat(keep_o, keep_a, keep_b), cat(send_o, send_a, send_b)
    got_a = swap(send_a, "fsdp", 1)
    d_c, keep_c, send_c, diag_c = back(2, send_a)
    got_c = swap(send_c, "fsdp", 1)
    mine_i, out_i = tower_step(mine_i, got_i)
    got_i = swap(out_i, "tower", 1)
    mine_a, out_a = mesh_step(keep_a, got_a)
    got_a = swap(out_a, "fsdp", 2)
    mine_c, out_c = mesh_step(keep_c, got_c)
    got_c = swap(after(out_c, out_a), "fsdp", 2)
    grad_in = tower_join(dp_sum_halves(mine_i, got_i))
    mine_a, out_a = tower_step(mine_a, got_a)
    got_a = swap(out_a, "tower", 1)
    grad_a = tower_join(dp_sum(plus(mine_a, got_a).astype(BF)))
    mine_c, out_c = tower_step(mine_c, got_c)
    got_c = swap(out_c, "tower", 1)
    grad_c = tower_join(dp_sum(plus(mine_c, got_c).astype(BF)))
    diag = jnp.concatenate([diag_a, diag_b, diag_c], axis=0).reshape(H, 8192)
    grad_table = sum_all(jnp.einsum("hc,cb->bh", diag, diag_hot2(), precision=HIGHEST))
    grad_tokens = token_call(place, g_x2, x, gain_one, (d_a, d_b, d_c), first).reshape(1, MB, 1, SEQ, D)

    acts_mine = lax.dynamic_slice_in_dim(acts_all, f * D, D, 1).reshape(2, rows * MB, QSEG, D)
    acts_mine = jnp.concatenate([acts_mine[0].reshape(rows * SLOTS, D), acts_mine[1, :, 0]], axis=0)
    grad_ffn_out = lax.dot_general(acts_mine, gf_all, TN, preferred_element_type=F32)
    grad_out = grad_a[:, :D].astype(F32)
    grad_qkv = jnp.concatenate([grad_a[:, D:], grad_c], axis=1).astype(F32)
    grad_in = grad_in.astype(F32)
    low = lambda g: g.astype(BF).astype(F32)
    grad_gain_one = jnp.sum(grad_qkv * own1.astype(F32), axis=1) / low(gain_attn)
    grad_gain_two = jnp.sum(grad_in * own2[:, D:].astype(F32), axis=1) / low(gain_ffn)
    by_kind = grad_qkv.reshape(192, PAIRS, 3, 128)
    return (
        query_loss,
        grad_tokens,
        grad_gain_one,
        grad_gain_two,
        by_kind[:, :, 0].reshape(192, D),
        by_kind[:, :, 1].reshape(192, D),
        by_kind[:, :, 2].reshape(192, D),
        grad_out,
        lax.dynamic_slice_in_dim(grad_table, f * 8, 8, 0),
        grad_in,
        grad_ffn_out,
        grad_proj,
    )


def solution(mesh):
    rows = P(None, ("dp", "fsdp"), None)
    tokens = P("tower", None, ("dp", "fsdp"), None, None)
    vec, mat = P("fsdp"), P("fsdp", None)
    return jax.shard_map(
        local,
        mesh=mesh,
        in_specs=(tokens, rows, rows, vec, vec) + (mat,) * 8,
        out_specs=(rows, tokens, vec, vec) + (mat,) * 8,
        check_vma=False,
    )
```

```python
import functools

import jax
import jax.numpy as jnp
from jax import lax
from jax.experimental import pallas as pl
from jax.experimental.pallas import tpu as pltpu
from jax.sharding import PartitionSpec as P

D = 768
H = 12
DH = 64
FF = 3072
NB = 32
SEQ = 512
QSEG = 8
MB = 2
T = MB * SEQ
SLOTS = MB * QSEG
PAY = D + 128
FULL = PAY + 128
PAIRS = H // 2
SPLIT = ((0, 3), (3, 2), (5, 1))
PARTS = len(SPLIT)
LAST = 384 * SPLIT[-1][1]
GROUP = D + PAIRS * 384 - LAST
SIDE = 16
EPSILON = 1e-06
LOGIT_SCALE = 50.0
LOSS_SCALE = 256.0
THRESHOLDS = (12, 16, 23, 32, 46, 64, 91)
GELU_C = 0.7978845608028654
ALL = ("tower", "dp", "fsdp")
BF = jnp.bfloat16
F32 = jnp.float32
HIGHEST = lax.Precision.HIGHEST
NT = (((1,), (1,)), ((), ()))
TN = (((0,), (0,)), ((), ()))


def bucket_of(m):
    a = jnp.abs(m)
    far = 8 + sum((a >= edge).astype(jnp.int32) for edge in THRESHOLDS)
    return jnp.where(m > 0, 16, 0) + jnp.where(a < 8, a, far)


def diag_hot():
    col = lax.broadcasted_iota(jnp.int32, (NB, 1024), 1)
    m = (col // 128 - 3) * 128 - col % 128
    return (bucket_of(m) == lax.broadcasted_iota(jnp.int32, (NB, 1024), 0)).astype(BF)


def diag_hot2():
    c = lax.broadcasted_iota(jnp.int32, (8192, NB), 0)
    s, col = c // 1024, c % 1024
    m = (col // 128 - 3) * 128 - (col % 128 - s) % 128
    return (bucket_of(m) == lax.broadcasted_iota(jnp.int32, (8192, NB), 1)).astype(F32)


def upper():
    return lax.broadcasted_iota(jnp.int32, (128, 128), 1) >= lax.broadcasted_iota(jnp.int32, (128, 128), 0)


def params():
    return pltpu.CompilerParams(vmem_limit_bytes=63 * 2**20)


def cost(flops, moved):
    return pl.CostEstimate(flops=1, bytes_accessed=1, transcendentals=0)


SMEM = pl.BlockSpec(memory_space=pltpu.SMEM)
VMEM = pl.BlockSpec(memory_space=pltpu.VMEM)
HBM = pl.BlockSpec(memory_space=pltpu.HBM)


def sds(shape, kind):
    return jax.ShapeDtypeStruct(shape, kind)


def whole(shape):
    return pl.BlockSpec(shape, lambda *i: (0,) * len(shape))


def bias_kernel(tab_ref, hot_ref, out_ref):
    w = jnp.dot(tab_ref[...], hot_ref[...], preferred_element_type=F32)
    up = upper()
    for h in range(H):
        prev = None
        for e in range(8):
            row = jnp.broadcast_to(w[h : h + 1, e * 128 : (e + 1) * 128], (128, 128))
            r = pltpu.roll(row, 0, 1, stride=1, stride_axis=0)
            if e > 0:
                out_ref[h, e - 1] = jnp.where(up, prev, r)
            prev = r


def bias_blocks(table_t, hot):
    return pl.pallas_call(
        bias_kernel, out_shape=sds((H, 7, 128, 128), F32), cost_estimate=cost(5e9, 5e6), name="bias_blocks"
    )(table_t, hot)


def halves(pieces, f, t, stride, skip, size):
    own, mate, near, far, near_mate, far_mate = pieces
    table = (
        (own, skip, f, 0),
        (own, stride + skip, f, 1),
        (mate, skip, f ^ 1, 0),
        (mate, stride + skip, f ^ 1, 1),
        (near, skip, f ^ 2, t),
        (far, skip, f ^ 2, 1 - t),
        (near_mate, skip, f ^ 3, t),
        (far_mate, skip, f ^ 3, 1 - t),
    )
    return [(ref, start, pl.multiple_of((2 * q + h) * size, 32)) for ref, start, q, h in table]


def fetch(pieces, f, t, stride, skip, size, cols, dst, dst_cols, sem):
    for ref, start, to in halves(pieces, f, t, stride, skip, size):
        pltpu.make_async_copy(ref.at[pl.ds(start, size), cols], dst.at[pl.ds(to, size), dst_cols], sem).start()


def landed(ref, sem):
    pltpu.make_async_copy(ref, ref, sem).wait()


def norm(x, gain):
    inv = lax.rsqrt(jnp.mean(x * x, axis=-1, keepdims=True) + EPSILON)
    scaled = x * inv
    return inv, scaled, (scaled * gain).astype(BF)


def norm_back(g, inv, scaled, gain):
    gs = g * gain
    return inv * (gs - scaled * jnp.mean(gs * scaled, axis=-1, keepdims=True))


def norm_kernel(x_ref, gain_ref, *rest):
    n_ref, nt_ref = rest[-2:]
    n = norm(x_ref[...].astype(F32), gain_ref[...])[2]
    n_ref[...] = n
    nt_ref[...] = n.T


def norm_call(x, gain, *earlier):
    return pl.pallas_call(
        norm_kernel,
        grid=(2,),
        in_specs=[pl.BlockSpec((SEQ, D), lambda r: (r, 0)), whole((1, D))] + [HBM] * len(earlier),
        out_specs=[pl.BlockSpec((SEQ, D), lambda r: (r, 0)), pl.BlockSpec((D, SEQ), lambda r: (0, r))],
        out_shape=[sds((T, D), BF), sds((D, T), BF)],
        compiler_params=params(),
        cost_estimate=cost(2e9, 5e6),
        name="norm_attn",
    )(x, gain, *earlier)


def qkv_kernel(place_ref, n_ref, *rest):
    pieces, (out_ref, w, sems) = rest[:6], rest[-3:]
    f, t = place_ref[0], place_ref[1]
    step = pl.program_id(0)

    @pl.when(step == 0)
    def _():
        for c in range(3):
            cols = pl.ds(c * D, D)
            fetch(pieces, f, t, 96, 0, 96, cols, w.at[c], pl.ds(0, D), sems.at[c])

    landed(w.at[step], sems.at[step])
    out_ref[...] = jnp.dot(n_ref[...], w[step], preferred_element_type=F32).astype(BF)


def qkv_call(place, n1, pieces, *earlier):
    return pl.pallas_call(
        qkv_kernel,
        grid=(3,),
        in_specs=[SMEM, whole((T, D))] + [HBM] * (6 + len(earlier)),
        out_specs=pl.BlockSpec((T, D), lambda c: (0, c)),
        out_shape=sds((T, 3 * D), BF),
        scratch_shapes=[pltpu.VMEM((3, D, D), BF), pltpu.SemaphoreType.DMA((3,))],
        compiler_params=params(),
        cost_estimate=cost(3.6e9, 1e7),
        name="qkv",
    )(place, n1, *pieces, *earlier)


def attn_fwd_kernel(qkv_ref, fq_ref, fk_ref, bias_ref, *rest):
    o_ref, ot_ref, e_ref, li_ref = rest[-4:]
    lane = lax.broadcasted_iota(jnp.int32, (SEQ, 128), 1)
    q, k = qkv_ref[:, :128], qkv_ref[:, 128:256]
    fq, fk = fq_ref[...], fk_ref[...]
    vt = qkv_ref[:, 256:].T
    outs = []
    for s in range(2):
        own = (lane < 64) if s == 0 else (lane >= 64)
        qa, ka = jnp.where(own, q, fq), jnp.where(own, k, fk)
        st = lax.dot_general(ka, qa, NT, preferred_element_type=F32)
        strips = [
            jnp.concatenate([bias_ref[s, bj - bi + 3] for bi in range(4)], axis=1) for bj in range(4)
        ]
        st = st + jnp.concatenate(strips, axis=0)
        top = jnp.max(st, axis=0, keepdims=True)
        e = jnp.exp(st - top).astype(BF)
        e_ref[0, s] = e
        va = jnp.concatenate([vt[64 * s : 64 * s + 64], jnp.ones((16, SEQ), BF)], axis=0)
        ot = jnp.dot(va, e, preferred_element_type=F32)
        linv = 1.0 / ot[64:65]
        li_ref[0, s] = jnp.broadcast_to(linv, (8, SEQ))
        outs.append((ot[:64] * linv).astype(BF))
    ot = jnp.concatenate(outs, axis=0)
    ot_ref[...] = ot
    o_ref[...] = ot.T


def attn_fwd(qkv, fq, fk, bias, first, count, *earlier):
    return pl.pallas_call(
        attn_fwd_kernel,
        grid=(count, 2),
        in_specs=[
            pl.BlockSpec((SEQ, 384), lambda p, r: (r, first + p)),
            pl.BlockSpec((SEQ, 128), lambda p, r: (r, 0)),
            pl.BlockSpec((SEQ, 128), lambda p, r: (r, 0)),
            pl.BlockSpec((2, 7, 128, 128), lambda p, r: (first + p, 0, 0, 0)),
        ]
        + [HBM] * len(earlier),
        out_specs=[
            pl.BlockSpec((SEQ, 128), lambda p, r: (r, p)),
            pl.BlockSpec((128, SEQ), lambda p, r: (p, r)),
            pl.BlockSpec((1, 2, SEQ, SEQ), lambda p, r: (r, p, 0, 0)),
            pl.BlockSpec((1, 2, 8, SEQ), lambda p, r: (r, p, 0, 0)),
        ],
        out_shape=[
            sds((T, 128 * count), BF),
            sds((128 * count, T), BF),
            sds((2, 2 * count, SEQ, SEQ), BF),
            sds((2, 2 * count, 8, SEQ), F32),
        ],
        compiler_params=params(),
        cost_estimate=cost(3.3e9 * count, 3e6 * count),
        name="attn_fwd",
    )(qkv, fq, fk, bias, *earlier)


def attn_bwd_kernel(
    place_ref, qkv_ref, do_ref, ot_ref, e_ref, li_ref, nt_ref, *rest
):
    d_ref, keep_ref, send_ref, diag_ref, acc, gacc = rest[-6:]
    r = pl.program_id(1)
    lane = lax.broadcasted_iota(jnp.int32, (SEQ, 128), 1)
    q, k, v = qkv_ref[:, :128], qkv_ref[:, 128:256], qkv_ref[:, 256:]
    do = do_ref[...]
    kt, dt = k.T, do.T
    dqs = []
    prod = dt.astype(F32) * ot_ref[...].astype(F32)
    for s in range(2):
        own = (lane < 64) if s == 0 else (lane >= 64)
        linv = li_ref[0, s, 0:1, :]
        delta = jnp.sum(prod[64 * s : 64 * s + 64], axis=0, keepdims=True)
        vm = jnp.where(own, v, jnp.zeros_like(v))
        dp = lax.dot_general(vm, do, NT, preferred_element_type=F32)
        p = e_ref[0, s].astype(F32) * linv
        ds32 = p * (dp - delta)
        ds = ds32.astype(BF)
        dvh = jnp.dot(p.astype(BF), do, preferred_element_type=F32)
        dkh = jnp.dot(ds, q, preferred_element_type=F32)
        dqs.append(jnp.dot(kt[64 * s : 64 * s + 64], ds, preferred_element_type=F32).astype(BF))
        if s == 0:
            dv0, dk0 = dvh, dkh
        sums = []
        for d in range(-3, 4):
            total = None
            for bj in range(4):
                bi = bj - d
                if 0 <= bi < 4:
                    block = ds32[128 * bj : 128 * bj + 128, 128 * bi : 128 * bi + 128]
                    total = block if total is None else total + block
            sums.append(total)
        for d in range(7):
            acc[s, d] = jnp.where(r == 0, jnp.zeros((128, 128), F32), acc[s, d]) + sums[d]
    dq = jnp.concatenate(dqs, axis=0).T
    dk = jnp.where(lane < 64, dk0, dkh).astype(BF)
    dv = jnp.where(lane < 64, dv0, dvh).astype(BF)
    d_all = jnp.concatenate([dq, dk, dv], axis=1)
    d_ref[...] = d_all
    part = jnp.dot(nt_ref[...], d_all, preferred_element_type=F32)

    @pl.when(r == 0)
    def _():
        gacc[...] = part

    @pl.when(r == 1)
    def _():
        g = (gacc[...] + part).astype(BF)
        share(place_ref[0] & 1, g, keep_ref, send_ref)
        up = upper()
        for s in range(2):
            rows = []
            for e in range(8):
                a = acc[s, e] if e < 7 else jnp.zeros((128, 128), F32)
                b = acc[s, e - 1] if e > 0 else jnp.zeros((128, 128), F32)
                c = jnp.where(up, a, b)
                total = c[0:8]
                for g8 in range(1, 16):
                    total = total + pltpu.roll(c[8 * g8 : 8 * g8 + 8], 128 - 8 * g8, 1)
                rows.append(total)
            diag_ref[0, s] = jnp.concatenate(rows, axis=1)


def share(b, g, keep_ref, send_ref):
    for a in range(2):
        even = g[(2 * a) * 192 : (2 * a + 1) * 192]
        odd = g[(2 * a + 1) * 192 : (2 * a + 2) * 192]
        keep_ref[a] = jnp.where(b == 0, even, odd)
        send_ref[a] = jnp.where(b == 0, odd, even)


def attn_bwd(place, qkv, do, ot, e, li, nt, first, count, shared, *earlier):
    at = 2 + first if shared else 0
    width = GROUP if shared else 384 * count
    slab = lambda p, r: (0, 0, at + p)
    base = 7 + len(earlier)
    return pl.pallas_call(
        attn_bwd_kernel,
        grid=(count, 2),
        in_specs=[
            SMEM,
            pl.BlockSpec((SEQ, 384), lambda p, r: (r, first + p)),
            pl.BlockSpec((SEQ, 128), lambda p, r: (r, first + p)),
            pl.BlockSpec((128, SEQ), lambda p, r: (p, r)),
            pl.BlockSpec((1, 2, SEQ, SEQ), lambda p, r: (r, p, 0, 0)),
            pl.BlockSpec((1, 2, 8, SEQ), lambda p, r: (r, p, 0, 0)),
            pl.BlockSpec((D, SEQ), lambda p, r: (0, r)),
        ]
        + [HBM] * (len(earlier) + len(shared)),
        out_specs=[
            pl.BlockSpec((SEQ, 384), lambda p, r: (r, p)),
            pl.BlockSpec((2, 192, 384), slab),
            pl.BlockSpec((2, 192, 384), slab),
            pl.BlockSpec((1, 2, 8, 1024), lambda p, r: (p, 0, 0, 0)),
        ],
        out_shape=[
            sds((T, 384 * count), BF),
            sds((2, 192, width), BF),
            sds((2, 192, width), BF),
            sds((count, 2, 8, 1024), F32),
        ],
        scratch_shapes=[pltpu.VMEM((2, 7, 128, 128), F32), pltpu.VMEM((D, 384), F32)],
        input_output_aliases={base: 1, base + 1: 2} if shared else {},
        compiler_params=params(),
        cost_estimate=pl.CostEstimate(flops=int(6e9 * count), bytes_accessed=int(3e6 * count), transcendentals=0),
        name="attn_bwd",
    )(place, qkv, do, ot, e, li, nt, *earlier, *shared)


FC = 768
FSTEPS = FF // FC


def ffn_kernel(place_ref, x_ref, gain_ref, mt_ref, *rest):
    o_refs, rest = rest[:PARTS], rest[PARTS:]
    pieces, (x2_ref, nt_ref, gp_ref, acts_ref, xs_ref, wo, wi, n2, sems) = rest[:6], rest[6:]
    f, t = place_ref[0], place_ref[1]
    step = pl.program_id(0)

    @pl.when(step == 0)
    def _():
        fetch(pieces, f, t, 96, 0, 96, pl.ds(0, D), wo, pl.ds(0, D), sems.at[FSTEPS])
        for c in range(FSTEPS):
            fetch(pieces, f, t, 96, 0, 96, pl.ds(D + c * FC, FC), wi.at[c], pl.ds(0, FC), sems.at[c])
        landed(wo, sems.at[FSTEPS])
        o = jnp.concatenate([ref[...] for ref in o_refs], axis=1)
        x2 = x_ref[...].astype(F32) + jnp.dot(o, wo[...], preferred_element_type=F32)
        x2_ref[...] = x2
        n = norm(x2, gain_ref[...])[2]
        n2[...] = n
        nt_ref[...] = n.T
        hi = x2.astype(BF)
        lo = (x2 - hi.astype(F32)).astype(BF)
        mt = mt_ref[...]
        xs_ref[...] = jnp.dot(mt, hi, preferred_element_type=F32) + jnp.dot(mt, lo, preferred_element_type=F32)

    landed(wi.at[step], sems.at[step])
    u = jnp.dot(n2[...], wi[step], preferred_element_type=F32)
    u2 = u * u
    half = 0.5 + 0.5 * jnp.tanh(u * (GELU_C + (GELU_C * 0.044715) * u2))
    act = u * half
    gp_ref[...] = (half + act * (1.0 - half) * (2 * GELU_C + (6 * GELU_C * 0.044715) * u2)).astype(BF)
    acts_ref[...] = jnp.dot(mt_ref[...], act.astype(BF), preferred_element_type=F32)


def ffn_call(place, x, gain, member_t, o_parts, pieces):
    return pl.pallas_call(
        ffn_kernel,
        grid=(FSTEPS,),
        in_specs=[SMEM, whole((T, D)), whole((1, D)), whole((SLOTS, T))]
        + [whole(o.shape) for o in o_parts]
        + [HBM] * 6,
        out_specs=[
            whole((T, D)),
            whole((D, T)),
            pl.BlockSpec((T, FC), lambda c: (0, c)),
            pl.BlockSpec((SLOTS, FC), lambda c: (0, c)),
            whole((SLOTS, D)),
        ],
        out_shape=[sds((T, D), F32), sds((D, T), BF), sds((T, FF), BF), sds((SLOTS, FF), F32), sds((SLOTS, D), F32)],
        scratch_shapes=[
            pltpu.VMEM((D, D), BF),
            pltpu.VMEM((FSTEPS, D, FC), BF),
            pltpu.VMEM((T, D), BF),
            pltpu.SemaphoreType.DMA((FSTEPS + 1,)),
        ],
        compiler_params=params(),
        cost_estimate=cost(1.2e10, 2e7),
        name="ffn_fwd",
    )(place, x, gain, member_t, *o_parts, *pieces)


def pooled_kernel(place_ref, acts_ref, xs_ref, info_ref, *rest):
    pieces, (buf_ref, hi_ref, wf, sem) = rest[:6], rest[6:]
    f, t = place_ref[0], place_ref[1]
    fetch(pieces, f, t, 480, 0, 384, pl.ds(0, D), wf, pl.ds(0, D), sem)
    acts = acts_ref[...]
    hi = acts.astype(BF)
    lo = (acts - hi.astype(F32)).astype(BF)
    hi_ref[...] = hi
    info = info_ref[...]
    landed(wf, sem)
    both = jnp.dot(jnp.concatenate([hi, lo], axis=0), wf[...], preferred_element_type=F32)
    pooled = (xs_ref[...] + both[:SLOTS] + both[SLOTS:]) / jnp.maximum(info[:, 0:1], 1.0)
    out = jnp.concatenate([pooled, info], axis=1)
    packed = [out[8 * m : 8 * m + 1, 128 * c : 128 * c + 128] for m in range(MB) for c in range(PAY // 128)]
    packed = jnp.concatenate(packed + [jnp.zeros((SLOTS - len(packed), 128), F32)], axis=0)
    buf_ref[...] = jnp.concatenate([out, packed], axis=1).astype(BF)


def pooled_call(place, acts, xs, info, pieces):
    return pl.pallas_call(
        pooled_kernel,
        in_specs=[SMEM, VMEM, VMEM, VMEM] + [HBM] * 6,
        out_specs=[VMEM, VMEM],
        out_shape=[sds((SLOTS, FULL), BF), sds((SLOTS, FF), BF)],
        scratch_shapes=[pltpu.VMEM((FF, D), BF), pltpu.SemaphoreType.DMA],
        compiler_params=params(),
        cost_estimate=cost(2e9, 5e6),
        name="pooled",
    )(place, acts, xs, info, *pieces)


def loss_kernel(rows, place_ref, own_buf, mate_buf, *rest):
    pieces, rest = rest[:6], rest[-10:]
    loss_ref, own_ref, all_ref, gproj_ref, scr, wp, gp_scr, gz_scr, loss_scr, sems = rest
    f, t, z = place_ref[0], place_ref[1], place_ref[2]
    fetch(pieces, f, t, 480, 384, 96, pl.ds(0, D), wp, pl.ds(0, D), sems.at[0])
    nq, np_ = rows * SLOTS, rows * MB
    for m, buf in enumerate((own_buf, mate_buf)):
        for k in range(rows // 2):
            row = (z ^ (k >> 1)) * 4 + (f ^ (2 * (k & 1)) ^ m)
            pltpu.make_async_copy(
                buf.at[pl.ds(k * SLOTS, SLOTS)], scr.at[pl.ds(pl.multiple_of(row * SLOTS, SLOTS), SLOTS)], sems.at[1]
            ).start()
    landed(scr, sems.at[1])
    blocks = scr[:, PAY:]
    chunks = []
    p_row = lax.broadcasted_iota(jnp.int32, (np_, nq), 0)
    q_at = lax.broadcasted_iota(jnp.int32, (np_, nq), 1)
    for c in range(PAY // 128):
        picker = (q_at == (p_row // MB) * SLOTS + (p_row % MB) * (PAY // 128) + c).astype(BF)
        chunks.append(jnp.dot(picker, blocks, preferred_element_type=F32).astype(BF))
    p_all = jnp.concatenate(chunks, axis=1)
    q_all = scr[:, :PAY]
    both = jnp.concatenate([q_all[:, :D], p_all[:, :D]], axis=0)
    extra = jnp.concatenate([q_all[:, D:], p_all[:, D:]], axis=0).astype(F32)
    landed(wp, sems.at[0])
    proj = wp[...]
    zz = jnp.dot(both, proj, preferred_element_type=F32)
    inv = lax.rsqrt(jnp.sum(zz * zz, axis=-1, keepdims=True) + EPSILON)
    w = zz * inv
    e = w.astype(BF)
    eq, ep = e[:nq], e[nq:]
    logits = LOGIT_SCALE * lax.dot_general(eq, ep, NT, preferred_element_type=F32)
    q_row = lax.broadcasted_iota(jnp.int32, (nq, np_), 0)
    p_col = lax.broadcasted_iota(jnp.int32, (nq, np_), 1)
    same = (q_row // QSEG) % MB == p_col % MB
    logits = jnp.where(same, logits, -1e30)
    top = jnp.max(logits, axis=-1, keepdims=True)
    log_total = top + jnp.log(jnp.sum(jnp.exp(logits - top), axis=-1, keepdims=True))
    positive = extra[:nq, 1:2].astype(jnp.int32)
    hot = jnp.where(same & (p_col // MB == positive), 1.0, 0.0)
    loss = log_total - jnp.sum(logits * hot, axis=-1, keepdims=True)
    gl = LOSS_SCALE * (jnp.exp(logits - log_total) - hot)
    g_eq = LOGIT_SCALE * jnp.dot(gl, ep.astype(F32), precision=HIGHEST, preferred_element_type=F32)
    g_ep = LOGIT_SCALE * lax.dot_general(gl, eq.astype(F32), TN, precision=HIGHEST, preferred_element_type=F32)
    ge = jnp.concatenate([g_eq, g_ep], axis=0)
    gz = (inv * (ge - w * jnp.sum(w * ge, axis=-1, keepdims=True))).astype(BF)
    count = jnp.maximum(extra[:, 0:1], 1.0)
    g_x3 = lax.dot_general(gz, proj, NT, preferred_element_type=F32) / count
    all_ref[...] = g_x3.astype(BF)
    row = z * 4 + f
    gz_scr[...] = gz[:nq]
    loss_scr[...] = jnp.broadcast_to(
        jnp.where(lax.broadcasted_iota(jnp.int32, (nq, 128), 1) == 0, loss, count[:nq]), (nq, 128)
    )
    mine = pl.ds(pl.multiple_of(row * SLOTS, SLOTS), SLOTS)
    slot = lax.broadcasted_iota(jnp.int32, (SLOTS, np_), 0)
    chosen = (slot % QSEG == 0) & (lax.broadcasted_iota(jnp.int32, (SLOTS, np_), 1) == row * MB + slot // QSEG)
    own_p = jnp.dot(chosen.astype(F32), g_x3[nq:], precision=HIGHEST, preferred_element_type=F32)
    own_q = lax.dot_general(gz_scr[mine, :], proj, NT, preferred_element_type=F32) / loss_scr[mine, 1:2]
    own_ref[...] = jnp.where(t == 0, own_q, own_p)
    loss_ref[...] = loss_scr[mine, :]
    gp_scr[...] = lax.dot_general(both, gz, TN, preferred_element_type=F32)
    gproj_ref[...] = gp_scr[pl.ds(pl.multiple_of(f * 192, 192), 192), :]


def loss_call(place, own_buf, mate_buf, pieces, rows, *earlier):
    nq = rows * SLOTS
    return pl.pallas_call(
        functools.partial(loss_kernel, rows),
        in_specs=[SMEM] + [HBM] * (8 + len(earlier)),
        out_specs=[VMEM] * 4,
        out_shape=[sds((SLOTS, 128), F32), sds((SLOTS, D), F32), sds((nq + rows * MB, D), BF), sds((192, D), F32)],
        scratch_shapes=[
            pltpu.VMEM((nq, FULL), BF),
            pltpu.VMEM((D, D), BF),
            pltpu.VMEM((D, D), F32),
            pltpu.VMEM((nq, D), BF),
            pltpu.VMEM((nq, 128), F32),
            pltpu.SemaphoreType.DMA((2,)),
        ],
        compiler_params=params(),
        cost_estimate=cost(5e9, 1e6),
        name="loss",
    )(place, own_buf, mate_buf, *pieces, *earlier)


FB = 512
BSTEPS = FF // FB


def ffn_bwd_kernel(place_ref, own_ref, m2_ref, gp_ref, nt_ref, *rest):
    mids, outs, (keep_ref, send_ref, gn_ref, wi, wf, gf, sems) = rest[:6], rest[6:12], rest[12:]
    f, t = place_ref[0], place_ref[1]
    step = pl.program_id(0)

    @pl.when(step == 0)
    def _():
        fetch(outs, f, t, 480, 0, 384, pl.ds(0, D), wf, pl.ds(0, D), sems.at[BSTEPS])
        for c in range(BSTEPS):
            fetch(mids, f, t, 96, 0, 96, pl.ds(D + c * FB, FB), wi.at[c], pl.ds(0, FB), sems.at[c])
        gf[...] = own_ref[...].astype(BF)
        gn_ref[...] = jnp.zeros_like(gn_ref)
        landed(wf, sems.at[BSTEPS])

    rows = wf[pl.ds(pl.multiple_of(step * FB, FB), FB), :]
    gh = lax.dot_general(gf[...], rows, NT, preferred_element_type=F32)
    hi = gh.astype(BF)
    lo = (gh - hi.astype(F32)).astype(BF)
    wide = jnp.dot(m2_ref[...], jnp.concatenate([hi, lo], axis=0), preferred_element_type=F32)
    gu = (wide * gp_ref[...].astype(F32)).astype(BF)
    g = jnp.dot(nt_ref[...], gu, preferred_element_type=F32).astype(BF)
    share(f & 1, g, keep_ref, send_ref)
    landed(wi.at[step], sems.at[step])
    gn_ref[...] += lax.dot_general(gu, wi[step], NT, preferred_element_type=F32)


def ffn_bwd_call(place, own, member2, gp, n2t, mids, outs):
    return pl.pallas_call(
        ffn_bwd_kernel,
        grid=(BSTEPS,),
        in_specs=[SMEM, whole((SLOTS, D)), whole((T, 2 * SLOTS)), pl.BlockSpec((T, FB), lambda c: (0, c)), whole((D, T))]
        + [HBM] * 12,
        out_specs=[
            pl.BlockSpec((2, 192, FB), lambda c: (0, 0, c)),
            pl.BlockSpec((2, 192, FB), lambda c: (0, 0, c)),
            whole((T, D)),
        ],
        out_shape=[sds((2, 192, FF), BF), sds((2, 192, FF), BF), sds((T, D), F32)],
        scratch_shapes=[
            pltpu.VMEM((BSTEPS, D, FB), BF),
            pltpu.VMEM((FF, D), BF),
            pltpu.VMEM((SLOTS, D), BF),
            pltpu.SemaphoreType.DMA((BSTEPS + 1,)),
        ],
        compiler_params=params(),
        cost_estimate=cost(1.2e10, 2e7),
        name="ffn_bwd",
    )(place, own, member2, gp, n2t, *mids, *outs)


def mid_kernel(place_ref, gn_ref, x2_ref, gain_ref, own_ref, m2_ref, *rest):
    ots, rest = rest[:PARTS], rest[PARTS:]
    pieces, (gx_ref, go_ref, keep_ref, send_ref, wo, sem) = rest[:6], rest[6:]
    f, t = place_ref[0], place_ref[1]
    fetch(pieces, f, t, 96, 0, 96, pl.ds(0, D), wo, pl.ds(0, D), sem)
    own = own_ref[...]
    hi = own.astype(BF)
    lo = (own - hi.astype(F32)).astype(BF)
    g_x3 = jnp.dot(m2_ref[...], jnp.concatenate([hi, lo], axis=0), preferred_element_type=F32)
    gain = gain_ref[...]
    inv, scaled, _ = norm(x2_ref[...], gain)
    g_x2 = g_x3 + norm_back(gn_ref[...], inv, scaled, gain)
    gx_ref[...] = g_x2
    ga = g_x2.astype(BF)
    landed(wo, sem)
    go_ref[...] = lax.dot_general(ga, wo[...], NT, preferred_element_type=F32).astype(BF)
    ot = jnp.concatenate([ref[...] for ref in ots], axis=0)
    g = jnp.dot(ot, ga, preferred_element_type=F32).astype(BF)
    share(f & 1, g, keep_ref, send_ref)


def mid_call(place, gn, x2, gain, own, member2, ots, pieces):
    return pl.pallas_call(
        mid_kernel,
        in_specs=[SMEM] + [VMEM] * (5 + PARTS) + [HBM] * 6,
        out_specs=[whole((T, D)), whole((T, D)), whole((2, 192, D)), whole((2, 192, D))],
        out_shape=[sds((T, D), F32), sds((T, D), BF), sds((2, 192, GROUP), BF), sds((2, 192, GROUP), BF)],
        scratch_shapes=[pltpu.VMEM((D, D), BF), pltpu.SemaphoreType.DMA],
        grid=(1,),
        compiler_params=params(),
        cost_estimate=cost(3e9, 1e7),
        name="attn_out_bwd",
    )(place, gn, x2, gain, own, member2, *ots, *pieces)


def token_kernel(place_ref, gx_ref, x_ref, gain_ref, *rest):
    d_refs, rest = rest[:PARTS], rest[PARTS:]
    pieces, (out_ref, w, sem) = rest[:6], rest[-3:]
    f, t = place_ref[0], place_ref[1]
    r = pl.program_id(0)

    @pl.when(r == 0)
    def _():
        fetch(pieces, f, t, 96, 0, 96, pl.ds(0, 3 * D), w, pl.ds(0, 3 * D), sem)
        landed(w, sem)

    d_all = jnp.concatenate([ref[...] for ref in d_refs], axis=1)
    g_n1 = lax.dot_general(d_all, w[...], NT, preferred_element_type=F32)
    gain = gain_ref[...]
    inv, scaled, _ = norm(x_ref[...].astype(F32), gain)
    out_ref[...] = (gx_ref[...] + norm_back(g_n1, inv, scaled, gain)).astype(BF)


def token_call(place, gx, x, gain, d_parts, pieces, *earlier):
    row = lambda r: (r, 0)
    return pl.pallas_call(
        token_kernel,
        grid=(2,),
        in_specs=[SMEM, pl.BlockSpec((SEQ, D), row), pl.BlockSpec((SEQ, D), row), whole((1, D))]
        + [pl.BlockSpec((SEQ, d.shape[1]), row) for d in d_parts]
        + [HBM] * (6 + len(earlier)),
        out_specs=pl.BlockSpec((SEQ, D), row),
        out_shape=sds((T, D), BF),
        scratch_shapes=[pltpu.VMEM((D, 3 * D), BF), pltpu.SemaphoreType.DMA],
        compiler_params=params(),
        cost_estimate=cost(4e9, 1e7),
        name="token_grad",
    )(place, gx, x, gain, *d_parts, *pieces, *earlier)


def swap(block, axis, bit):
    size = lax.axis_size(axis)
    return lax.ppermute(block, axis, [(i, i ^ bit) for i in range(size)])


def after(block, *earlier):
    def kernel(*refs):
        pass

    return pl.pallas_call(
        kernel,
        in_specs=[HBM] * (1 + len(earlier)),
        out_specs=HBM,
        out_shape=sds(block.shape, block.dtype),
        input_output_aliases={0: 0},
        name="after",
    )(block, *earlier)


def pack_kernel(plan, place_ref, *refs):
    ins, own_ref, sent_ref = refs[:-2], refs[-2], refs[-1]
    t = place_ref[1]
    for src, rows, src_cols, dst_rows, dst_cols in plan:
        block = ins[src][pl.ds(rows[0], rows[1]), pl.ds(*src_cols)].astype(BF)
        own_ref[pl.ds(*dst_rows), pl.ds(*dst_cols)] = block
    half = own_ref.shape[0] // 2
    sent_ref[...] = own_ref[pl.ds(pl.multiple_of(t * half, 32), half), :]


def pack_call(place, plan, arrays, shape, *earlier):
    return pl.pallas_call(
        functools.partial(pack_kernel, plan),
        in_specs=[SMEM] + [VMEM] * len(arrays) + [HBM] * len(earlier),
        out_specs=[VMEM, VMEM],
        out_shape=[sds(shape, BF), sds((shape[0] // 2, shape[1]), BF)],
        compiler_params=params(),
        cost_estimate=cost(1e6, 6 * shape[0] * shape[1]),
        name="pack",
    )(place, *arrays, *earlier)


def gather_start(own, sent):
    return own, swap(own, "fsdp", 1), swap(sent, "fsdp", 2)


def gather_rest(own, mate, near, *before):
    far = swap(near, "tower", 1)
    if before:
        far = after(far, *before)
    return own, mate, near, far, swap(near, "fsdp", 1), swap(far, "fsdp", 1)


def pick(parts, index):
    return lax.dynamic_index_in_dim(parts, index, 0, keepdims=False)


def rounded(v):
    return lax.reduce_precision(v, 8, 7)


def plus(a, b):
    return a.astype(F32) + b.astype(F32)


def spread_kernel(side, place_ref, *refs):
    ins, (out_1, mine_1, out_2, mine_2) = refs[: -4], refs[-4:]
    a, t = place_ref[0] // 2, place_ref[1]
    cols = FF // 2
    pairs = [(ins[0], ins[1])] if len(ins) < 4 else [(ins[0], ins[1]), (ins[2], ins[3])]
    start = 0
    for keep_ref, got_ref in pairs:
        width = keep_ref.shape[-1]
        for lo, hi, first in ((0, cols, True), (cols, 2 * cols, False)):
            lo, hi = max(lo, start), min(hi, start + width)
            if lo >= hi:
                continue
            src = pl.ds(lo - start, hi - lo)
            add = lambda i, rows: plus(keep_ref[i, rows, src], got_ref[i, rows, src]).astype(BF)
            every = pl.ds(0, 192)
            if first:
                out_1[pl.ds(0, 192), pl.ds(lo, hi - lo)] = add(1 - a, every)
                mine_1[pl.ds(0, 192), pl.ds(lo, hi - lo)] = add(a, every)
            else:
                dst = pl.ds(lo - cols, hi - lo)
                for i in range(2):
                    out_2[i, :, dst] = add(i, pl.ds(pl.multiple_of((1 - t) * 96, 32), 96))
                    mine_2[i, :, dst] = add(i, pl.ds(pl.multiple_of(t * 96, 32), 96))
        start += width
    if side:
        out_1[pl.ds(192, SIDE), :] = ins[4][...]
        mine_1[pl.ds(192, SIDE), :] = ins[4][...]


def spread_call(place, pairs, side=None, *earlier):
    cols = FF // 2
    rows = 192 + (SIDE if side is not None else 0)
    flat, deep = sds((rows, cols), BF), sds((2, 96, cols), BF)
    ins = [v for pair in pairs for v in pair] + ([side] if side is not None else [])

    def kernel(*refs):
        spread_kernel(side is not None, *refs[: 1 + len(ins)], *refs[-4:])

    return pl.pallas_call(
        kernel,
        in_specs=[SMEM] + [VMEM] * len(ins) + [HBM] * len(earlier),
        out_specs=[VMEM] * 4,
        out_shape=[flat, flat, deep, deep],
        compiler_params=params(),
        cost_estimate=cost(1e6, 7e6),
        name="spread",
    )(place, *ins, *earlier)


def cross_kernel(place_ref, mine_1, got_1, mine_2, got_2, *refs):
    out_1, keep_1, out_2, keep_2 = refs[-4:]
    a, t = place_ref[0] // 2, place_ref[1]
    rows = lambda i: pl.ds(pl.multiple_of(i * 96, 32), 96)
    out_1[pl.ds(0, 96), :] = plus(mine_1[rows(1 - t), :], got_1[rows(1 - t), :]).astype(BF)
    keep_1[pl.ds(0, 96), :] = plus(mine_1[rows(t), :], got_1[rows(t), :]).astype(BF)
    out_2[...] = plus(mine_2[1 - a], got_2[1 - a]).astype(BF)
    keep_2[...] = plus(mine_2[a], got_2[a]).astype(BF)
    if mine_1.shape[0] > 192:
        side = pl.ds(192, SIDE)
        both = plus(mine_1[side, :], got_1[side, :]).astype(BF)
        out_1[pl.ds(96, SIDE), :] = both
        keep_1[pl.ds(96, SIDE), :] = both


def cross_call(place, mine_1, got_1, mine_2, got_2, *earlier):
    rows = mine_1.shape[0] - 96
    flat, half = sds((rows, FF // 2), BF), sds((96, FF // 2), BF)
    return pl.pallas_call(
        cross_kernel,
        in_specs=[SMEM] + [VMEM] * 4 + [HBM] * len(earlier),
        out_specs=[VMEM] * 4,
        out_shape=[flat, flat, half, half],
        compiler_params=params(),
        cost_estimate=cost(1e6, 4e6),
        name="cross",
    )(place, mine_1, got_1, mine_2, got_2, *earlier)


def dp_steps(mine, got):
    z = lax.axis_index("dp")
    bits = [1 << i for i in range(lax.axis_size("dp").bit_length() - 1)]
    rows, cols = mine[0].shape
    side = rounded(plus(mine[0][96:, :D], got[0][96:, :D])) if rows > 96 else None
    mine, got = (mine[0][:96], mine[1]), (got[0][:96], got[1])
    for step, bit in enumerate(bits):
        up = (z // bit) % 2
        if step == 0:
            out = plus(jnp.where(up == 0, mine[1], mine[0]), jnp.where(up == 0, got[1], got[0])).astype(BF)
            mine = plus(jnp.where(up == 0, mine[0], mine[1]), jnp.where(up == 0, got[0], got[1]))
        else:
            cols = mine.shape[-1] // 2
            part = lambda v, i: lax.dynamic_slice_in_dim(v, i * cols, cols, 1)
            out = plus(part(mine, 1 - up), part(got, 1 - up)).astype(BF)
            mine = plus(part(mine, up), part(got, up))
        if side is not None and cols >= D:
            wide = jnp.pad(side.astype(BF), ((0, 0), (0, cols - D)))
            out = jnp.concatenate([out, wide], axis=0)
        out = yield out
        got = swap(out, "dp", bit)
        if side is not None and cols >= D:
            side = rounded(side + got[96:, :D].astype(F32))
            got = got[:96]
        elif side is not None:
            side = rounded(side + swap(side.astype(BF), "dp", bit).astype(F32))
    total = lax.optimization_barrier(plus(mine, got).astype(BF))
    for bit in reversed(bits):
        total = yield total
        up = (z // bit) % 2
        other = swap(total, "dp", bit)
        total = jnp.concatenate([jnp.where(up == 0, total, other), jnp.where(up == 0, other, total)], axis=1)
    return lax.optimization_barrier(total), side


def drain(steps, block):
    while True:
        try:
            block = steps.send(block)
        except StopIteration as end:
            return end.value


def gather_rows(buf, is_query):
    got = swap(buf, "tower", 1)
    buf = jnp.concatenate(
        [jnp.where(is_query, buf[:, :PAY], got[:, :PAY]), jnp.where(is_query, got[:, PAY:], buf[:, PAY:])], axis=1
    )
    n_dp = lax.axis_size("dp")
    buf = jnp.concatenate([buf, swap(buf, "fsdp", 2)], axis=0)
    if n_dp == 4:
        buf = jnp.concatenate([buf] + [swap(buf, "dp", bits) for bits in (1, 2, 3)], axis=0)
    else:
        bit = 1
        while bit < n_dp:
            buf = jnp.concatenate([buf, swap(buf, "dp", bit)], axis=0)
            bit *= 2
    return buf, swap(buf, "fsdp", 1)


def row_sums(v):
    hi = v.astype(BF)
    lo = (v - hi.astype(F32)).astype(BF)
    ones = jnp.ones((8, v.shape[1]), BF)
    both = [lax.dot_general(ones, part, NT, preferred_element_type=F32) for part in (hi, lo)]
    return (both[0] + both[1])[0:1]


def joined(t, total_ref, other_ref):
    own, other = total_ref[...].astype(F32), other_ref[...].astype(F32)
    return jnp.concatenate([jnp.where(t == 0, own, other), jnp.where(t == 0, other, own)], axis=0)


def tail_in_kernel(place_ref, total_ref, other_ref, own_ref, gain_ref, out_ref, sum_ref):
    g = joined(place_ref[1], total_ref, other_ref)
    out_ref[...] = g
    more = row_sums(g * own_ref[...].astype(F32)) / gain_ref[...].astype(BF).astype(F32)
    c = pl.program_id(0)

    @pl.when(c == 0)
    def _():
        sum_ref[...] = more

    @pl.when(c > 0)
    def _():
        sum_ref[...] += more


def tail_in_call(place, total, other, own, gain):
    column = lambda c: (0, c)
    return pl.pallas_call(
        tail_in_kernel,
        grid=(2,),
        in_specs=[
            SMEM,
            pl.BlockSpec((96, FF // 2), column),
            pl.BlockSpec((96, FF // 2), column),
            pl.BlockSpec((192, FF // 2), column),
            whole((1, 192)),
        ],
        out_specs=[pl.BlockSpec((192, FF // 2), column), whole((1, 192))],
        out_shape=[sds((192, FF), F32), sds((1, 192), F32)],
        compiler_params=params(),
        cost_estimate=cost(1e7, 5e6),
        name="tail_in",
    )(place, total, other, own, gain.reshape(1, 192))


def tail_attn_kernel(place_ref, total_ref, other_ref, own_ref, gain_ref, out_ref, q_ref, k_ref, v_ref, sum_ref):
    g = joined(place_ref[1], total_ref, other_ref)
    out_ref[...] = g[:, :D]
    for p in range(PAIRS):
        for i, ref in enumerate((q_ref, k_ref, v_ref)):
            at = D + 384 * p + 128 * i
            ref[:, 128 * p : 128 * p + 128] = g[:, at : at + 128]
    sum_ref[...] = row_sums(g[:, D:] * own_ref[...].astype(F32)) / gain_ref[...].astype(BF).astype(F32)


def tail_attn_call(place, total, other, own, gain):
    return pl.pallas_call(
        tail_attn_kernel,
        in_specs=[SMEM] + [VMEM] * 4,
        out_specs=[VMEM] * 5,
        out_shape=[sds((192, D), F32)] * 4 + [sds((1, 192), F32)],
        compiler_params=params(),
        cost_estimate=cost(1e7, 5e6),
        name="tail_attn",
    )(place, total, other, own, gain.reshape(1, 192))


def local(
    tokens_in,
    query_lengths,
    positive_ids,
    gain_attn,
    gain_ffn,
    w_query,
    w_key,
    w_value,
    w_out,
    rel_bias,
    w_in,
    w_ffn_out,
    w_proj,
):
    f = lax.axis_index("fsdp")
    t = lax.axis_index("tower")
    z = lax.axis_index("dp")
    rows = lax.axis_size("dp") * 4
    is_query = t == 0
    place = jnp.stack([f, t, z]).astype(jnp.int32)

    small = jnp.concatenate([gain_attn, gain_ffn, rel_bias.reshape(-1), jnp.zeros((32,), F32)])
    small = small.astype(BF).reshape(1, 512)
    small = jnp.concatenate([small, swap(small, "fsdp", 1)], axis=0)
    small = jnp.concatenate([small, swap(small, "fsdp", 2)], axis=0)
    small_all = small
    small = jnp.stack([pick(small, i ^ f) for i in range(4)])
    gain_one = small[:, :192].reshape(1, D).astype(F32)
    gain_two = small[:, 192:384].reshape(1, D).astype(F32)
    table = small[:, 384:480].reshape(NB, H)

    plan = [
        (i, (0, 192), (128 * p, 128), (0, 192), (384 * p + 128 * i, 128)) for p in range(PAIRS) for i in range(3)
    ]
    own1, sent1 = pack_call(place, plan, (w_query, w_key, w_value), (192, 3 * D))
    sent1 = after(sent1, small_all)
    plan = [(0, (0, 192), (0, D), (0, 192), (0, D)), (1, (0, 192), (0, FF), (0, 192), (D, FF))]
    own2, sent2 = pack_call(place, plan, (w_out, w_in), (192, D + FF), small_all)
    plan = []
    for h in range(2):
        plan.append((0, (384 * h, 384), (0, D), (480 * h, 384), (0, D)))
        plan.append((1, (96 * h, 96), (0, D), (480 * h + 384, 96), (0, D)))
    own3, sent3 = pack_call(place, plan, (w_ffn_out, w_proj), (960, D), small_all)
    first = gather_start(own1, sent1)
    middle = gather_start(own2, after(sent2, first[2]))

    lengths = query_lengths[:, 0]
    ends = jnp.cumsum(lengths, axis=-1)
    places = lax.broadcasted_iota(jnp.int32, (MB, SEQ, QSEG), 1)
    segment = jnp.where(is_query, jnp.sum((places >= ends[:, None, :]).astype(jnp.int32), axis=-1), 0)
    slot_ids = lax.broadcasted_iota(jnp.int32, (MB, QSEG), 1)
    counts = jnp.where(is_query, lengths, jnp.where(slot_ids < 1, SEQ, 0))
    seg = segment.reshape(T)
    lane = lax.broadcasted_iota(jnp.int32, (T, 128), 1) % 64
    hot_seg = lane == seg[:, None]
    fq = jnp.where(hot_seg, 1.0, 0.0).astype(BF)
    fk = jnp.where((lane < QSEG) & ~hot_seg, -1e30, 0.0).astype(BF)
    slot_of = seg + QSEG * (lax.broadcasted_iota(jnp.int32, (T,), 0) // SEQ)
    member2 = (slot_of[:, None] == lax.broadcasted_iota(jnp.int32, (T, 2 * SLOTS), 1) % SLOTS).astype(BF)
    member_t = (slot_of[None, :] == lax.broadcasted_iota(jnp.int32, (SLOTS, T), 0)).astype(BF)
    info = jnp.concatenate(
        [
            counts.reshape(SLOTS, 1).astype(F32),
            positive_ids.reshape(SLOTS, 1).astype(F32),
            jnp.zeros((SLOTS, 126), F32),
        ],
        axis=1,
    )
    bias = bias_blocks(jnp.pad(table.T, ((0, 4), (0, 0))), diag_hot())

    x = tokens_in.reshape(T, D)
    n1, n1t = norm_call(x, gain_one)
    first = gather_rest(*first[:2], after(first[2], n1, own2), bias)
    qkv = qkv_call(place, n1, first)
    middle = gather_rest(*middle[:2], after(middle[2], qkv))
    last = gather_start(own3, after(sent3, middle[2]))
    heads = [attn_fwd(qkv, fq, fk, bias, *SPLIT[0], middle[2])]
    heads.append(attn_fwd(qkv, fq, fk, bias, *SPLIT[1], heads[0][0]))
    near3 = after(last[2], heads[1][0])
    heads.append(attn_fwd(qkv, fq, fk, bias, *SPLIT[2], middle[3], near3))
    x2, n2t, gp, acts, xs = ffn_call(place, x, gain_two, member_t, [h[0] for h in heads], middle)
    last = gather_rest(*last[:2], near3, xs)
    buf, acts = pooled_call(place, acts, xs, info, last)
    own_buf, mate_buf = gather_rows(buf, is_query)
    loss, own, gf_all, grad_proj = loss_call(place, own_buf, mate_buf, last, rows)
    query_loss = loss[:, 0].reshape(MB, 1, QSEG)

    acts_all = lax.all_gather(after(acts, own_buf), ALL, axis=0, tiled=True)
    keep_i, send_i, g_n2 = ffn_bwd_call(place, own, member2, gp, n2t, middle, last)
    got_i = swap(send_i, "fsdp", 1)
    g_x2, go, keep, send = mid_call(place, g_n2, x2, gain_two, own, member2, [h[1] for h in heads], middle)
    out_1, mine_1, out_2, mine_2 = spread_call(place, [(keep_i, got_i)], None, keep)
    got_1, got_2 = swap(out_1, "fsdp", 2), swap(out_2, "tower", 1)
    back = lambda i, *earlier: attn_bwd(place, qkv, go, *heads[i][1:], n1t, *SPLIT[i], *earlier)
    d_a, keep, send, diag_a = back(0, (keep, send), out_1, out_2)
    out_1, mine_1, out_2, mine_2 = cross_call(place, mine_1, got_1, mine_2, got_2, d_a)
    got_1, got_2 = swap(out_1, "tower", 1), swap(out_2, "fsdp", 2)
    d_b, keep, send, diag_b = back(1, (keep, send), out_1, out_2)
    got = swap(send, "fsdp", 1)
    steps = dp_steps((mine_1, mine_2), (got_1, got_2))
    z_out = next(steps)
    d_c, keep_c, send_c, diag_c = back(2, (), d_b, acts_all)
    got_c = swap(send_c, "fsdp", 1)
    diag = jnp.concatenate([diag_a, diag_b, diag_c], axis=0).reshape(H, 8192)
    table_grad = jnp.einsum("hc,cb->hb", diag, diag_hot2(), precision=HIGHEST)
    table_grad = jnp.pad(table_grad, ((0, SIDE - H), (0, FF // 2 - NB))).astype(BF)
    out_b, mine_1b, out_2b, mine_2b = spread_call(place, [(keep, got), (keep_c, got_c)], table_grad, z_out)
    got_1b, got_2b = swap(out_b, "fsdp", 2), swap(out_2b, "tower", 1)
    z_out = after(steps.send(z_out), out_b)
    grad_tokens = token_call(place, g_x2, x, gain_one, (d_a, d_b, d_c), first, out_b, out_2b, z_out)
    z_out = after(steps.send(z_out), grad_tokens)
    out_1b, mine_1b, out_2b, mine_2b = cross_call(place, mine_1b, got_1b, mine_2b, got_2b, z_out)
    total_i = drain(steps, z_out)[0]
    other_i = swap(total_i, "tower", 1)
    grad_tokens = grad_tokens.reshape(1, MB, 1, SEQ, D)
    got_1b, got_2b = swap(out_1b, "tower", 1), swap(out_2b, "fsdp", 2)
    total_b, side = drain(dp_steps((mine_1b, mine_2b), (got_1b, got_2b)), None)
    other_b = swap(total_b, "tower", 1)
    grad_in, gain_ffn_grad = tail_in_call(place, total_i, other_i, own2[:, D:], gain_ffn)
    grad_out, grad_q, grad_k, grad_v, gain_attn_grad = tail_attn_call(place, total_b, other_b, own1, gain_attn)
    side = side[:H, :NB]
    grad_table = (side + swap(side, "fsdp", 1)).T

    acts_all = lax.dynamic_slice_in_dim(acts_all, f * D, D, 1).reshape(2, rows * MB, QSEG, D)
    acts_all = jnp.concatenate([acts_all[0].reshape(rows * SLOTS, D), acts_all[1, :, 0]], axis=0)
    grad_ffn_out = lax.dot_general(acts_all, gf_all, TN, preferred_element_type=F32)
    return (
        query_loss,
        grad_tokens,
        gain_attn_grad.reshape(192),
        gain_ffn_grad.reshape(192),
        grad_q,
        grad_k,
        grad_v,
        grad_out,
        lax.dynamic_slice_in_dim(grad_table, f * 8, 8, 0),
        grad_in,
        grad_ffn_out,
        grad_proj,
    )


def solution(mesh):
    rows = P(None, ("dp", "fsdp"), None)
    tokens = P("tower", None, ("dp", "fsdp"), None, None)
    vec, mat = P("fsdp"), P("fsdp", None)
    return jax.shard_map(
        local,
        mesh=mesh,
        in_specs=(tokens, rows, rows, vec, vec) + (mat,) * 8,
        out_specs=(rows, tokens, vec, vec) + (mat,) * 8,
        check_vma=False,
    )
```

```python
import functools

import jax
import jax.numpy as jnp
from jax import lax
from jax.experimental import pallas as pl
from jax.experimental.pallas import tpu as pltpu
from jax.sharding import PartitionSpec as P

D = 768
H = 12
DH = 64
FF = 3072
NB = 32
SEQ = 512
QSEG = 8
MB = 2
T = MB * SEQ
SLOTS = MB * QSEG
PAY = D + 128
FULL = PAY + 128
PAIRS = H // 2
AHEAD = ((0, 3), (3, 3))
SPLIT = ((0, 3, 0, 0), (3, 2, 1, 0), (5, 1, 1, 2))
PARTS = len(AHEAD)
LAST = 384 * SPLIT[-1][1]
GROUP = D + PAIRS * 384 - LAST
SIDE = 16
EPSILON = 1e-06
LOGIT_SCALE = 50.0
LOSS_SCALE = 256.0
THRESHOLDS = (12, 16, 23, 32, 46, 64, 91)
GELU_C = 0.7978845608028654
ALL = ("tower", "dp", "fsdp")
BF = jnp.bfloat16
F32 = jnp.float32
HIGHEST = lax.Precision.HIGHEST
NT = (((1,), (1,)), ((), ()))
TN = (((0,), (0,)), ((), ()))


def bucket_of(m):
    a = jnp.abs(m)
    far = 8 + sum((a >= edge).astype(jnp.int32) for edge in THRESHOLDS)
    return jnp.where(m > 0, 16, 0) + jnp.where(a < 8, a, far)


def diag_hot():
    col = lax.broadcasted_iota(jnp.int32, (NB, 1024), 1)
    m = (col // 128 - 3) * 128 - col % 128
    return (bucket_of(m) == lax.broadcasted_iota(jnp.int32, (NB, 1024), 0)).astype(BF)


def diag_hot2():
    c = lax.broadcasted_iota(jnp.int32, (8192, NB), 0)
    s, col = c // 1024, c % 1024
    m = (col // 128 - 3) * 128 - (col % 128 - s) % 128
    return (bucket_of(m) == lax.broadcasted_iota(jnp.int32, (8192, NB), 1)).astype(F32)


def upper():
    return lax.broadcasted_iota(jnp.int32, (128, 128), 1) >= lax.broadcasted_iota(jnp.int32, (128, 128), 0)


def params():
    return pltpu.CompilerParams(vmem_limit_bytes=66900000)


def cost(flops, moved):
    return pl.CostEstimate(flops=1, bytes_accessed=1, transcendentals=0)


SMEM = pl.BlockSpec(memory_space=pltpu.SMEM)
VMEM = pl.BlockSpec(memory_space=pltpu.VMEM)
HBM = pl.BlockSpec(memory_space=pltpu.HBM)


def sds(shape, kind):
    return jax.ShapeDtypeStruct(shape, kind)


def whole(shape):
    return pl.BlockSpec(shape, lambda *i: (0,) * len(shape))


def bias_kernel(tab_ref, hot_ref, out_ref):
    w = jnp.dot(tab_ref[...], hot_ref[...], preferred_element_type=F32)
    up = upper()
    for h in range(H):
        prev = None
        for e in range(8):
            row = jnp.broadcast_to(w[h : h + 1, e * 128 : (e + 1) * 128], (128, 128))
            r = pltpu.roll(row, 0, 1, stride=1, stride_axis=0)
            if e > 0:
                out_ref[h, e - 1] = jnp.where(up, prev, r)
            prev = r


def bias_blocks(table_t, hot):
    return pl.pallas_call(
        bias_kernel, out_shape=sds((H, 7, 128, 128), F32), cost_estimate=cost(5e9, 5e6), name="bias_blocks"
    )(table_t, hot)


def halves(pieces, f, t, stride, skip, size):
    own, mate, near, far, near_mate, far_mate = pieces
    table = (
        (own, skip, f, 0),
        (own, stride + skip, f, 1),
        (mate, skip, f ^ 1, 0),
        (mate, stride + skip, f ^ 1, 1),
        (near, skip, f ^ 2, t),
        (far, skip, f ^ 2, 1 - t),
        (near_mate, skip, f ^ 3, t),
        (far_mate, skip, f ^ 3, 1 - t),
    )
    return [(ref, start, pl.multiple_of((2 * q + h) * size, 32)) for ref, start, q, h in table]


def fetch(pieces, f, t, stride, skip, size, cols, dst, dst_cols, sem):
    for ref, start, to in halves(pieces, f, t, stride, skip, size):
        pltpu.make_async_copy(ref.at[pl.ds(start, size), cols], dst.at[pl.ds(to, size), dst_cols], sem).start()


def landed(ref, sem):
    pltpu.make_async_copy(ref, ref, sem).wait()


def norm(x, gain):
    inv = lax.rsqrt(jnp.mean(x * x, axis=-1, keepdims=True) + EPSILON)
    scaled = x * inv
    return inv, scaled, (scaled * gain).astype(BF)


def norm_back(g, inv, scaled, gain):
    gs = g * gain
    return inv * (gs - scaled * jnp.mean(gs * scaled, axis=-1, keepdims=True))


def norm_kernel(x_ref, gain_ref, *rest):
    n_ref, nt_ref = rest[-2:]
    n = norm(x_ref[...].astype(F32), gain_ref[...])[2]
    n_ref[...] = n
    nt_ref[...] = n.T


def norm_call(x, gain, *earlier):
    return pl.pallas_call(
        norm_kernel,
        grid=(2,),
        in_specs=[pl.BlockSpec((SEQ, D), lambda r: (r, 0)), whole((1, D))] + [HBM] * len(earlier),
        out_specs=[pl.BlockSpec((SEQ, D), lambda r: (r, 0)), pl.BlockSpec((D, SEQ), lambda r: (0, r))],
        out_shape=[sds((T, D), BF), sds((D, T), BF)],
        compiler_params=params(),
        cost_estimate=cost(2e9, 5e6),
        name="norm_attn",
    )(x, gain, *earlier)


def qkv_kernel(place_ref, n_ref, *rest):
    pieces, (out_ref, w, sems) = rest[:6], rest[-3:]
    f, t = place_ref[0], place_ref[1]
    step = pl.program_id(0)

    @pl.when(step == 0)
    def _():
        for c in range(3):
            cols = pl.ds(c * D, D)
            fetch(pieces, f, t, 96, 0, 96, cols, w.at[c], pl.ds(0, D), sems.at[c])

    landed(w.at[step], sems.at[step])
    out_ref[...] = jnp.dot(n_ref[...], w[step], preferred_element_type=F32).astype(BF)


def qkv_call(place, n1, pieces, *earlier):
    return pl.pallas_call(
        qkv_kernel,
        grid=(3,),
        in_specs=[SMEM, whole((T, D))] + [HBM] * (6 + len(earlier)),
        out_specs=pl.BlockSpec((T, D), lambda c: (0, c)),
        out_shape=sds((T, 3 * D), BF),
        scratch_shapes=[pltpu.VMEM((3, D, D), BF), pltpu.SemaphoreType.DMA((3,))],
        compiler_params=params(),
        cost_estimate=cost(3.6e9, 1e7),
        name="qkv",
    )(place, n1, *pieces, *earlier)


def attn_fwd_kernel(qkv_ref, fq_ref, fk_ref, bias_ref, *rest):
    o_ref, ot_ref, e_ref, li_ref = rest[-4:]
    lane = lax.broadcasted_iota(jnp.int32, (SEQ, 128), 1)
    q, k = qkv_ref[:, :128], qkv_ref[:, 128:256]
    fq, fk = fq_ref[...], fk_ref[...]
    vt = qkv_ref[:, 256:].T
    scores = []
    for s in range(2):
        own = (lane < 64) if s == 0 else (lane >= 64)
        qa, ka = jnp.where(own, q, fq), jnp.where(own, k, fk)
        scores.append(lax.dot_general(ka, qa, NT, preferred_element_type=F32))
    es = []
    for s in range(2):
        strips = [
            jnp.concatenate([bias_ref[s, bj - bi + 3] for bi in range(4)], axis=1) for bj in range(4)
        ]
        st = scores[s] + jnp.concatenate(strips, axis=0)
        top = jnp.max(st, axis=0, keepdims=True)
        es.append(jnp.exp(st - top).astype(BF))
        e_ref[0, s] = es[s]
    outs = []
    for s in range(2):
        va = jnp.concatenate([vt[64 * s : 64 * s + 64], jnp.ones((16, SEQ), BF)], axis=0)
        ot = jnp.dot(va, es[s], preferred_element_type=F32)
        linv = 1.0 / ot[64:65]
        li_ref[0, s] = jnp.broadcast_to(linv, (8, SEQ))
        outs.append((ot[:64] * linv).astype(BF))
    ot = jnp.concatenate(outs, axis=0)
    ot_ref[...] = ot
    o_ref[...] = ot.T


def attn_fwd(qkv, fq, fk, bias, first, count, *earlier):
    return pl.pallas_call(
        attn_fwd_kernel,
        grid=(count, 2),
        in_specs=[
            pl.BlockSpec((SEQ, 384), lambda p, r: (r, first + p)),
            pl.BlockSpec((SEQ, 128), lambda p, r: (r, 0)),
            pl.BlockSpec((SEQ, 128), lambda p, r: (r, 0)),
            pl.BlockSpec((2, 7, 128, 128), lambda p, r: (first + p, 0, 0, 0)),
        ]
        + [HBM] * len(earlier),
        out_specs=[
            pl.BlockSpec((SEQ, 128), lambda p, r: (r, p)),
            pl.BlockSpec((128, SEQ), lambda p, r: (p, r)),
            pl.BlockSpec((1, 2, SEQ, SEQ), lambda p, r: (r, p, 0, 0)),
            pl.BlockSpec((1, 2, 8, SEQ), lambda p, r: (r, p, 0, 0)),
        ],
        out_shape=[
            sds((T, 128 * count), BF),
            sds((128 * count, T), BF),
            sds((2, 2 * count, SEQ, SEQ), BF),
            sds((2, 2 * count, 8, SEQ), F32),
        ],
        compiler_params=params(),
        cost_estimate=cost(3.3e9 * count, 3e6 * count),
        name="attn_fwd",
    )(qkv, fq, fk, bias, *earlier)


def attn_bwd_kernel(
    place_ref, qkv_ref, do_ref, ot_ref, e_ref, li_ref, nt_ref, *rest
):
    d_ref, keep_ref, send_ref, diag_ref, acc, gacc = rest[-6:]
    r = pl.program_id(1)
    lane = lax.broadcasted_iota(jnp.int32, (SEQ, 128), 1)
    q, k, v = qkv_ref[:, :128], qkv_ref[:, 128:256], qkv_ref[:, 256:]
    do = do_ref[...]
    kt, dt = k.T, do.T
    dqs = []
    prod = dt.astype(F32) * ot_ref[...].astype(F32)
    dps = []
    for s in range(2):
        own = (lane < 64) if s == 0 else (lane >= 64)
        vm = jnp.where(own, v, jnp.zeros_like(v))
        dps.append(lax.dot_general(vm, do, NT, preferred_element_type=F32))
    ds32s, dss, pbs = [], [], []
    for s in range(2):
        linv = li_ref[0, s, 0:1, :]
        delta = jnp.sum(prod[64 * s : 64 * s + 64], axis=0, keepdims=True)
        p = e_ref[0, s].astype(F32) * linv
        pbs.append(p.astype(BF))
        ds32s.append(p * (dps[s] - delta))
        dss.append(ds32s[s].astype(BF))
    dvs, dks = [], []
    for s in range(2):
        dvs.append(jnp.dot(pbs[s], do, preferred_element_type=F32))
        dks.append(jnp.dot(dss[s], q, preferred_element_type=F32))
        dqs.append(jnp.dot(kt[64 * s : 64 * s + 64], dss[s], preferred_element_type=F32).astype(BF))
    for s in range(2):
        ds32 = ds32s[s]
        sums = []
        for d in range(-3, 4):
            total = None
            for bj in range(4):
                bi = bj - d
                if 0 <= bi < 4:
                    block = ds32[128 * bj : 128 * bj + 128, 128 * bi : 128 * bi + 128]
                    total = block if total is None else total + block
            sums.append(total)
        for d in range(7):
            acc[s, d] = jnp.where(r == 0, jnp.zeros((128, 128), F32), acc[s, d]) + sums[d]
    dv0, dvh, dk0, dkh = dvs[0], dvs[1], dks[0], dks[1]
    dq = jnp.concatenate(dqs, axis=0).T
    dk = jnp.where(lane < 64, dk0, dkh).astype(BF)
    dv = jnp.where(lane < 64, dv0, dvh).astype(BF)
    d_all = jnp.concatenate([dq, dk, dv], axis=1)
    d_ref[...] = d_all
    part = jnp.dot(nt_ref[...], d_all, preferred_element_type=F32)

    @pl.when(r == 0)
    def _():
        gacc[...] = part

    @pl.when(r == 1)
    def _():
        g = (gacc[...] + part).astype(BF)
        share(place_ref[0] & 1, g, keep_ref, send_ref)
        up = upper()
        for s in range(2):
            rows = []
            for e in range(8):
                a = acc[s, e] if e < 7 else jnp.zeros((128, 128), F32)
                b = acc[s, e - 1] if e > 0 else jnp.zeros((128, 128), F32)
                c = jnp.where(up, a, b)
                total = c[0:8]
                for g8 in range(1, 16):
                    total = total + pltpu.roll(c[8 * g8 : 8 * g8 + 8], 128 - 8 * g8, 1)
                rows.append(total)
            diag_ref[0, s] = jnp.concatenate(rows, axis=1)


def share(b, g, keep_ref, send_ref):
    for a in range(2):
        even = g[(2 * a) * 192 : (2 * a + 1) * 192]
        odd = g[(2 * a + 1) * 192 : (2 * a + 2) * 192]
        keep_ref[a] = jnp.where(b == 0, even, odd)
        send_ref[a] = jnp.where(b == 0, odd, even)


def attn_bwd(place, qkv, do, nt, heads, first, count, part, skip, shared, *earlier):
    ot, e, li = heads[part][1:]
    at = 2 + first if shared else 0
    width = GROUP if shared else 384 * count
    slab = lambda p, r: (0, 0, at + p)
    base = 7 + len(earlier)
    return pl.pallas_call(
        attn_bwd_kernel,
        grid=(count, 2),
        in_specs=[
            SMEM,
            pl.BlockSpec((SEQ, 384), lambda p, r: (r, first + p)),
            pl.BlockSpec((SEQ, 128), lambda p, r: (r, first + p)),
            pl.BlockSpec((128, SEQ), lambda p, r: (skip + p, r)),
            pl.BlockSpec((1, 2, SEQ, SEQ), lambda p, r: (r, skip + p, 0, 0)),
            pl.BlockSpec((1, 2, 8, SEQ), lambda p, r: (r, skip + p, 0, 0)),
            pl.BlockSpec((D, SEQ), lambda p, r: (0, r)),
        ]
        + [HBM] * (len(earlier) + len(shared)),
        out_specs=[
            pl.BlockSpec((SEQ, 384), lambda p, r: (r, p)),
            pl.BlockSpec((2, 192, 384), slab),
            pl.BlockSpec((2, 192, 384), slab),
            pl.BlockSpec((1, 2, 8, 1024), lambda p, r: (p, 0, 0, 0)),
        ],
        out_shape=[
            sds((T, 384 * count), BF),
            sds((2, 192, width), BF),
            sds((2, 192, width), BF),
            sds((count, 2, 8, 1024), F32),
        ],
        scratch_shapes=[pltpu.VMEM((2, 7, 128, 128), F32), pltpu.VMEM((D, 384), F32)],
        input_output_aliases={base: 1, base + 1: 2} if shared else {},
        compiler_params=params(),
        cost_estimate=pl.CostEstimate(flops=int(6e9 * count), bytes_accessed=int(3e6 * count), transcendentals=0),
        name="attn_bwd",
    )(place, qkv, do, ot, e, li, nt, *earlier, *shared)


FC = 768
FSTEPS = FF // FC


def ffn_kernel(place_ref, x_ref, gain_ref, mt_ref, *rest):
    o_refs, rest = rest[:PARTS], rest[PARTS:]
    pieces, (x2_ref, nt_ref, gp_ref, acts_ref, xs_ref, wo, wi, n2, sems) = rest[:6], rest[6:]
    f, t = place_ref[0], place_ref[1]
    step = pl.program_id(0)

    @pl.when(step == 0)
    def _():
        fetch(pieces, f, t, 96, 0, 96, pl.ds(0, D), wo, pl.ds(0, D), sems.at[FSTEPS])
        for c in range(FSTEPS):
            fetch(pieces, f, t, 96, 0, 96, pl.ds(D + c * FC, FC), wi.at[c], pl.ds(0, FC), sems.at[c])
        landed(wo, sems.at[FSTEPS])
        o = jnp.concatenate([ref[...] for ref in o_refs], axis=1)
        x2 = x_ref[...].astype(F32) + jnp.dot(o, wo[...], preferred_element_type=F32)
        x2_ref[...] = x2
        n = norm(x2, gain_ref[...])[2]
        n2[...] = n
        nt_ref[...] = n.T
        hi = x2.astype(BF)
        lo = (x2 - hi.astype(F32)).astype(BF)
        mt = mt_ref[...]
        xs_ref[...] = jnp.dot(mt, hi, preferred_element_type=F32) + jnp.dot(mt, lo, preferred_element_type=F32)

    landed(wi.at[step], sems.at[step])
    u = jnp.dot(n2[...], wi[step], preferred_element_type=F32)
    u2 = u * u
    half = 0.5 + 0.5 * jnp.tanh(u * (GELU_C + (GELU_C * 0.044715) * u2))
    act = u * half
    gp_ref[...] = (half + act * (1.0 - half) * (2 * GELU_C + (6 * GELU_C * 0.044715) * u2)).astype(BF)
    acts_ref[...] = jnp.dot(mt_ref[...], act.astype(BF), preferred_element_type=F32)


def ffn_call(place, x, gain, member_t, o_parts, pieces):
    return pl.pallas_call(
        ffn_kernel,
        grid=(FSTEPS,),
        in_specs=[SMEM, whole((T, D)), whole((1, D)), whole((SLOTS, T))]
        + [whole(o.shape) for o in o_parts]
        + [HBM] * 6,
        out_specs=[
            whole((T, D)),
            whole((D, T)),
            pl.BlockSpec((T, FC), lambda c: (0, c)),
            pl.BlockSpec((SLOTS, FC), lambda c: (0, c)),
            whole((SLOTS, D)),
        ],
        out_shape=[sds((T, D), F32), sds((D, T), BF), sds((T, FF), BF), sds((SLOTS, FF), F32), sds((SLOTS, D), F32)],
        scratch_shapes=[
            pltpu.VMEM((D, D), BF),
            pltpu.VMEM((FSTEPS, D, FC), BF),
            pltpu.VMEM((T, D), BF),
            pltpu.SemaphoreType.DMA((FSTEPS + 1,)),
        ],
        compiler_params=params(),
        cost_estimate=cost(1.2e10, 2e7),
        name="ffn_fwd",
    )(place, x, gain, member_t, *o_parts, *pieces)


def pooled_kernel(place_ref, acts_ref, xs_ref, info_ref, *rest):
    pieces, (buf_ref, hi_ref, wf, sem) = rest[:6], rest[6:]
    f, t = place_ref[0], place_ref[1]
    fetch(pieces, f, t, 480, 0, 384, pl.ds(0, D), wf, pl.ds(0, D), sem)
    acts = acts_ref[...]
    hi = acts.astype(BF)
    lo = (acts - hi.astype(F32)).astype(BF)
    hi_ref[...] = hi
    info = info_ref[...]
    landed(wf, sem)
    both = jnp.dot(jnp.concatenate([hi, lo], axis=0), wf[...], preferred_element_type=F32)
    pooled = (xs_ref[...] + both[:SLOTS] + both[SLOTS:]) / jnp.maximum(info[:, 0:1], 1.0)
    out = jnp.concatenate([pooled, info], axis=1)
    packed = [out[8 * m : 8 * m + 1, 128 * c : 128 * c + 128] for m in range(MB) for c in range(PAY // 128)]
    packed = jnp.concatenate(packed + [jnp.zeros((SLOTS - len(packed), 128), F32)], axis=0)
    buf_ref[...] = jnp.concatenate([out, packed], axis=1).astype(BF)


def pooled_call(place, acts, xs, info, pieces):
    return pl.pallas_call(
        pooled_kernel,
        in_specs=[SMEM, VMEM, VMEM, VMEM] + [HBM] * 6,
        out_specs=[VMEM, VMEM],
        out_shape=[sds((SLOTS, FULL), BF), sds((SLOTS, FF), BF)],
        scratch_shapes=[pltpu.VMEM((FF, D), BF), pltpu.SemaphoreType.DMA],
        compiler_params=params(),
        cost_estimate=cost(2e9, 5e6),
        name="pooled",
    )(place, acts, xs, info, *pieces)


def loss_kernel(rows, place_ref, own_buf, mate_buf, *rest):
    pieces, rest = rest[:6], rest[-10:]
    loss_ref, own_ref, all_ref, gproj_ref, scr, wp, gp_scr, gz_scr, loss_scr, sems = rest
    f, t, z = place_ref[0], place_ref[1], place_ref[2]
    fetch(pieces, f, t, 480, 384, 96, pl.ds(0, D), wp, pl.ds(0, D), sems.at[0])
    nq, np_ = rows * SLOTS, rows * MB
    for m, buf in enumerate((own_buf, mate_buf)):
        for k in range(rows // 2):
            row = (z ^ (k >> 1)) * 4 + (f ^ (2 * (k & 1)) ^ m)
            pltpu.make_async_copy(
                buf.at[pl.ds(k * SLOTS, SLOTS)], scr.at[pl.ds(pl.multiple_of(row * SLOTS, SLOTS), SLOTS)], sems.at[1]
            ).start()
    landed(scr, sems.at[1])
    blocks = scr[:, PAY:]
    chunks = []
    p_row = lax.broadcasted_iota(jnp.int32, (np_, nq), 0)
    q_at = lax.broadcasted_iota(jnp.int32, (np_, nq), 1)
    for c in range(PAY // 128):
        picker = (q_at == (p_row // MB) * SLOTS + (p_row % MB) * (PAY // 128) + c).astype(BF)
        chunks.append(jnp.dot(picker, blocks, preferred_element_type=F32).astype(BF))
    p_all = jnp.concatenate(chunks, axis=1)
    q_all = scr[:, :PAY]
    both = jnp.concatenate([q_all[:, :D], p_all[:, :D]], axis=0)
    extra = jnp.concatenate([q_all[:, D:], p_all[:, D:]], axis=0).astype(F32)
    landed(wp, sems.at[0])
    proj = wp[...]
    zz = jnp.dot(both, proj, preferred_element_type=F32)
    inv = lax.rsqrt(jnp.sum(zz * zz, axis=-1, keepdims=True) + EPSILON)
    w = zz * inv
    e = w.astype(BF)
    eq, ep = e[:nq], e[nq:]
    logits = LOGIT_SCALE * lax.dot_general(eq, ep, NT, preferred_element_type=F32)
    q_row = lax.broadcasted_iota(jnp.int32, (nq, np_), 0)
    p_col = lax.broadcasted_iota(jnp.int32, (nq, np_), 1)
    same = (q_row // QSEG) % MB == p_col % MB
    logits = jnp.where(same, logits, -1e30)
    top = jnp.max(logits, axis=-1, keepdims=True)
    log_total = top + jnp.log(jnp.sum(jnp.exp(logits - top), axis=-1, keepdims=True))
    positive = extra[:nq, 1:2].astype(jnp.int32)
    hot = jnp.where(same & (p_col // MB == positive), 1.0, 0.0)
    loss = log_total - jnp.sum(logits * hot, axis=-1, keepdims=True)
    gl = LOSS_SCALE * (jnp.exp(logits - log_total) - hot)
    g_eq = LOGIT_SCALE * jnp.dot(gl, ep.astype(F32), precision=HIGHEST, preferred_element_type=F32)
    g_ep = LOGIT_SCALE * lax.dot_general(gl, eq.astype(F32), TN, precision=HIGHEST, preferred_element_type=F32)
    ge = jnp.concatenate([g_eq, g_ep], axis=0)
    gz = (inv * (ge - w * jnp.sum(w * ge, axis=-1, keepdims=True))).astype(BF)
    count = jnp.maximum(extra[:, 0:1], 1.0)
    g_x3 = lax.dot_general(gz, proj, NT, preferred_element_type=F32) / count
    all_ref[...] = g_x3.astype(BF)
    row = z * 4 + f
    gz_scr[...] = gz[:nq]
    loss_scr[...] = jnp.broadcast_to(
        jnp.where(lax.broadcasted_iota(jnp.int32, (nq, 128), 1) == 0, loss, count[:nq]), (nq, 128)
    )
    mine = pl.ds(pl.multiple_of(row * SLOTS, SLOTS), SLOTS)
    slot = lax.broadcasted_iota(jnp.int32, (SLOTS, np_), 0)
    chosen = (slot % QSEG == 0) & (lax.broadcasted_iota(jnp.int32, (SLOTS, np_), 1) == row * MB + slot // QSEG)
    own_p = jnp.dot(chosen.astype(F32), g_x3[nq:], precision=HIGHEST, preferred_element_type=F32)
    own_q = lax.dot_general(gz_scr[mine, :], proj, NT, preferred_element_type=F32) / loss_scr[mine, 1:2]
    own_ref[...] = jnp.where(t == 0, own_q, own_p)
    loss_ref[...] = loss_scr[mine, :]
    gp_scr[...] = lax.dot_general(both, gz, TN, preferred_element_type=F32)
    gproj_ref[...] = gp_scr[pl.ds(pl.multiple_of(f * 192, 192), 192), :]


def loss_call(place, own_buf, mate_buf, pieces, rows, *earlier):
    nq = rows * SLOTS
    return pl.pallas_call(
        functools.partial(loss_kernel, rows),
        in_specs=[SMEM] + [HBM] * (8 + len(earlier)),
        out_specs=[VMEM] * 4,
        out_shape=[sds((SLOTS, 128), F32), sds((SLOTS, D), F32), sds((nq + rows * MB, D), BF), sds((192, D), F32)],
        scratch_shapes=[
            pltpu.VMEM((nq, FULL), BF),
            pltpu.VMEM((D, D), BF),
            pltpu.VMEM((D, D), F32),
            pltpu.VMEM((nq, D), BF),
            pltpu.VMEM((nq, 128), F32),
            pltpu.SemaphoreType.DMA((2,)),
        ],
        compiler_params=params(),
        cost_estimate=cost(5e9, 1e6),
        name="loss",
    )(place, own_buf, mate_buf, *pieces, *earlier)


FB = 512
BSTEPS = FF // FB


def ffn_bwd_kernel(place_ref, own_ref, m2_ref, gp_ref, nt_ref, *rest):
    mids, outs, (keep_ref, send_ref, gn_ref, wi, wf, gf, sems) = rest[:6], rest[6:12], rest[12:]
    f, t = place_ref[0], place_ref[1]
    step = pl.program_id(0)

    @pl.when(step == 0)
    def _():
        fetch(outs, f, t, 480, 0, 384, pl.ds(0, D), wf, pl.ds(0, D), sems.at[BSTEPS])
        for c in range(BSTEPS):
            fetch(mids, f, t, 96, 0, 96, pl.ds(D + c * FB, FB), wi.at[c], pl.ds(0, FB), sems.at[c])
        gf[...] = own_ref[...].astype(BF)
        gn_ref[...] = jnp.zeros_like(gn_ref)
        landed(wf, sems.at[BSTEPS])

    rows = wf[pl.ds(pl.multiple_of(step * FB, FB), FB), :]
    gh = lax.dot_general(gf[...], rows, NT, preferred_element_type=F32)
    hi = gh.astype(BF)
    lo = (gh - hi.astype(F32)).astype(BF)
    wide = jnp.dot(m2_ref[...], jnp.concatenate([hi, lo], axis=0), preferred_element_type=F32)
    gu = (wide * gp_ref[...].astype(F32)).astype(BF)
    g = jnp.dot(nt_ref[...], gu, preferred_element_type=F32).astype(BF)
    share(f & 1, g, keep_ref, send_ref)
    landed(wi.at[step], sems.at[step])
    gn_ref[...] += lax.dot_general(gu, wi[step], NT, preferred_element_type=F32)


def ffn_bwd_call(place, own, member2, gp, n2t, mids, outs):
    return pl.pallas_call(
        ffn_bwd_kernel,
        grid=(BSTEPS,),
        in_specs=[SMEM, whole((SLOTS, D)), whole((T, 2 * SLOTS)), pl.BlockSpec((T, FB), lambda c: (0, c)), whole((D, T))]
        + [HBM] * 12,
        out_specs=[
            pl.BlockSpec((2, 192, FB), lambda c: (0, 0, c)),
            pl.BlockSpec((2, 192, FB), lambda c: (0, 0, c)),
            whole((T, D)),
        ],
        out_shape=[sds((2, 192, FF), BF), sds((2, 192, FF), BF), sds((T, D), F32)],
        scratch_shapes=[
            pltpu.VMEM((BSTEPS, D, FB), BF),
            pltpu.VMEM((FF, D), BF),
            pltpu.VMEM((SLOTS, D), BF),
            pltpu.SemaphoreType.DMA((BSTEPS + 1,)),
        ],
        compiler_params=params(),
        cost_estimate=cost(1.2e10, 2e7),
        name="ffn_bwd",
    )(place, own, member2, gp, n2t, *mids, *outs)


def mid_kernel(place_ref, gn_ref, x2_ref, gain_ref, own_ref, m2_ref, *rest):
    ots, rest = rest[:PARTS], rest[PARTS:]
    pieces, (gx_ref, go_ref, keep_ref, send_ref, wo, sem) = rest[:6], rest[6:]
    f, t = place_ref[0], place_ref[1]
    fetch(pieces, f, t, 96, 0, 96, pl.ds(0, D), wo, pl.ds(0, D), sem)
    own = own_ref[...]
    hi = own.astype(BF)
    lo = (own - hi.astype(F32)).astype(BF)
    g_x3 = jnp.dot(m2_ref[...], jnp.concatenate([hi, lo], axis=0), preferred_element_type=F32)
    gain = gain_ref[...]
    inv, scaled, _ = norm(x2_ref[...], gain)
    g_x2 = g_x3 + norm_back(gn_ref[...], inv, scaled, gain)
    gx_ref[...] = g_x2
    ga = g_x2.astype(BF)
    landed(wo, sem)
    go_ref[...] = lax.dot_general(ga, wo[...], NT, preferred_element_type=F32).astype(BF)
    ot = jnp.concatenate([ref[...] for ref in ots], axis=0)
    g = jnp.dot(ot, ga, preferred_element_type=F32).astype(BF)
    share(f & 1, g, keep_ref, send_ref)


def mid_call(place, gn, x2, gain, own, member2, ots, pieces):
    return pl.pallas_call(
        mid_kernel,
        in_specs=[SMEM] + [VMEM] * (5 + PARTS) + [HBM] * 6,
        out_specs=[whole((T, D)), whole((T, D)), whole((2, 192, D)), whole((2, 192, D))],
        out_shape=[sds((T, D), F32), sds((T, D), BF), sds((2, 192, GROUP), BF), sds((2, 192, GROUP), BF)],
        scratch_shapes=[pltpu.VMEM((D, D), BF), pltpu.SemaphoreType.DMA],
        grid=(1,),
        compiler_params=params(),
        cost_estimate=cost(3e9, 1e7),
        name="attn_out_bwd",
    )(place, gn, x2, gain, own, member2, *ots, *pieces)


def token_kernel(place_ref, gx_ref, x_ref, gain_ref, *rest):
    d_refs, rest = rest[: len(SPLIT)], rest[len(SPLIT) :]
    pieces, (out_ref, w, sem) = rest[:6], rest[-3:]
    f, t = place_ref[0], place_ref[1]
    r = pl.program_id(0)

    @pl.when(r == 0)
    def _():
        fetch(pieces, f, t, 96, 0, 96, pl.ds(0, 3 * D), w, pl.ds(0, 3 * D), sem)
        landed(w, sem)

    d_all = jnp.concatenate([ref[...] for ref in d_refs], axis=1)
    g_n1 = lax.dot_general(d_all, w[...], NT, preferred_element_type=F32)
    gain = gain_ref[...]
    inv, scaled, _ = norm(x_ref[...].astype(F32), gain)
    out_ref[...] = (gx_ref[...] + norm_back(g_n1, inv, scaled, gain)).astype(BF)


def token_call(place, gx, x, gain, d_parts, pieces, *earlier):
    row = lambda r: (r, 0)
    return pl.pallas_call(
        token_kernel,
        grid=(2,),
        in_specs=[SMEM, pl.BlockSpec((SEQ, D), row), pl.BlockSpec((SEQ, D), row), whole((1, D))]
        + [pl.BlockSpec((SEQ, d.shape[1]), row) for d in d_parts]
        + [HBM] * (6 + len(earlier)),
        out_specs=pl.BlockSpec((SEQ, D), row),
        out_shape=sds((T, D), BF),
        scratch_shapes=[pltpu.VMEM((D, 3 * D), BF), pltpu.SemaphoreType.DMA],
        compiler_params=params(),
        cost_estimate=cost(4e9, 1e7),
        name="token_grad",
    )(place, gx, x, gain, *d_parts, *pieces, *earlier)


def swap(block, axis, bit):
    size = lax.axis_size(axis)
    return lax.ppermute(block, axis, [(i, i ^ bit) for i in range(size)])


def after(block, *earlier):
    def kernel(*refs):
        pass

    return pl.pallas_call(
        kernel,
        in_specs=[HBM] * (1 + len(earlier)),
        out_specs=HBM,
        out_shape=sds(block.shape, block.dtype),
        input_output_aliases={0: 0},
        name="after",
    )(block, *earlier)


def pack_kernel(plan, place_ref, *refs):
    ins, own_ref, sent_ref = refs[:-2], refs[-2], refs[-1]
    t = place_ref[1]
    for src, rows, src_cols, dst_rows, dst_cols in plan:
        block = ins[src][pl.ds(rows[0], rows[1]), pl.ds(*src_cols)].astype(BF)
        own_ref[pl.ds(*dst_rows), pl.ds(*dst_cols)] = block
    half = own_ref.shape[0] // 2
    sent_ref[...] = own_ref[pl.ds(pl.multiple_of(t * half, 32), half), :]


def pack_call(place, plan, arrays, shape, *earlier):
    return pl.pallas_call(
        functools.partial(pack_kernel, plan),
        in_specs=[SMEM] + [VMEM] * len(arrays) + [HBM] * len(earlier),
        out_specs=[VMEM, VMEM],
        out_shape=[sds(shape, BF), sds((shape[0] // 2, shape[1]), BF)],
        compiler_params=params(),
        cost_estimate=cost(1e6, 6 * shape[0] * shape[1]),
        name="pack",
    )(place, *arrays, *earlier)


def gather_start(own, sent):
    return own, swap(own, "fsdp", 1), swap(sent, "fsdp", 2)


def gather_rest(own, mate, near, *before):
    far = swap(near, "tower", 1)
    if before:
        far = after(far, *before)
    return own, mate, near, far, swap(near, "fsdp", 1), swap(far, "fsdp", 1)


def pick(parts, index):
    return lax.dynamic_index_in_dim(parts, index, 0, keepdims=False)


def rounded(v):
    return lax.reduce_precision(v, 8, 7)


def plus(a, b):
    return a.astype(F32) + b.astype(F32)


def spread_kernel(side, place_ref, *refs):
    ins, (out_1, mine_1, out_2, mine_2) = refs[: -4], refs[-4:]
    a, t = place_ref[0] // 2, place_ref[1]
    cols = FF // 2
    pairs = [(ins[0], ins[1])] if len(ins) < 4 else [(ins[0], ins[1]), (ins[2], ins[3])]
    start = 0
    for keep_ref, got_ref in pairs:
        width = keep_ref.shape[-1]
        for lo, hi, first in ((0, cols, True), (cols, 2 * cols, False)):
            lo, hi = max(lo, start), min(hi, start + width)
            if lo >= hi:
                continue
            src = pl.ds(lo - start, hi - lo)
            add = lambda i, rows: plus(keep_ref[i, rows, src], got_ref[i, rows, src]).astype(BF)
            every = pl.ds(0, 192)
            if first:
                out_1[pl.ds(0, 192), pl.ds(lo, hi - lo)] = add(1 - a, every)
                mine_1[pl.ds(0, 192), pl.ds(lo, hi - lo)] = add(a, every)
            else:
                dst = pl.ds(lo - cols, hi - lo)
                for i in range(2):
                    out_2[i, :, dst] = add(i, pl.ds(pl.multiple_of((1 - t) * 96, 32), 96))
                    mine_2[i, :, dst] = add(i, pl.ds(pl.multiple_of(t * 96, 32), 96))
        start += width
    if side:
        out_1[pl.ds(192, SIDE), :] = ins[4][...]
        mine_1[pl.ds(192, SIDE), :] = ins[4][...]


def spread_call(place, pairs, side=None, *earlier):
    cols = FF // 2
    rows = 192 + (SIDE if side is not None else 0)
    flat, deep = sds((rows, cols), BF), sds((2, 96, cols), BF)
    ins = [v for pair in pairs for v in pair] + ([side] if side is not None else [])

    def kernel(*refs):
        spread_kernel(side is not None, *refs[: 1 + len(ins)], *refs[-4:])

    return pl.pallas_call(
        kernel,
        in_specs=[SMEM] + [VMEM] * len(ins) + [HBM] * len(earlier),
        out_specs=[VMEM] * 4,
        out_shape=[flat, flat, deep, deep],
        compiler_params=params(),
        cost_estimate=cost(1e6, 7e6),
        name="spread",
    )(place, *ins, *earlier)


def cross_kernel(place_ref, mine_1, got_1, mine_2, got_2, *refs):
    out_1, keep_1, out_2, keep_2 = refs[-4:]
    a, t = place_ref[0] // 2, place_ref[1]
    rows = lambda i: pl.ds(pl.multiple_of(i * 96, 32), 96)
    out_1[pl.ds(0, 96), :] = plus(mine_1[rows(1 - t), :], got_1[rows(1 - t), :]).astype(BF)
    keep_1[pl.ds(0, 96), :] = plus(mine_1[rows(t), :], got_1[rows(t), :]).astype(BF)
    out_2[...] = plus(mine_2[1 - a], got_2[1 - a]).astype(BF)
    keep_2[...] = plus(mine_2[a], got_2[a]).astype(BF)
    if mine_1.shape[0] > 192:
        side = pl.ds(192, SIDE)
        both = plus(mine_1[side, :], got_1[side, :]).astype(BF)
        out_1[pl.ds(96, SIDE), :] = both
        keep_1[pl.ds(96, SIDE), :] = both


def cross_call(place, mine_1, got_1, mine_2, got_2, *earlier):
    rows = mine_1.shape[0] - 96
    flat, half = sds((rows, FF // 2), BF), sds((96, FF // 2), BF)
    return pl.pallas_call(
        cross_kernel,
        in_specs=[SMEM] + [VMEM] * 4 + [HBM] * len(earlier),
        out_specs=[VMEM] * 4,
        out_shape=[flat, flat, half, half],
        compiler_params=params(),
        cost_estimate=cost(1e6, 4e6),
        name="cross",
    )(place, mine_1, got_1, mine_2, got_2, *earlier)


def dp_steps(mine, got):
    z = lax.axis_index("dp")
    bits = [1 << i for i in range(lax.axis_size("dp").bit_length() - 1)]
    rows, cols = mine[0].shape
    side = rounded(plus(mine[0][96:, :D], got[0][96:, :D])) if rows > 96 else None
    mine, got = (mine[0][:96], mine[1]), (got[0][:96], got[1])
    for step, bit in enumerate(bits):
        up = (z // bit) % 2
        if step == 0:
            out = plus(jnp.where(up == 0, mine[1], mine[0]), jnp.where(up == 0, got[1], got[0])).astype(BF)
            mine = plus(jnp.where(up == 0, mine[0], mine[1]), jnp.where(up == 0, got[0], got[1]))
        else:
            cols = mine.shape[-1] // 2
            part = lambda v, i: lax.dynamic_slice_in_dim(v, i * cols, cols, 1)
            out = plus(part(mine, 1 - up), part(got, 1 - up)).astype(BF)
            mine = plus(part(mine, up), part(got, up))
        if side is not None and cols >= D:
            wide = jnp.pad(side.astype(BF), ((0, 0), (0, cols - D)))
            out = jnp.concatenate([out, wide], axis=0)
        out = yield out
        got = swap(out, "dp", bit)
        if side is not None and cols >= D:
            side = rounded(side + got[96:, :D].astype(F32))
            got = got[:96]
        elif side is not None:
            side = rounded(side + swap(side.astype(BF), "dp", bit).astype(F32))
    total = lax.optimization_barrier(plus(mine, got).astype(BF))
    for bit in reversed(bits[1:]):
        total = yield total
        up = (z // bit) % 2
        other = swap(total, "dp", bit)
        total = jnp.concatenate([jnp.where(up == 0, total, other), jnp.where(up == 0, other, total)], axis=1)
    return lax.optimization_barrier(total), side


def four(total, send, far_send, use):
    start = total if send is None else after(total, send)
    near = swap(start, "dp", 1)
    high = swap(start, "tower", 1)
    far = swap(after(near, high) if far_send is None else after(near, high, far_send), "tower", 1)
    return total, near, high if use is None else after(high, use), far


def drain(steps, block):
    while True:
        try:
            block = steps.send(block)
        except StopIteration as end:
            return end.value


def gather_rows(buf, is_query):
    got = swap(buf, "tower", 1)
    buf = jnp.concatenate(
        [jnp.where(is_query, buf[:, :PAY], got[:, :PAY]), jnp.where(is_query, got[:, PAY:], buf[:, PAY:])], axis=1
    )
    n_dp = lax.axis_size("dp")
    buf = jnp.concatenate([buf, swap(buf, "fsdp", 2)], axis=0)
    if n_dp == 4:
        buf = jnp.concatenate([buf] + [swap(buf, "dp", bits) for bits in (1, 2, 3)], axis=0)
    else:
        bit = 1
        while bit < n_dp:
            buf = jnp.concatenate([buf, swap(buf, "dp", bit)], axis=0)
            bit *= 2
    return buf, swap(buf, "fsdp", 1)


def row_sums(v):
    hi = v.astype(BF)
    lo = (v - hi.astype(F32)).astype(BF)
    ones = jnp.ones((8, v.shape[1]), BF)
    both = [lax.dot_general(ones, part, NT, preferred_element_type=F32) for part in (hi, lo)]
    return (both[0] + both[1])[0:1]


def joined(place_ref, refs):
    t, up = place_ref[1], place_ref[2] % 2
    own, near, high, far = (ref[...].astype(F32) for ref in refs)
    mine = jnp.concatenate([jnp.where(up == 0, own, near), jnp.where(up == 0, near, own)], axis=1)
    other = jnp.concatenate([jnp.where(up == 0, high, far), jnp.where(up == 0, far, high)], axis=1)
    return jnp.concatenate([jnp.where(t == 0, mine, other), jnp.where(t == 0, other, mine)], axis=0)


def tail_in_kernel(place_ref, a, b, c, d, own_ref, gain_ref, out_ref, sum_ref):
    g = joined(place_ref, (a, b, c, d))
    out_ref[...] = g
    sum_ref[...] = row_sums(g * own_ref[:, D:].astype(F32)) / gain_ref[...].astype(BF).astype(F32)


def tail_in_call(place, pieces, own, gain):
    return pl.pallas_call(
        tail_in_kernel,
        in_specs=[SMEM] + [VMEM] * 6,
        out_specs=[VMEM] * 2,
        out_shape=[sds((192, FF), F32), sds((1, 192), F32)],
        compiler_params=params(),
        cost_estimate=cost(1e7, 5e6),
        name="tail_in",
    )(place, *pieces, own, gain.reshape(1, 192))


def tail_attn_kernel(place_ref, a, b, c, d, own_ref, gain_ref, out_ref, q_ref, k_ref, v_ref, sum_ref):
    g = joined(place_ref, (a, b, c, d))
    out_ref[...] = g[:, :D]
    for p in range(PAIRS):
        for i, ref in enumerate((q_ref, k_ref, v_ref)):
            at = D + 384 * p + 128 * i
            ref[:, 128 * p : 128 * p + 128] = g[:, at : at + 128]
    sum_ref[...] = row_sums(g[:, D:] * own_ref[...].astype(F32)) / gain_ref[...].astype(BF).astype(F32)


def tail_attn_call(place, pieces, own, gain):
    return pl.pallas_call(
        tail_attn_kernel,
        in_specs=[SMEM] + [VMEM] * 6,
        out_specs=[VMEM] * 5,
        out_shape=[sds((192, D), F32)] * 4 + [sds((1, 192), F32)],
        compiler_params=params(),
        cost_estimate=cost(1e7, 5e6),
        name="tail_attn",
    )(place, *pieces, own, gain.reshape(1, 192))


def local(
    tokens_in,
    query_lengths,
    positive_ids,
    gain_attn,
    gain_ffn,
    w_query,
    w_key,
    w_value,
    w_out,
    rel_bias,
    w_in,
    w_ffn_out,
    w_proj,
):
    f = lax.axis_index("fsdp")
    t = lax.axis_index("tower")
    z = lax.axis_index("dp")
    rows = lax.axis_size("dp") * 4
    is_query = t == 0
    place = jnp.stack([f, t, z]).astype(jnp.int32)

    small = jnp.concatenate([gain_attn, gain_ffn, rel_bias.reshape(-1), jnp.zeros((32,), F32)])
    small = small.astype(BF).reshape(1, 512)
    small = jnp.concatenate([small, swap(small, "fsdp", 1)], axis=0)
    small = jnp.concatenate([small, swap(small, "fsdp", 2)], axis=0)
    small_all = small
    small = jnp.stack([pick(small, i ^ f) for i in range(4)])
    gain_one = small[:, :192].reshape(1, D).astype(F32)
    gain_two = small[:, 192:384].reshape(1, D).astype(F32)
    table = small[:, 384:480].reshape(NB, H)

    plan = [
        (i, (0, 192), (128 * p, 128), (0, 192), (384 * p + 128 * i, 128)) for p in range(PAIRS) for i in range(3)
    ]
    own1, sent1 = pack_call(place, plan, (w_query, w_key, w_value), (192, 3 * D))
    sent1 = after(sent1, small_all)
    plan = [(0, (0, 192), (0, D), (0, 192), (0, D)), (1, (0, 192), (0, FF), (0, 192), (D, FF))]
    own2, sent2 = pack_call(place, plan, (w_out, w_in), (192, D + FF), small_all)
    plan = []
    for h in range(2):
        plan.append((0, (384 * h, 384), (0, D), (480 * h, 384), (0, D)))
        plan.append((1, (96 * h, 96), (0, D), (480 * h + 384, 96), (0, D)))
    own3, sent3 = pack_call(place, plan, (w_ffn_out, w_proj), (960, D), small_all)
    first = gather_start(own1, sent1)
    near1 = after(first[2], own2, own3)
    middle = gather_start(own2, after(sent2, near1))

    lengths = query_lengths[:, 0]
    ends = jnp.cumsum(lengths, axis=-1)
    places = lax.broadcasted_iota(jnp.int32, (MB, SEQ, QSEG), 1)
    segment = jnp.where(is_query, jnp.sum((places >= ends[:, None, :]).astype(jnp.int32), axis=-1), 0)
    slot_ids = lax.broadcasted_iota(jnp.int32, (MB, QSEG), 1)
    counts = jnp.where(is_query, lengths, jnp.where(slot_ids < 1, SEQ, 0))
    seg = segment.reshape(T)
    lane = lax.broadcasted_iota(jnp.int32, (T, 128), 1) % 64
    hot_seg = lane == seg[:, None]
    fq = jnp.where(hot_seg, 1.0, 0.0).astype(BF)
    fk = jnp.where((lane < QSEG) & ~hot_seg, -1e30, 0.0).astype(BF)
    slot_of = seg + QSEG * (lax.broadcasted_iota(jnp.int32, (T,), 0) // SEQ)
    member2 = (slot_of[:, None] == lax.broadcasted_iota(jnp.int32, (T, 2 * SLOTS), 1) % SLOTS).astype(BF)
    member_t = (slot_of[None, :] == lax.broadcasted_iota(jnp.int32, (SLOTS, T), 0)).astype(BF)
    info = jnp.concatenate(
        [
            counts.reshape(SLOTS, 1).astype(F32),
            positive_ids.reshape(SLOTS, 1).astype(F32),
            jnp.zeros((SLOTS, 126), F32),
        ],
        axis=1,
    )
    bias = bias_blocks(jnp.pad(table.T, ((0, 4), (0, 0))), diag_hot())

    x = tokens_in.reshape(T, D)
    n1, n1t = norm_call(x, gain_one)
    first = gather_rest(*first[:2], near1, bias, n1)
    qkv = qkv_call(place, n1, first)
    middle = gather_rest(*middle[:2], after(middle[2], qkv))
    last = gather_start(own3, after(sent3, middle[2]))
    heads = [attn_fwd(qkv, fq, fk, bias, *AHEAD[0], middle[2])]
    heads.append(attn_fwd(qkv, fq, fk, bias, *AHEAD[1], heads[0][0]))
    near3 = after(last[2], heads[1][0])
    x2, n2t, gp, acts, xs = ffn_call(place, x, gain_two, member_t, [h[0] for h in heads], middle)
    last = gather_rest(*last[:2], near3, xs)
    buf, acts = pooled_call(place, acts, xs, info, last)
    own_buf, mate_buf = gather_rows(buf, is_query)
    loss, own, gf_all, grad_proj = loss_call(place, own_buf, mate_buf, last, rows)
    query_loss = loss[:, 0].reshape(MB, 1, QSEG)

    acts_all = lax.all_gather(after(acts, own_buf), ALL, axis=0, tiled=True)
    keep_i, send_i, g_n2 = ffn_bwd_call(place, own, member2, gp, n2t, middle, last)
    got_i = swap(send_i, "fsdp", 1)
    g_x2, go, keep, send = mid_call(place, g_n2, x2, gain_two, own, member2, [h[1] for h in heads], middle)
    out_1, mine_1, out_2, mine_2 = spread_call(place, [(keep_i, got_i)], None, keep)
    got_1, got_2 = swap(out_1, "fsdp", 2), swap(out_2, "tower", 1)
    back = lambda i, *earlier: attn_bwd(place, qkv, go, n1t, heads, *SPLIT[i], *earlier)
    d_a, keep, send, diag_a = back(0, (keep, send), out_1, out_2)
    out_1, mine_1, out_2, mine_2 = cross_call(place, mine_1, got_1, mine_2, got_2, d_a)
    got_1, got_2 = swap(out_1, "tower", 1), swap(out_2, "fsdp", 2)
    d_b, keep, send, diag_b = back(1, (keep, send), out_1, out_2)
    got = swap(send, "fsdp", 1)
    steps = dp_steps((mine_1, mine_2), (got_1, got_2))
    z_out = next(steps)
    d_c, keep_c, send_c, diag_c = back(2, (), d_b, acts_all)
    got_c = swap(send_c, "fsdp", 1)
    diag = jnp.concatenate([diag_a, diag_b, diag_c], axis=0).reshape(H, 8192)
    table_grad = jnp.einsum("hc,cb->hb", diag, diag_hot2(), precision=HIGHEST)
    table_grad = jnp.pad(table_grad, ((0, SIDE - H), (0, FF // 2 - NB))).astype(BF)
    out_b, mine_1b, out_2b, mine_2b = spread_call(place, [(keep, got), (keep_c, got_c)], table_grad, z_out)
    got_1b, got_2b = swap(out_b, "fsdp", 2), swap(out_2b, "tower", 1)
    z_out = after(steps.send(z_out), out_b)
    grad_tokens = token_call(place, g_x2, x, gain_one, (d_a, d_b, d_c), first, out_b, out_2b, z_out)
    z_out = after(steps.send(z_out), grad_tokens)
    out_1b, mine_1b, out_2b, mine_2b = cross_call(place, mine_1b, got_1b, mine_2b, got_2b, z_out)
    total_i = drain(steps, z_out)[0]
    grad_tokens = grad_tokens.reshape(1, MB, 1, SEQ, D)
    got_1b, got_2b = swap(out_1b, "tower", 1), swap(out_2b, "fsdp", 2)
    steps = dp_steps((mine_1b, mine_2b), (got_1b, got_2b))
    z_two = steps.send(next(steps))
    z_three = steps.send(z_two)
    total_b, side = drain(steps, z_three)
    four_i = four(total_i, z_two, z_three, total_b)
    four_b = four(total_b, None, None, None)
    grad_in, gain_ffn_grad = tail_in_call(place, four_i, own2, gain_ffn)
    grad_out, grad_q, grad_k, grad_v, gain_attn_grad = tail_attn_call(place, four_b, own1, gain_attn)
    side = side[:H, :NB]
    grad_table = (side + swap(side, "fsdp", 1)).T

    acts_all = lax.dynamic_slice_in_dim(after(acts_all, total_b), f * D, D, 1).reshape(2, rows * MB, QSEG, D)
    acts_all = jnp.concatenate([acts_all[0].reshape(rows * SLOTS, D), acts_all[1, :, 0]], axis=0)
    grad_ffn_out = lax.dot_general(acts_all, gf_all, TN, preferred_element_type=F32)
    return (
        query_loss,
        grad_tokens,
        gain_attn_grad.reshape(192),
        gain_ffn_grad.reshape(192),
        grad_q,
        grad_k,
        grad_v,
        grad_out,
        lax.dynamic_slice_in_dim(grad_table, f * 8, 8, 0),
        grad_in,
        grad_ffn_out,
        grad_proj,
    )


def solution(mesh):
    rows = P(None, ("dp", "fsdp"), None)
    tokens = P("tower", None, ("dp", "fsdp"), None, None)
    vec, mat = P("fsdp"), P("fsdp", None)
    return jax.shard_map(
        local,
        mesh=mesh,
        in_specs=(tokens, rows, rows, vec, vec) + (mat,) * 8,
        out_specs=(rows, tokens, vec, vec) + (mat,) * 8,
        check_vma=False,
    )
```

```python
import functools

import jax
import jax.numpy as jnp
from jax import lax
from jax.experimental import pallas as pl
from jax.experimental.pallas import tpu as pltpu
from jax.sharding import PartitionSpec as P

D = 768
H = 12
DH = 64
FF = 3072
NB = 32
SEQ = 512
QSEG = 8
MB = 2
T = MB * SEQ
SLOTS = MB * QSEG
PAY = D + 128
FULL = PAY + 128
PAIRS = H // 2
AHEAD = ((0, 3), (3, 3))
SPLIT = ((0, 3, 0, 0), (3, 2, 1, 0), (5, 1, 1, 2))
PARTS = len(AHEAD)
LAST = 384 * SPLIT[-1][1]
GROUP = D + PAIRS * 384 - LAST
SIDE = 16
EPSILON = 1e-06
LOGIT_SCALE = 50.0
LOSS_SCALE = 256.0
THRESHOLDS = (12, 16, 23, 32, 46, 64, 91)
GELU_C = 0.7978845608028654
ALL = ("tower", "dp", "fsdp")
BF = jnp.bfloat16
F32 = jnp.float32
HIGHEST = lax.Precision.HIGHEST
NT = (((1,), (1,)), ((), ()))
TN = (((0,), (0,)), ((), ()))


def bucket_of(m):
    a = jnp.abs(m)
    far = 8 + sum((a >= edge).astype(jnp.int32) for edge in THRESHOLDS)
    return jnp.where(m > 0, 16, 0) + jnp.where(a < 8, a, far)


def diag_hot():
    col = lax.broadcasted_iota(jnp.int32, (NB, 1024), 1)
    m = (col // 128 - 3) * 128 - col % 128
    return (bucket_of(m) == lax.broadcasted_iota(jnp.int32, (NB, 1024), 0)).astype(BF)


def diag_hot2():
    c = lax.broadcasted_iota(jnp.int32, (8192, NB), 0)
    s, col = c // 1024, c % 1024
    m = (col // 128 - 3) * 128 - (col % 128 - s) % 128
    return (bucket_of(m) == lax.broadcasted_iota(jnp.int32, (8192, NB), 1)).astype(F32)


def upper():
    return lax.broadcasted_iota(jnp.int32, (128, 128), 1) >= lax.broadcasted_iota(jnp.int32, (128, 128), 0)


def params():
    return pltpu.CompilerParams(vmem_limit_bytes=66900000)


def cost(flops, moved):
    return pl.CostEstimate(flops=1, bytes_accessed=1, transcendentals=0)


SMEM = pl.BlockSpec(memory_space=pltpu.SMEM)
VMEM = pl.BlockSpec(memory_space=pltpu.VMEM)
HBM = pl.BlockSpec(memory_space=pltpu.HBM)


def sds(shape, kind):
    return jax.ShapeDtypeStruct(shape, kind)


def whole(shape):
    return pl.BlockSpec(shape, lambda *i: (0,) * len(shape))


def bias_kernel(tab_ref, hot_ref, out_ref):
    w = jnp.dot(tab_ref[...], hot_ref[...], preferred_element_type=F32)
    up = upper()
    for h in range(H):
        prev = None
        for e in range(8):
            row = jnp.broadcast_to(w[h : h + 1, e * 128 : (e + 1) * 128], (128, 128))
            r = pltpu.roll(row, 0, 1, stride=1, stride_axis=0)
            if e > 0:
                out_ref[h, e - 1] = jnp.where(up, prev, r)
            prev = r


def bias_blocks(table_t, hot):
    return pl.pallas_call(
        bias_kernel, out_shape=sds((H, 7, 128, 128), F32), cost_estimate=cost(5e9, 5e6), name="bias_blocks"
    )(table_t, hot)


def halves(pieces, f, t, stride, skip, size):
    own, mate, near, far, near_mate, far_mate = pieces
    table = (
        (own, skip, f, 0),
        (own, stride + skip, f, 1),
        (mate, skip, f ^ 1, 0),
        (mate, stride + skip, f ^ 1, 1),
        (near, skip, f ^ 2, t),
        (far, skip, f ^ 2, 1 - t),
        (near_mate, skip, f ^ 3, t),
        (far_mate, skip, f ^ 3, 1 - t),
    )
    return [(ref, start, pl.multiple_of((2 * q + h) * size, 32)) for ref, start, q, h in table]


def fetch(pieces, f, t, stride, skip, size, cols, dst, dst_cols, sem):
    for ref, start, to in halves(pieces, f, t, stride, skip, size):
        pltpu.make_async_copy(ref.at[pl.ds(start, size), cols], dst.at[pl.ds(to, size), dst_cols], sem).start()


def landed(ref, sem):
    pltpu.make_async_copy(ref, ref, sem).wait()


def norm(x, gain):
    inv = lax.rsqrt(jnp.mean(x * x, axis=-1, keepdims=True) + EPSILON)
    scaled = x * inv
    return inv, scaled, (scaled * gain).astype(BF)


def norm_back(g, inv, scaled, gain):
    gs = g * gain
    return inv * (gs - scaled * jnp.mean(gs * scaled, axis=-1, keepdims=True))


def norm_kernel(x_ref, gain_ref, *rest):
    n_ref, nt_ref = rest[-2:]
    n = norm(x_ref[...].astype(F32), gain_ref[...])[2]
    n_ref[...] = n
    nt_ref[...] = n.T


def norm_call(x, gain, *earlier):
    return pl.pallas_call(
        norm_kernel,
        grid=(2,),
        in_specs=[pl.BlockSpec((SEQ, D), lambda r: (r, 0)), whole((1, D))] + [HBM] * len(earlier),
        out_specs=[pl.BlockSpec((SEQ, D), lambda r: (r, 0)), pl.BlockSpec((D, SEQ), lambda r: (0, r))],
        out_shape=[sds((T, D), BF), sds((D, T), BF)],
        compiler_params=params(),
        cost_estimate=cost(2e9, 5e6),
        name="norm_attn",
    )(x, gain, *earlier)


def qkv_kernel(place_ref, n_ref, *rest):
    pieces, (out_ref, w, sems) = rest[:6], rest[-3:]
    f, t = place_ref[0], place_ref[1]
    step = pl.program_id(0)

    @pl.when(step == 0)
    def _():
        for c in range(3):
            cols = pl.ds(c * D, D)
            fetch(pieces, f, t, 96, 0, 96, cols, w.at[c], pl.ds(0, D), sems.at[c])

    landed(w.at[step], sems.at[step])
    out_ref[...] = jnp.dot(n_ref[...], w[step], preferred_element_type=F32).astype(BF)


def qkv_call(place, n1, pieces, *earlier):
    return pl.pallas_call(
        qkv_kernel,
        grid=(3,),
        in_specs=[SMEM, whole((T, D))] + [HBM] * (6 + len(earlier)),
        out_specs=pl.BlockSpec((T, D), lambda c: (0, c)),
        out_shape=sds((T, 3 * D), BF),
        scratch_shapes=[pltpu.VMEM((3, D, D), BF), pltpu.SemaphoreType.DMA((3,))],
        compiler_params=params(),
        cost_estimate=cost(3.6e9, 1e7),
        name="qkv",
    )(place, n1, *pieces, *earlier)


def attn_fwd_kernel(qkv_ref, fq_ref, fk_ref, bias_ref, *rest):
    o_ref, ot_ref, e_ref, li_ref = rest[-4:]
    lane = lax.broadcasted_iota(jnp.int32, (SEQ, 128), 1)
    q, k = qkv_ref[:, :128], qkv_ref[:, 128:256]
    fq, fk = fq_ref[...], fk_ref[...]
    vt = qkv_ref[:, 256:].T
    scores = []
    for s in range(2):
        own = (lane < 64) if s == 0 else (lane >= 64)
        qa, ka = jnp.where(own, q, fq), jnp.where(own, k, fk)
        scores.append(lax.dot_general(ka, qa, NT, preferred_element_type=F32))
    es = []
    for s in range(2):
        strips = [
            jnp.concatenate([bias_ref[s, bj - bi + 3] for bi in range(4)], axis=1) for bj in range(4)
        ]
        st = scores[s] + jnp.concatenate(strips, axis=0)
        top = jnp.max(st, axis=0, keepdims=True)
        es.append(jnp.exp(st - top).astype(BF))
        e_ref[0, s] = es[s]
    outs = []
    for s in range(2):
        va = jnp.concatenate([vt[64 * s : 64 * s + 64], jnp.ones((16, SEQ), BF)], axis=0)
        ot = jnp.dot(va, es[s], preferred_element_type=F32)
        linv = 1.0 / ot[64:65]
        li_ref[0, s] = jnp.broadcast_to(linv, (8, SEQ))
        outs.append((ot[:64] * linv).astype(BF))
    ot = jnp.concatenate(outs, axis=0)
    ot_ref[...] = ot
    o_ref[...] = ot.T


def attn_fwd(qkv, fq, fk, bias, first, count, *earlier):
    return pl.pallas_call(
        attn_fwd_kernel,
        grid=(count, 2),
        in_specs=[
            pl.BlockSpec((SEQ, 384), lambda p, r: (r, first + p)),
            pl.BlockSpec((SEQ, 128), lambda p, r: (r, 0)),
            pl.BlockSpec((SEQ, 128), lambda p, r: (r, 0)),
            pl.BlockSpec((2, 7, 128, 128), lambda p, r: (first + p, 0, 0, 0)),
        ]
        + [HBM] * len(earlier),
        out_specs=[
            pl.BlockSpec((SEQ, 128), lambda p, r: (r, p)),
            pl.BlockSpec((128, SEQ), lambda p, r: (p, r)),
            pl.BlockSpec((1, 2, SEQ, SEQ), lambda p, r: (r, p, 0, 0)),
            pl.BlockSpec((1, 2, 8, SEQ), lambda p, r: (r, p, 0, 0)),
        ],
        out_shape=[
            sds((T, 128 * count), BF),
            sds((128 * count, T), BF),
            sds((2, 2 * count, SEQ, SEQ), BF),
            sds((2, 2 * count, 8, SEQ), F32),
        ],
        compiler_params=params(),
        cost_estimate=cost(3.3e9 * count, 3e6 * count),
        name="attn_fwd",
    )(qkv, fq, fk, bias, *earlier)


def attn_bwd_kernel(
    place_ref, qkv_ref, do_ref, ot_ref, e_ref, li_ref, nt_ref, *rest
):
    d_ref, keep_ref, send_ref, diag_ref, acc, gacc = rest[-6:]
    r = pl.program_id(1)
    lane = lax.broadcasted_iota(jnp.int32, (SEQ, 128), 1)
    q, k, v = qkv_ref[:, :128], qkv_ref[:, 128:256], qkv_ref[:, 256:]
    do = do_ref[...]
    kt, dt = k.T, do.T
    dqs = []
    prod = dt.astype(F32) * ot_ref[...].astype(F32)
    dps = []
    for s in range(2):
        own = (lane < 64) if s == 0 else (lane >= 64)
        vm = jnp.where(own, v, jnp.zeros_like(v))
        dps.append(lax.dot_general(vm, do, NT, preferred_element_type=F32))
    ds32s, dss, pbs = [], [], []
    for s in range(2):
        linv = li_ref[0, s, 0:1, :]
        delta = jnp.sum(prod[64 * s : 64 * s + 64], axis=0, keepdims=True)
        p = e_ref[0, s].astype(F32) * linv
        pbs.append(p.astype(BF))
        ds32s.append(p * (dps[s] - delta))
        dss.append(ds32s[s].astype(BF))
    dvs, dks = [], []
    for s in range(2):
        dvs.append(jnp.dot(pbs[s], do, preferred_element_type=F32))
        dks.append(jnp.dot(dss[s], q, preferred_element_type=F32))
        dqs.append(jnp.dot(kt[64 * s : 64 * s + 64], dss[s], preferred_element_type=F32).astype(BF))
    for s in range(2):
        ds32 = ds32s[s]
        sums = []
        for d in range(-3, 4):
            total = None
            for bj in range(4):
                bi = bj - d
                if 0 <= bi < 4:
                    block = ds32[128 * bj : 128 * bj + 128, 128 * bi : 128 * bi + 128]
                    total = block if total is None else total + block
            sums.append(total)
        for d in range(7):
            acc[s, d] = jnp.where(r == 0, jnp.zeros((128, 128), F32), acc[s, d]) + sums[d]
    dv0, dvh, dk0, dkh = dvs[0], dvs[1], dks[0], dks[1]
    dq = jnp.concatenate(dqs, axis=0).T
    dk = jnp.where(lane < 64, dk0, dkh).astype(BF)
    dv = jnp.where(lane < 64, dv0, dvh).astype(BF)
    d_all = jnp.concatenate([dq, dk, dv], axis=1)
    d_ref[...] = d_all
    part = jnp.dot(nt_ref[...], d_all, preferred_element_type=F32)

    @pl.when(r == 0)
    def _():
        gacc[...] = part

    @pl.when(r == 1)
    def _():
        g = (gacc[...] + part).astype(BF)
        share(place_ref[0] & 1, g, keep_ref, send_ref)
        up = upper()
        for s in range(2):
            rows = []
            for e in range(8):
                a = acc[s, e] if e < 7 else jnp.zeros((128, 128), F32)
                b = acc[s, e - 1] if e > 0 else jnp.zeros((128, 128), F32)
                c = jnp.where(up, a, b)
                total = c[0:8]
                for g8 in range(1, 16):
                    total = total + pltpu.roll(c[8 * g8 : 8 * g8 + 8], 128 - 8 * g8, 1)
                rows.append(total)
            diag_ref[0, s] = jnp.concatenate(rows, axis=1)


def share(b, g, keep_ref, send_ref):
    for a in range(2):
        even = g[(2 * a) * 192 : (2 * a + 1) * 192]
        odd = g[(2 * a + 1) * 192 : (2 * a + 2) * 192]
        keep_ref[a] = jnp.where(b == 0, even, odd)
        send_ref[a] = jnp.where(b == 0, odd, even)


def attn_bwd(place, qkv, do, nt, heads, first, count, part, skip, shared, *earlier):
    ot, e, li = heads[part][1:]
    at = 2 + first if shared else 0
    width = GROUP if shared else 384 * count
    slab = lambda p, r: (0, 0, at + p)
    base = 7 + len(earlier)
    return pl.pallas_call(
        attn_bwd_kernel,
        grid=(count, 2),
        in_specs=[
            SMEM,
            pl.BlockSpec((SEQ, 384), lambda p, r: (r, first + p)),
            pl.BlockSpec((SEQ, 128), lambda p, r: (r, first + p)),
            pl.BlockSpec((128, SEQ), lambda p, r: (skip + p, r)),
            pl.BlockSpec((1, 2, SEQ, SEQ), lambda p, r: (r, skip + p, 0, 0)),
            pl.BlockSpec((1, 2, 8, SEQ), lambda p, r: (r, skip + p, 0, 0)),
            pl.BlockSpec((D, SEQ), lambda p, r: (0, r)),
        ]
        + [HBM] * (len(earlier) + len(shared)),
        out_specs=[
            pl.BlockSpec((SEQ, 384), lambda p, r: (r, p)),
            pl.BlockSpec((2, 192, 384), slab),
            pl.BlockSpec((2, 192, 384), slab),
            pl.BlockSpec((1, 2, 8, 1024), lambda p, r: (p, 0, 0, 0)),
        ],
        out_shape=[
            sds((T, 384 * count), BF),
            sds((2, 192, width), BF),
            sds((2, 192, width), BF),
            sds((count, 2, 8, 1024), F32),
        ],
        scratch_shapes=[pltpu.VMEM((2, 7, 128, 128), F32), pltpu.VMEM((D, 384), F32)],
        input_output_aliases={base: 1, base + 1: 2} if shared else {},
        compiler_params=params(),
        cost_estimate=pl.CostEstimate(flops=int(6e9 * count), bytes_accessed=int(3e6 * count), transcendentals=0),
        name="attn_bwd",
    )(place, qkv, do, ot, e, li, nt, *earlier, *shared)


FC = 768
FSTEPS = FF // FC


def ffn_kernel(place_ref, x_ref, gain_ref, mt_ref, *rest):
    o_refs, rest = rest[:PARTS], rest[PARTS:]
    pieces, (x2_ref, nt_ref, gp_ref, acts_ref, xs_ref, wo, wi, n2, sems) = rest[:6], rest[6:]
    f, t = place_ref[0], place_ref[1]
    step = pl.program_id(0)

    @pl.when(step == 0)
    def _():
        fetch(pieces, f, t, 96, 0, 96, pl.ds(0, D), wo, pl.ds(0, D), sems.at[FSTEPS])
        for c in range(FSTEPS):
            fetch(pieces, f, t, 96, 0, 96, pl.ds(D + c * FC, FC), wi.at[c], pl.ds(0, FC), sems.at[c])
        landed(wo, sems.at[FSTEPS])
        o = jnp.concatenate([ref[...] for ref in o_refs], axis=1)
        x2 = x_ref[...].astype(F32) + jnp.dot(o, wo[...], preferred_element_type=F32)
        x2_ref[...] = x2
        n = norm(x2, gain_ref[...])[2]
        n2[...] = n
        nt_ref[...] = n.T
        hi = x2.astype(BF)
        lo = (x2 - hi.astype(F32)).astype(BF)
        mt = mt_ref[...]
        xs_ref[...] = jnp.dot(mt, hi, preferred_element_type=F32) + jnp.dot(mt, lo, preferred_element_type=F32)

    landed(wi.at[step], sems.at[step])
    u = jnp.dot(n2[...], wi[step], preferred_element_type=F32)
    u2 = u * u
    half = 0.5 + 0.5 * jnp.tanh(u * (GELU_C + (GELU_C * 0.044715) * u2))
    act = u * half
    gp_ref[...] = (half + act * (1.0 - half) * (2 * GELU_C + (6 * GELU_C * 0.044715) * u2)).astype(BF)
    acts_ref[...] = jnp.dot(mt_ref[...], act.astype(BF), preferred_element_type=F32)


def ffn_call(place, x, gain, member_t, o_parts, pieces):
    return pl.pallas_call(
        ffn_kernel,
        grid=(FSTEPS,),
        in_specs=[SMEM, whole((T, D)), whole((1, D)), whole((SLOTS, T))]
        + [whole(o.shape) for o in o_parts]
        + [HBM] * 6,
        out_specs=[
            whole((T, D)),
            whole((D, T)),
            pl.BlockSpec((T, FC), lambda c: (0, c)),
            pl.BlockSpec((SLOTS, FC), lambda c: (0, c)),
            whole((SLOTS, D)),
        ],
        out_shape=[sds((T, D), F32), sds((D, T), BF), sds((T, FF), BF), sds((SLOTS, FF), F32), sds((SLOTS, D), F32)],
        scratch_shapes=[
            pltpu.VMEM((D, D), BF),
            pltpu.VMEM((FSTEPS, D, FC), BF),
            pltpu.VMEM((T, D), BF),
            pltpu.SemaphoreType.DMA((FSTEPS + 1,)),
        ],
        compiler_params=params(),
        cost_estimate=cost(1.2e10, 2e7),
        name="ffn_fwd",
    )(place, x, gain, member_t, *o_parts, *pieces)


def pooled_kernel(place_ref, acts_ref, xs_ref, info_ref, *rest):
    pieces, (buf_ref, hi_ref, wf, sem) = rest[:6], rest[6:]
    f, t = place_ref[0], place_ref[1]
    fetch(pieces, f, t, 480, 0, 384, pl.ds(0, D), wf, pl.ds(0, D), sem)
    acts = acts_ref[...]
    hi = acts.astype(BF)
    lo = (acts - hi.astype(F32)).astype(BF)
    hi_ref[...] = hi
    info = info_ref[...]
    landed(wf, sem)
    both = jnp.dot(jnp.concatenate([hi, lo], axis=0), wf[...], preferred_element_type=F32)
    pooled = (xs_ref[...] + both[:SLOTS] + both[SLOTS:]) / jnp.maximum(info[:, 0:1], 1.0)
    out = jnp.concatenate([pooled, info], axis=1)
    packed = [out[8 * m : 8 * m + 1, 128 * c : 128 * c + 128] for m in range(MB) for c in range(PAY // 128)]
    packed = jnp.concatenate(packed + [jnp.zeros((SLOTS - len(packed), 128), F32)], axis=0)
    buf_ref[...] = jnp.concatenate([out, packed], axis=1).astype(BF)


def pooled_call(place, acts, xs, info, pieces):
    return pl.pallas_call(
        pooled_kernel,
        in_specs=[SMEM, VMEM, VMEM, VMEM] + [HBM] * 6,
        out_specs=[VMEM, VMEM],
        out_shape=[sds((SLOTS, FULL), BF), sds((SLOTS, FF), BF)],
        scratch_shapes=[pltpu.VMEM((FF, D), BF), pltpu.SemaphoreType.DMA],
        compiler_params=params(),
        cost_estimate=cost(2e9, 5e6),
        name="pooled",
    )(place, acts, xs, info, *pieces)


def loss_kernel(rows, place_ref, own_buf, mate_buf, *rest):
    pieces, rest = rest[:6], rest[-10:]
    loss_ref, own_ref, all_ref, gproj_ref, scr, wp, gp_scr, gz_scr, loss_scr, sems = rest
    f, t, z = place_ref[0], place_ref[1], place_ref[2]
    fetch(pieces, f, t, 480, 384, 96, pl.ds(0, D), wp, pl.ds(0, D), sems.at[0])
    nq, np_ = rows * SLOTS, rows * MB
    for m, buf in enumerate((own_buf, mate_buf)):
        for k in range(rows // 2):
            row = (z ^ (k >> 1)) * 4 + (f ^ (2 * (k & 1)) ^ m)
            pltpu.make_async_copy(
                buf.at[pl.ds(k * SLOTS, SLOTS)], scr.at[pl.ds(pl.multiple_of(row * SLOTS, SLOTS), SLOTS)], sems.at[1]
            ).start()
    landed(scr, sems.at[1])
    blocks = scr[:, PAY:]
    chunks = []
    p_row = lax.broadcasted_iota(jnp.int32, (np_, nq), 0)
    q_at = lax.broadcasted_iota(jnp.int32, (np_, nq), 1)
    for c in range(PAY // 128):
        picker = (q_at == (p_row // MB) * SLOTS + (p_row % MB) * (PAY // 128) + c).astype(BF)
        chunks.append(jnp.dot(picker, blocks, preferred_element_type=F32).astype(BF))
    p_all = jnp.concatenate(chunks, axis=1)
    q_all = scr[:, :PAY]
    both = jnp.concatenate([q_all[:, :D], p_all[:, :D]], axis=0)
    extra = jnp.concatenate([q_all[:, D:], p_all[:, D:]], axis=0).astype(F32)
    landed(wp, sems.at[0])
    proj = wp[...]
    zz = jnp.dot(both, proj, preferred_element_type=F32)
    inv = lax.rsqrt(jnp.sum(zz * zz, axis=-1, keepdims=True) + EPSILON)
    w = zz * inv
    e = w.astype(BF)
    eq, ep = e[:nq], e[nq:]
    logits = LOGIT_SCALE * lax.dot_general(eq, ep, NT, preferred_element_type=F32)
    q_row = lax.broadcasted_iota(jnp.int32, (nq, np_), 0)
    p_col = lax.broadcasted_iota(jnp.int32, (nq, np_), 1)
    same = (q_row // QSEG) % MB == p_col % MB
    logits = jnp.where(same, logits, -1e30)
    top = jnp.max(logits, axis=-1, keepdims=True)
    log_total = top + jnp.log(jnp.sum(jnp.exp(logits - top), axis=-1, keepdims=True))
    positive = extra[:nq, 1:2].astype(jnp.int32)
    hot = jnp.where(same & (p_col // MB == positive), 1.0, 0.0)
    loss = log_total - jnp.sum(logits * hot, axis=-1, keepdims=True)
    gl = LOSS_SCALE * (jnp.exp(logits - log_total) - hot)
    g_eq = LOGIT_SCALE * jnp.dot(gl, ep.astype(F32), precision=HIGHEST, preferred_element_type=F32)
    g_ep = LOGIT_SCALE * lax.dot_general(gl, eq.astype(F32), TN, precision=HIGHEST, preferred_element_type=F32)
    ge = jnp.concatenate([g_eq, g_ep], axis=0)
    gz = (inv * (ge - w * jnp.sum(w * ge, axis=-1, keepdims=True))).astype(BF)
    count = jnp.maximum(extra[:, 0:1], 1.0)
    g_x3 = lax.dot_general(gz, proj, NT, preferred_element_type=F32) / count
    all_ref[...] = g_x3.astype(BF)
    row = z * 4 + f
    gz_scr[...] = gz[:nq]
    loss_scr[...] = jnp.broadcast_to(
        jnp.where(lax.broadcasted_iota(jnp.int32, (nq, 128), 1) == 0, loss, count[:nq]), (nq, 128)
    )
    mine = pl.ds(pl.multiple_of(row * SLOTS, SLOTS), SLOTS)
    slot = lax.broadcasted_iota(jnp.int32, (SLOTS, np_), 0)
    chosen = (slot % QSEG == 0) & (lax.broadcasted_iota(jnp.int32, (SLOTS, np_), 1) == row * MB + slot // QSEG)
    own_p = jnp.dot(chosen.astype(F32), g_x3[nq:], precision=HIGHEST, preferred_element_type=F32)
    own_q = lax.dot_general(gz_scr[mine, :], proj, NT, preferred_element_type=F32) / loss_scr[mine, 1:2]
    own_ref[...] = jnp.where(t == 0, own_q, own_p)
    loss_ref[...] = loss_scr[mine, :]
    gp_scr[...] = lax.dot_general(both, gz, TN, preferred_element_type=F32)
    gproj_ref[...] = gp_scr[pl.ds(pl.multiple_of(f * 192, 192), 192), :]


def loss_call(place, own_buf, mate_buf, pieces, rows, *earlier):
    nq = rows * SLOTS
    return pl.pallas_call(
        functools.partial(loss_kernel, rows),
        in_specs=[SMEM] + [HBM] * (8 + len(earlier)),
        out_specs=[VMEM] * 4,
        out_shape=[sds((SLOTS, 128), F32), sds((SLOTS, D), F32), sds((nq + rows * MB, D), BF), sds((192, D), F32)],
        scratch_shapes=[
            pltpu.VMEM((nq, FULL), BF),
            pltpu.VMEM((D, D), BF),
            pltpu.VMEM((D, D), F32),
            pltpu.VMEM((nq, D), BF),
            pltpu.VMEM((nq, 128), F32),
            pltpu.SemaphoreType.DMA((2,)),
        ],
        compiler_params=params(),
        cost_estimate=cost(5e9, 1e6),
        name="loss",
    )(place, own_buf, mate_buf, *pieces, *earlier)


FB = 512
BSTEPS = FF // FB


def ffn_bwd_kernel(place_ref, own_ref, m2_ref, gp_ref, nt_ref, *rest):
    mids, outs, (keep_ref, send_ref, gn_ref, wi, wf, gf, sems) = rest[:6], rest[6:12], rest[12:]
    f, t = place_ref[0], place_ref[1]
    step = pl.program_id(0)

    @pl.when(step == 0)
    def _():
        for ref, start, to in halves(outs, f, t, 480, 0, 384):
            pltpu.make_async_copy(
                ref.at[pl.ds(start, 384), :], wf.at[pl.ds(to, 384), :], sems.at[BSTEPS + to // 384]
            ).start()
        for c in range(BSTEPS):
            fetch(mids, f, t, 96, 0, 96, pl.ds(D + c * FB, FB), wi.at[c], pl.ds(0, FB), sems.at[c])
        gf[...] = own_ref[...].astype(BF)
        gn_ref[...] = jnp.zeros_like(gn_ref)

    due = 0
    for c in range(BSTEPS):
        until = -(-(c + 1) * FB // 384)

        @pl.when(step == c)
        def _(due=due, until=until):
            for h in range(due, until):
                landed(wf.at[pl.ds(384 * h, 384), :], sems.at[BSTEPS + h])

        due = until

    rows = wf[pl.ds(pl.multiple_of(step * FB, FB), FB), :]
    gh = lax.dot_general(gf[...], rows, NT, preferred_element_type=F32)
    hi = gh.astype(BF)
    lo = (gh - hi.astype(F32)).astype(BF)
    wide = jnp.dot(m2_ref[...], jnp.concatenate([hi, lo], axis=0), preferred_element_type=F32)
    gu = (wide * gp_ref[...].astype(F32)).astype(BF)
    g = jnp.dot(nt_ref[...], gu, preferred_element_type=F32).astype(BF)
    share(f & 1, g, keep_ref, send_ref)
    landed(wi.at[step], sems.at[step])
    gn_ref[...] += lax.dot_general(gu, wi[step], NT, preferred_element_type=F32)


def ffn_bwd_call(place, own, member2, gp, n2t, mids, outs):
    return pl.pallas_call(
        ffn_bwd_kernel,
        grid=(BSTEPS,),
        in_specs=[SMEM, whole((SLOTS, D)), whole((T, 2 * SLOTS)), pl.BlockSpec((T, FB), lambda c: (0, c)), whole((D, T))]
        + [HBM] * 12,
        out_specs=[
            pl.BlockSpec((2, 192, FB), lambda c: (0, 0, c)),
            pl.BlockSpec((2, 192, FB), lambda c: (0, 0, c)),
            whole((T, D)),
        ],
        out_shape=[sds((2, 192, FF), BF), sds((2, 192, FF), BF), sds((T, D), F32)],
        scratch_shapes=[
            pltpu.VMEM((BSTEPS, D, FB), BF),
            pltpu.VMEM((FF, D), BF),
            pltpu.VMEM((SLOTS, D), BF),
            pltpu.SemaphoreType.DMA((BSTEPS + 8,)),
        ],
        compiler_params=params(),
        cost_estimate=cost(1.2e10, 2e7),
        name="ffn_bwd",
    )(place, own, member2, gp, n2t, *mids, *outs)


def mid_kernel(place_ref, gn_ref, x2_ref, gain_ref, own_ref, m2_ref, *rest):
    ots, rest = rest[:PARTS], rest[PARTS:]
    pieces, (gx_ref, go_ref, keep_ref, send_ref, wo, sem) = rest[:6], rest[6:]
    f, t = place_ref[0], place_ref[1]
    fetch(pieces, f, t, 96, 0, 96, pl.ds(0, D), wo, pl.ds(0, D), sem)
    own = own_ref[...]
    hi = own.astype(BF)
    lo = (own - hi.astype(F32)).astype(BF)
    g_x3 = jnp.dot(m2_ref[...], jnp.concatenate([hi, lo], axis=0), preferred_element_type=F32)
    gain = gain_ref[...]
    inv, scaled, _ = norm(x2_ref[...], gain)
    g_x2 = g_x3 + norm_back(gn_ref[...], inv, scaled, gain)
    gx_ref[...] = g_x2
    ga = g_x2.astype(BF)
    landed(wo, sem)
    go_ref[...] = lax.dot_general(ga, wo[...], NT, preferred_element_type=F32).astype(BF)
    ot = jnp.concatenate([ref[...] for ref in ots], axis=0)
    g = jnp.dot(ot, ga, preferred_element_type=F32).astype(BF)
    share(f & 1, g, keep_ref, send_ref)


def mid_call(place, gn, x2, gain, own, member2, ots, pieces):
    return pl.pallas_call(
        mid_kernel,
        in_specs=[SMEM] + [VMEM] * (5 + PARTS) + [HBM] * 6,
        out_specs=[whole((T, D)), whole((T, D)), whole((2, 192, D)), whole((2, 192, D))],
        out_shape=[sds((T, D), F32), sds((T, D), BF), sds((2, 192, GROUP), BF), sds((2, 192, GROUP), BF)],
        scratch_shapes=[pltpu.VMEM((D, D), BF), pltpu.SemaphoreType.DMA],
        grid=(1,),
        compiler_params=params(),
        cost_estimate=cost(3e9, 1e7),
        name="attn_out_bwd",
    )(place, gn, x2, gain, own, member2, *ots, *pieces)


def token_kernel(place_ref, gx_ref, x_ref, gain_ref, *rest):
    d_refs, rest = rest[: len(SPLIT)], rest[len(SPLIT) :]
    pieces, (out_ref, w, sem) = rest[:6], rest[-3:]
    f, t = place_ref[0], place_ref[1]
    r = pl.program_id(0)

    @pl.when(r == 0)
    def _():
        fetch(pieces, f, t, 96, 0, 96, pl.ds(0, 3 * D), w, pl.ds(0, 3 * D), sem)
        landed(w, sem)

    d_all = jnp.concatenate([ref[...] for ref in d_refs], axis=1)
    g_n1 = lax.dot_general(d_all, w[...], NT, preferred_element_type=F32)
    gain = gain_ref[...]
    inv, scaled, _ = norm(x_ref[...].astype(F32), gain)
    out_ref[...] = (gx_ref[...] + norm_back(g_n1, inv, scaled, gain)).astype(BF)


def token_call(place, gx, x, gain, d_parts, pieces, *earlier):
    row = lambda r: (r, 0)
    return pl.pallas_call(
        token_kernel,
        grid=(2,),
        in_specs=[SMEM, pl.BlockSpec((SEQ, D), row), pl.BlockSpec((SEQ, D), row), whole((1, D))]
        + [pl.BlockSpec((SEQ, d.shape[1]), row) for d in d_parts]
        + [HBM] * (6 + len(earlier)),
        out_specs=pl.BlockSpec((SEQ, D), row),
        out_shape=sds((T, D), BF),
        scratch_shapes=[pltpu.VMEM((D, 3 * D), BF), pltpu.SemaphoreType.DMA],
        compiler_params=params(),
        cost_estimate=cost(4e9, 1e7),
        name="token_grad",
    )(place, gx, x, gain, *d_parts, *pieces, *earlier)


def swap(block, axis, bit):
    size = lax.axis_size(axis)
    return lax.ppermute(block, axis, [(i, i ^ bit) for i in range(size)])


def after(block, *earlier):
    def kernel(*refs):
        pass

    return pl.pallas_call(
        kernel,
        in_specs=[HBM] * (1 + len(earlier)),
        out_specs=HBM,
        out_shape=sds(block.shape, block.dtype),
        input_output_aliases={0: 0},
        name="after",
    )(block, *earlier)


def pack_kernel(plan, place_ref, *refs):
    ins, own_ref, sent_ref = refs[:-2], refs[-2], refs[-1]
    t = place_ref[1]
    for src, rows, src_cols, dst_rows, dst_cols in plan:
        block = ins[src][pl.ds(rows[0], rows[1]), pl.ds(*src_cols)].astype(BF)
        own_ref[pl.ds(*dst_rows), pl.ds(*dst_cols)] = block
    half = own_ref.shape[0] // 2
    sent_ref[...] = own_ref[pl.ds(pl.multiple_of(t * half, 32), half), :]


def pack_call(place, plan, arrays, shape, *earlier):
    return pl.pallas_call(
        functools.partial(pack_kernel, plan),
        in_specs=[SMEM] + [VMEM] * len(arrays) + [HBM] * len(earlier),
        out_specs=[VMEM, VMEM],
        out_shape=[sds(shape, BF), sds((shape[0] // 2, shape[1]), BF)],
        compiler_params=params(),
        cost_estimate=cost(1e6, 6 * shape[0] * shape[1]),
        name="pack",
    )(place, *arrays, *earlier)


def gather_start(own, sent):
    return own, swap(own, "fsdp", 1), swap(sent, "fsdp", 2)


def gather_rest(own, mate, near, *before):
    far = swap(near, "tower", 1)
    if before:
        far = after(far, *before)
    return own, mate, near, far, swap(near, "fsdp", 1), swap(far, "fsdp", 1)


def pick(parts, index):
    return lax.dynamic_index_in_dim(parts, index, 0, keepdims=False)


def rounded(v):
    return lax.reduce_precision(v, 8, 7)


def plus(a, b):
    return a.astype(F32) + b.astype(F32)


def spread_kernel(side, place_ref, *refs):
    ins, (out_1, mine_1, out_2, mine_2) = refs[: -4], refs[-4:]
    a, t = place_ref[0] // 2, place_ref[1]
    cols = FF // 2
    pairs = [(ins[0], ins[1])] if len(ins) < 4 else [(ins[0], ins[1]), (ins[2], ins[3])]
    start = 0
    for keep_ref, got_ref in pairs:
        width = keep_ref.shape[-1]
        for lo, hi, first in ((0, cols, True), (cols, 2 * cols, False)):
            lo, hi = max(lo, start), min(hi, start + width)
            if lo >= hi:
                continue
            src = pl.ds(lo - start, hi - lo)
            add = lambda i, rows: plus(keep_ref[i, rows, src], got_ref[i, rows, src]).astype(BF)
            every = pl.ds(0, 192)
            if first:
                out_1[pl.ds(0, 192), pl.ds(lo, hi - lo)] = add(1 - a, every)
                mine_1[pl.ds(0, 192), pl.ds(lo, hi - lo)] = add(a, every)
            else:
                dst = pl.ds(lo - cols, hi - lo)
                for i in range(2):
                    out_2[i, :, dst] = add(i, pl.ds(pl.multiple_of((1 - t) * 96, 32), 96))
                    mine_2[i, :, dst] = add(i, pl.ds(pl.multiple_of(t * 96, 32), 96))
        start += width
    if side:
        out_1[pl.ds(192, SIDE), :] = ins[4][...]
        mine_1[pl.ds(192, SIDE), :] = ins[4][...]


def spread_call(place, pairs, side=None, *earlier):
    cols = FF // 2
    rows = 192 + (SIDE if side is not None else 0)
    flat, deep = sds((rows, cols), BF), sds((2, 96, cols), BF)
    ins = [v for pair in pairs for v in pair] + ([side] if side is not None else [])

    def kernel(*refs):
        spread_kernel(side is not None, *refs[: 1 + len(ins)], *refs[-4:])

    return pl.pallas_call(
        kernel,
        in_specs=[SMEM] + [VMEM] * len(ins) + [HBM] * len(earlier),
        out_specs=[VMEM] * 4,
        out_shape=[flat, flat, deep, deep],
        compiler_params=params(),
        cost_estimate=cost(1e6, 7e6),
        name="spread",
    )(place, *ins, *earlier)


def cross_kernel(place_ref, mine_1, got_1, mine_2, got_2, *refs):
    out_1, keep_1, out_2, keep_2 = refs[-4:]
    a, t = place_ref[0] // 2, place_ref[1]
    rows = lambda i: pl.ds(pl.multiple_of(i * 96, 32), 96)
    out_1[pl.ds(0, 96), :] = plus(mine_1[rows(1 - t), :], got_1[rows(1 - t), :]).astype(BF)
    keep_1[pl.ds(0, 96), :] = plus(mine_1[rows(t), :], got_1[rows(t), :]).astype(BF)
    out_2[...] = plus(mine_2[1 - a], got_2[1 - a]).astype(BF)
    keep_2[...] = plus(mine_2[a], got_2[a]).astype(BF)
    if mine_1.shape[0] > 192:
        side = pl.ds(192, SIDE)
        both = plus(mine_1[side, :], got_1[side, :]).astype(BF)
        out_1[pl.ds(96, SIDE), :] = both
        keep_1[pl.ds(96, SIDE), :] = both


def cross_call(place, mine_1, got_1, mine_2, got_2, *earlier):
    rows = mine_1.shape[0] - 96
    flat, half = sds((rows, FF // 2), BF), sds((96, FF // 2), BF)
    return pl.pallas_call(
        cross_kernel,
        in_specs=[SMEM] + [VMEM] * 4 + [HBM] * len(earlier),
        out_specs=[VMEM] * 4,
        out_shape=[flat, flat, half, half],
        compiler_params=params(),
        cost_estimate=cost(1e6, 4e6),
        name="cross",
    )(place, mine_1, got_1, mine_2, got_2, *earlier)


def dp_steps(mine, got):
    z = lax.axis_index("dp")
    bits = [1 << i for i in range(lax.axis_size("dp").bit_length() - 1)]
    rows, cols = mine[0].shape
    side = rounded(plus(mine[0][96:, :D], got[0][96:, :D])) if rows > 96 else None
    mine, got = (mine[0][:96], mine[1]), (got[0][:96], got[1])
    for step, bit in enumerate(bits):
        up = (z // bit) % 2
        if step == 0:
            out = plus(jnp.where(up == 0, mine[1], mine[0]), jnp.where(up == 0, got[1], got[0])).astype(BF)
            mine = plus(jnp.where(up == 0, mine[0], mine[1]), jnp.where(up == 0, got[0], got[1]))
        else:
            cols = mine.shape[-1] // 2
            part = lambda v, i: lax.dynamic_slice_in_dim(v, i * cols, cols, 1)
            out = plus(part(mine, 1 - up), part(got, 1 - up)).astype(BF)
            mine = plus(part(mine, up), part(got, up))
        if side is not None and cols >= D:
            wide = jnp.pad(side.astype(BF), ((0, 0), (0, cols - D)))
            out = jnp.concatenate([out, wide], axis=0)
        out = yield out
        got = swap(out, "dp", bit)
        if side is not None and cols >= D:
            side = rounded(side + got[96:, :D].astype(F32))
            got = got[:96]
        elif side is not None:
            side = rounded(side + swap(side.astype(BF), "dp", bit).astype(F32))
    total = lax.optimization_barrier(plus(mine, got).astype(BF))
    for bit in reversed(bits[1:]):
        total = yield total
        up = (z // bit) % 2
        other = swap(total, "dp", bit)
        total = jnp.concatenate([jnp.where(up == 0, total, other), jnp.where(up == 0, other, total)], axis=1)
    return lax.optimization_barrier(total), side


def four(total, send, far_send, use):
    start = total if send is None else after(total, send)
    near = swap(start, "dp", 1)
    high = swap(start, "tower", 1)
    far = swap(after(near, high) if far_send is None else after(near, high, far_send), "tower", 1)
    return total, near, high if use is None else after(high, use), far


def drain(steps, block):
    while True:
        try:
            block = steps.send(block)
        except StopIteration as end:
            return end.value


def gather_rows(buf, is_query):
    got = swap(buf, "tower", 1)
    buf = jnp.concatenate(
        [jnp.where(is_query, buf[:, :PAY], got[:, :PAY]), jnp.where(is_query, got[:, PAY:], buf[:, PAY:])], axis=1
    )
    n_dp = lax.axis_size("dp")
    buf = jnp.concatenate([buf, swap(buf, "fsdp", 2)], axis=0)
    if n_dp == 4:
        buf = jnp.concatenate([buf] + [swap(buf, "dp", bits) for bits in (1, 2, 3)], axis=0)
    else:
        bit = 1
        while bit < n_dp:
            buf = jnp.concatenate([buf, swap(buf, "dp", bit)], axis=0)
            bit *= 2
    return buf, swap(buf, "fsdp", 1)


def row_sums(v):
    hi = v.astype(BF)
    lo = (v - hi.astype(F32)).astype(BF)
    ones = jnp.ones((8, v.shape[1]), BF)
    both = [lax.dot_general(ones, part, NT, preferred_element_type=F32) for part in (hi, lo)]
    return (both[0] + both[1])[0:1]


def joined(place_ref, refs):
    t, up = place_ref[1], place_ref[2] % 2
    own, near, high, far = (ref[...].astype(F32) for ref in refs)
    mine = jnp.concatenate([jnp.where(up == 0, own, near), jnp.where(up == 0, near, own)], axis=1)
    other = jnp.concatenate([jnp.where(up == 0, high, far), jnp.where(up == 0, far, high)], axis=1)
    return jnp.concatenate([jnp.where(t == 0, mine, other), jnp.where(t == 0, other, mine)], axis=0)


def tail_in_kernel(place_ref, a, b, c, d, own_ref, gain_ref, out_ref, sum_ref):
    g = joined(place_ref, (a, b, c, d))
    out_ref[...] = g
    sum_ref[...] = row_sums(g * own_ref[:, D:].astype(F32)) / gain_ref[...].astype(BF).astype(F32)


def tail_in_call(place, pieces, own, gain):
    return pl.pallas_call(
        tail_in_kernel,
        in_specs=[SMEM] + [VMEM] * 6,
        out_specs=[VMEM] * 2,
        out_shape=[sds((192, FF), F32), sds((1, 192), F32)],
        compiler_params=params(),
        cost_estimate=cost(1e7, 5e6),
        name="tail_in",
    )(place, *pieces, own, gain.reshape(1, 192))


def tail_attn_kernel(place_ref, a, b, c, d, own_ref, gain_ref, out_ref, q_ref, k_ref, v_ref, sum_ref):
    g = joined(place_ref, (a, b, c, d))
    out_ref[...] = g[:, :D]
    for p in range(PAIRS):
        for i, ref in enumerate((q_ref, k_ref, v_ref)):
            at = D + 384 * p + 128 * i
            ref[:, 128 * p : 128 * p + 128] = g[:, at : at + 128]
    sum_ref[...] = row_sums(g[:, D:] * own_ref[...].astype(F32)) / gain_ref[...].astype(BF).astype(F32)


def tail_attn_call(place, pieces, own, gain):
    return pl.pallas_call(
        tail_attn_kernel,
        in_specs=[SMEM] + [VMEM] * 6,
        out_specs=[VMEM] * 5,
        out_shape=[sds((192, D), F32)] * 4 + [sds((1, 192), F32)],
        compiler_params=params(),
        cost_estimate=cost(1e7, 5e6),
        name="tail_attn",
    )(place, *pieces, own, gain.reshape(1, 192))


def local(
    tokens_in,
    query_lengths,
    positive_ids,
    gain_attn,
    gain_ffn,
    w_query,
    w_key,
    w_value,
    w_out,
    rel_bias,
    w_in,
    w_ffn_out,
    w_proj,
):
    f = lax.axis_index("fsdp")
    t = lax.axis_index("tower")
    z = lax.axis_index("dp")
    rows = lax.axis_size("dp") * 4
    is_query = t == 0
    place = jnp.stack([f, t, z]).astype(jnp.int32)

    small = jnp.concatenate([gain_attn, gain_ffn, rel_bias.reshape(-1), jnp.zeros((32,), F32)])
    small = small.astype(BF).reshape(1, 512)
    small = jnp.concatenate([small, swap(small, "fsdp", 1)], axis=0)
    small = jnp.concatenate([small, swap(small, "fsdp", 2)], axis=0)
    small_all = small
    small = jnp.stack([pick(small, i ^ f) for i in range(4)])
    gain_one = small[:, :192].reshape(1, D).astype(F32)
    gain_two = small[:, 192:384].reshape(1, D).astype(F32)
    table = small[:, 384:480].reshape(NB, H)

    plan = [
        (i, (0, 192), (128 * p, 128), (0, 192), (384 * p + 128 * i, 128)) for p in range(PAIRS) for i in range(3)
    ]
    own1, sent1 = pack_call(place, plan, (w_query, w_key, w_value), (192, 3 * D))
    sent1 = after(sent1, small_all)
    plan = [(0, (0, 192), (0, D), (0, 192), (0, D)), (1, (0, 192), (0, FF), (0, 192), (D, FF))]
    own2, sent2 = pack_call(place, plan, (w_out, w_in), (192, D + FF), small_all)
    plan = []
    for h in range(2):
        plan.append((0, (384 * h, 384), (0, D), (480 * h, 384), (0, D)))
        plan.append((1, (96 * h, 96), (0, D), (480 * h + 384, 96), (0, D)))
    own3, sent3 = pack_call(place, plan, (w_ffn_out, w_proj), (960, D), small_all)
    first = gather_start(own1, sent1)
    near1 = after(first[2], own2, own3)
    middle = gather_start(own2, after(sent2, near1))

    lengths = query_lengths[:, 0]
    ends = jnp.cumsum(lengths, axis=-1)
    places = lax.broadcasted_iota(jnp.int32, (MB, SEQ, QSEG), 1)
    segment = jnp.where(is_query, jnp.sum((places >= ends[:, None, :]).astype(jnp.int32), axis=-1), 0)
    slot_ids = lax.broadcasted_iota(jnp.int32, (MB, QSEG), 1)
    counts = jnp.where(is_query, lengths, jnp.where(slot_ids < 1, SEQ, 0))
    seg = segment.reshape(T)
    lane = lax.broadcasted_iota(jnp.int32, (T, 128), 1) % 64
    hot_seg = lane == seg[:, None]
    fq = jnp.where(hot_seg, 1.0, 0.0).astype(BF)
    fk = jnp.where((lane < QSEG) & ~hot_seg, -1e30, 0.0).astype(BF)
    slot_of = seg + QSEG * (lax.broadcasted_iota(jnp.int32, (T,), 0) // SEQ)
    member2 = (slot_of[:, None] == lax.broadcasted_iota(jnp.int32, (T, 2 * SLOTS), 1) % SLOTS).astype(BF)
    member_t = (slot_of[None, :] == lax.broadcasted_iota(jnp.int32, (SLOTS, T), 0)).astype(BF)
    info = jnp.concatenate(
        [
            counts.reshape(SLOTS, 1).astype(F32),
            positive_ids.reshape(SLOTS, 1).astype(F32),
            jnp.zeros((SLOTS, 126), F32),
        ],
        axis=1,
    )
    bias = bias_blocks(jnp.pad(table.T, ((0, 4), (0, 0))), diag_hot())

    x = tokens_in.reshape(T, D)
    n1, n1t = norm_call(x, gain_one)
    first = gather_rest(*first[:2], near1, bias, n1)
    qkv = qkv_call(place, n1, first)
    middle = gather_rest(*middle[:2], after(middle[2], qkv))
    last = gather_start(own3, after(sent3, middle[2]))
    heads = [attn_fwd(qkv, fq, fk, bias, *AHEAD[0], middle[2])]
    heads.append(attn_fwd(qkv, fq, fk, bias, *AHEAD[1], heads[0][0]))
    near3 = after(last[2], heads[1][0])
    x2, n2t, gp, acts, xs = ffn_call(place, x, gain_two, member_t, [h[0] for h in heads], middle)
    last = gather_rest(*last[:2], near3, xs)
    buf, acts = pooled_call(place, acts, xs, info, last)
    own_buf, mate_buf = gather_rows(buf, is_query)
    loss, own, gf_all, grad_proj = loss_call(place, own_buf, mate_buf, last, rows)
    query_loss = loss[:, 0].reshape(MB, 1, QSEG)

    acts_all = lax.all_gather(after(acts, own_buf), ALL, axis=0, tiled=True)
    keep_i, send_i, g_n2 = ffn_bwd_call(place, own, member2, gp, n2t, middle, last)
    got_i = swap(send_i, "fsdp", 1)
    g_x2, go, keep, send = mid_call(place, g_n2, x2, gain_two, own, member2, [h[1] for h in heads], middle)
    out_1, mine_1, out_2, mine_2 = spread_call(place, [(keep_i, got_i)], None, keep)
    got_1, got_2 = swap(out_1, "fsdp", 2), swap(out_2, "tower", 1)
    back = lambda i, *earlier: attn_bwd(place, qkv, go, n1t, heads, *SPLIT[i], *earlier)
    d_a, keep, send, diag_a = back(0, (keep, send), out_1, out_2)
    out_1, mine_1, out_2, mine_2 = cross_call(place, mine_1, got_1, mine_2, got_2, d_a)
    got_1, got_2 = swap(out_1, "tower", 1), swap(out_2, "fsdp", 2)
    d_b, keep, send, diag_b = back(1, (keep, send), out_1, out_2)
    got = swap(send, "fsdp", 1)
    steps = dp_steps((mine_1, mine_2), (got_1, got_2))
    z_out = next(steps)
    d_c, keep_c, send_c, diag_c = back(2, (), d_b, acts_all)
    got_c = swap(send_c, "fsdp", 1)
    diag = jnp.concatenate([diag_a, diag_b, diag_c], axis=0).reshape(H, 8192)
    table_grad = jnp.einsum("hc,cb->hb", diag, diag_hot2(), precision=HIGHEST)
    table_grad = jnp.pad(table_grad, ((0, SIDE - H), (0, FF // 2 - NB))).astype(BF)
    out_b, mine_1b, out_2b, mine_2b = spread_call(place, [(keep, got), (keep_c, got_c)], table_grad, z_out)
    got_1b, got_2b = swap(out_b, "fsdp", 2), swap(out_2b, "tower", 1)
    z_out = after(steps.send(z_out), out_b)
    grad_tokens = token_call(place, g_x2, x, gain_one, (d_a, d_b, d_c), first, out_b, out_2b, z_out)
    z_out = after(steps.send(z_out), grad_tokens)
    out_1b, mine_1b, out_2b, mine_2b = cross_call(place, mine_1b, got_1b, mine_2b, got_2b, z_out)
    total_i = drain(steps, z_out)[0]
    grad_tokens = grad_tokens.reshape(1, MB, 1, SEQ, D)
    got_1b, got_2b = swap(out_1b, "tower", 1), swap(out_2b, "fsdp", 2)
    steps = dp_steps((mine_1b, mine_2b), (got_1b, got_2b))
    z_two = steps.send(next(steps))
    z_three = steps.send(z_two)
    total_b, side = drain(steps, z_three)
    four_i = four(total_i, z_two, z_three, total_b)
    four_b = four(total_b, None, None, None)
    grad_in, gain_ffn_grad = tail_in_call(place, four_i, own2, gain_ffn)
    grad_out, grad_q, grad_k, grad_v, gain_attn_grad = tail_attn_call(place, four_b, own1, gain_attn)
    side = side[:H, :NB]
    grad_table = (side + swap(side, "fsdp", 1)).T

    acts_all = lax.dynamic_slice_in_dim(after(acts_all, total_b), f * D, D, 1).reshape(2, rows * MB, QSEG, D)
    acts_all = jnp.concatenate([acts_all[0].reshape(rows * SLOTS, D), acts_all[1, :, 0]], axis=0)
    grad_ffn_out = lax.dot_general(acts_all, gf_all, TN, preferred_element_type=F32)
    return (
        query_loss,
        grad_tokens,
        gain_attn_grad.reshape(192),
        gain_ffn_grad.reshape(192),
        grad_q,
        grad_k,
        grad_v,
        grad_out,
        lax.dynamic_slice_in_dim(grad_table, f * 8, 8, 0),
        grad_in,
        grad_ffn_out,
        grad_proj,
    )


def solution(mesh):
    rows = P(None, ("dp", "fsdp"), None)
    tokens = P("tower", None, ("dp", "fsdp"), None, None)
    vec, mat = P("fsdp"), P("fsdp", None)
    return jax.shard_map(
        local,
        mesh=mesh,
        in_specs=(tokens, rows, rows, vec, vec) + (mat,) * 8,
        out_specs=(rows, tokens, vec, vec) + (mat,) * 8,
        check_vma=False,
    )
```
